256 devices in a mesh: slab: 128 (over y_hi, z, x, core), feat: 2 (over y_lo).
Axes of the slice: x: 4, y: 4 (y_hi: 2, y_lo: 2; y = y_hi * 2 + y_lo), z: 8, core: 2. Of those that a mesh axis runs over, the one named last changes fastest.
Arguments:
- node_feats: bfloat16 [128, 524288], P('feat', 'slab'), may hold values from -6 to 6
- neighbours: int32 [16, 524288], P(None, 'slab'), may hold values from 0 to 12287, as said below
- degrees: int32 [524288], P('slab'), may hold values from 1 to 16
- hub_rows: int32 [4096], P('slab'), may hold values from 0 to 4095, as said below
- weight: bfloat16 [128, 128], replicated, may hold values from -0.5 to 0.5
- bias_terms: float32 [128], replicated, may hold values from -3 to 3
Outputs:
- new_feats: bfloat16 [128, 524288], P('feat', 'slab')
The draws below stay inside these ranges and needn't reach their ends.
Inputs may be any that keep to these rules, and one draw needn't show every extreme that they name: `neighbours`: slots index frame columns; positions 0..2047 are the lower halo (never used by slab 0), 6144..8191 the upper halo (never used by the last slab), from 8192 on the hub panel. `hub_rows`: distinct within each slab.
All inputs are finite; a program needn't handle non-finite values.
Results may differ from the reference program's by a relative error of at most 0.0034.
Values may be sent and summed in bfloat16 or wider, within the bound.
No kernel may reach another device: no remote copies, remote signals or barrier semaphores. Data moves between devices by JAX's collectives and lax.ppermute only.
A program may use at most 64 MiB of HBM per device.

```python
import jax
import jax.numpy as jnp
from jax import lax

F = 128
ROWS = 4096
DEGREE = 16
HUB_DEV = 32
NODES = 524288
N_SLAB = 128


def draw_neighbours(key, part):
    key = jax.random.fold_in(key, 11)
    key_kind, key_inside, key_side, key_offset, key_hub = jax.random.split(key, 5)
    node_count = ROWS * N_SLAB
    halo_width = ROWS // 2
    shape = (node_count, DEGREE)
    choose = jax.random.randint(key_kind, shape, 0, 20)
    inside = halo_width + jax.random.randint(key_inside, shape, 0, ROWS)
    upper_side = jax.random.randint(key_side, shape, 0, 2)
    slab_index = (jnp.arange(node_count, dtype=jnp.int32) // ROWS)[:, None]
    upper_side = jnp.where(slab_index == 0, 1, jnp.where(slab_index == N_SLAB - 1, 0, upper_side))
    offset = jax.random.randint(key_offset, shape, 0, halo_width)
    rim_ids = jnp.where(upper_side == 0, offset, halo_width + ROWS + offset)
    hub_ids = 2 * halo_width + ROWS + jax.random.randint(key_hub, shape, 0, HUB_DEV * N_SLAB)
    result = jnp.where(choose < 12, inside, jnp.where(choose < 17, rim_ids, hub_ids))
    result = result.at[0, DEGREE - 1].set(2 * ROWS + HUB_DEV * N_SLAB - 1)
    result = result.at[ROWS, 0].set(0)
    return result.T.astype(jnp.int32)


def draw_degrees(key, part):
    key = jax.random.fold_in(key, 12)
    result = jax.random.randint(key, (ROWS * N_SLAB,), 1, DEGREE + 1)
    result = result.at[0].set(DEGREE).at[1].set(1)
    return result.astype(jnp.int32)


def draw_hub_rows(key, part):
    key = jax.random.fold_in(key, 13)
    slab_keys = jax.random.split(key, N_SLAB)
    picked = jax.vmap(lambda one_key: jax.random.permutation(one_key, ROWS)[:HUB_DEV])(slab_keys)
    return picked.reshape(N_SLAB * HUB_DEV).astype(jnp.int32)


def level_of(stream_key, extent, pieces, low, high):
    gain = 1.0
    for dim, parts in pieces:
        heights = jax.random.uniform(jax.random.fold_in(jax.random.fold_in(stream_key, 6), dim), (parts,), jnp.float32, low / len(pieces), high / len(pieces))
        gain = gain * jnp.repeat(jnp.exp(heights), extent[dim] // parts).reshape((-1,) + (1,) * (len(extent) - 1 - dim))
    return gain


def gaussian(key, extent, scale, reach, cuts=(), kind=jnp.bfloat16):
    entries = jax.random.normal(key, extent, jnp.float32) * scale
    if len(cuts) > 0:
        entries = level_of(key, extent, cuts, -0.22, 0.18) * entries
    return jnp.clip(entries, min=-reach, max=reach).astype(kind)


def setup_inputs(seed: int = 0) -> dict:
    key_of = jax.random.split(jax.random.key(seed), 7)
    node_feats = gaussian(key_of[0], (F, NODES), 1.0, 6.0, ((0, 2), (1, 128)))
    neighbours = draw_neighbours(jax.random.fold_in(key_of[6], 71), 0)
    degrees = draw_degrees(jax.random.fold_in(key_of[6], 71), 0)
    hub_rows = draw_hub_rows(jax.random.fold_in(key_of[6], 71), 0)
    weight = gaussian(key_of[4], (F, F), F ** -0.5, 0.5)
    bias_terms = gaussian(key_of[5], (F,), 0.5, 3.0, (), jnp.float32)
    return {"node_feats": node_feats, "neighbours": neighbours, "degrees": degrees, "hub_rows": hub_rows, "weight": weight, "bias_terms": bias_terms}


def aggregate(frame, slot_ids, degree_counts, own_rows):
    picked = jnp.take(frame, slot_ids, axis=0).astype(jnp.float32)
    slot_mask = jnp.arange(slot_ids.shape[1], dtype=jnp.int32)[None, :] < degree_counts[:, None]
    totals = jnp.sum(jnp.where(slot_mask[:, :, None], picked, jnp.zeros_like(picked)), axis=1)
    totals = totals + own_rows.astype(jnp.float32)
    return (totals / (degree_counts + 1).astype(jnp.float32)[:, None]).astype(jnp.bfloat16)


def reference(node_feats, neighbours, degrees, hub_rows, weight, bias_terms):
    row_major = node_feats.T
    slots_major = neighbours.T
    halo_width = ROWS // 2
    hub_slab = jnp.arange(N_SLAB * HUB_DEV, dtype=jnp.int32) // HUB_DEV
    hub_panel = jnp.take(row_major, (hub_slab * ROWS + hub_rows).astype(jnp.int32), axis=0)
    zero_rows = jnp.zeros((halo_width, F), row_major.dtype)
    padded = jnp.concatenate([zero_rows, row_major, zero_rows], axis=0)

    def one_slab(slab_index):
        first_row = (slab_index * ROWS).astype(jnp.int32)
        window = lax.dynamic_slice_in_dim(padded, first_row, ROWS + 2 * halo_width, 0)
        frame = jnp.concatenate([window, hub_panel], axis=0)
        slot_ids = lax.dynamic_slice_in_dim(slots_major, first_row, ROWS, 0)
        degree_counts = lax.dynamic_slice_in_dim(degrees, first_row, ROWS, 0)
        own_rows = lax.dynamic_slice_in_dim(row_major, first_row, ROWS, 0)
        return aggregate(frame, slot_ids, degree_counts, own_rows)

    mean_rows = lax.map(one_slab, jnp.arange(N_SLAB, dtype=jnp.int32)).reshape(N_SLAB * ROWS, F)
    product = jnp.dot(mean_rows, weight, preferred_element_type=jnp.float32)
    result = jax.nn.relu(product + bias_terms.astype(jnp.float32)[None, :]).astype(jnp.bfloat16)
    return result.T
```

```python
import functools

import jax
import jax.numpy as jnp
from jax import lax
from jax.experimental import pallas as pl
from jax.experimental.pallas import tpu as pltpu
from jax.sharding import PartitionSpec as P

VMEM = pltpu.VMEM
SMEM = pltpu.SMEM
LANES = 128
CHUNK = 1024
GROUP = 16
STAGES = (32, 8, 16, 64, 4, 2, 1)


def hub_pick_kernel(rows_ref, x_ref, out_ref):
    hubs, nodes = rows_ref.shape[1], x_ref.shape[1]
    diagonal = lax.broadcasted_iota(jnp.int32, (hubs, hubs), 0) == lax.broadcasted_iota(
        jnp.int32, (hubs, hubs), 1
    )
    rows = jnp.sum(jnp.where(diagonal, rows_ref[...], 0), axis=1, keepdims=True)
    onehot = (lax.broadcasted_iota(jnp.int32, (hubs, nodes), 1) == rows).astype(jnp.bfloat16)
    picked = lax.dot_general(
        onehot, x_ref[...], (((1,), (1,)), ((), ())), preferred_element_type=jnp.float32
    ).astype(jnp.bfloat16)
    out_ref[...] = jnp.concatenate([picked[: hubs // 2], picked[hubs // 2 :]], axis=1)


def frame_kernel(low_ref, x_ref, high_ref, after_ref, frame_ref):
    nodes = x_ref.shape[1]
    half = low_ref.shape[1]
    step = 256
    unit = (
        lax.broadcasted_iota(jnp.int32, (step, step), 0)
        == lax.broadcasted_iota(jnp.int32, (step, step), 1)
    ).astype(jnp.bfloat16)

    def fill(ref, first, count):
        for at in range(0, count, step):
            cols = ref[:, at : at + step]
            frame_ref[first + at : first + at + step, :] = lax.dot_general(
                unit,
                jnp.concatenate([cols, cols], axis=0),
                (((1,), (1,)), ((), ())),
                preferred_element_type=jnp.float32,
            )

    fill(low_ref, 0, half)
    fill(x_ref, half, nodes)
    fill(high_ref, half + nodes, half)
    frame_ref[2 * half + nodes :, :] = jnp.zeros((8, LANES), jnp.float32)


def hub_frame_kernel(near_ref, far_ref, frame_ref):
    blocks = near_ref.shape[0] // 16
    me = lax.axis_index("slab")
    lane = lax.broadcasted_iota(jnp.int32, (16, LANES), 1)
    for p in range(2 * blocks):
        ref, i = (near_ref, p) if p < blocks else (far_ref, p - blocks)
        differs = sum(bit for k, bit in enumerate(STAGES) if p >> k & 1)
        pair = ref[16 * i : 16 * i + 16, :].astype(jnp.float32)
        turned = pltpu.roll(pair, LANES // 2, 1)
        at = pl.multiple_of((me ^ differs) * 32, 32)
        frame_ref[pl.ds(at, 16), :] = jnp.where(lane < LANES // 2, pair, turned)
        frame_ref[pl.ds(at + 16, 16), :] = jnp.where(lane < LANES // 2, turned, pair)
    frame_ref[64 * blocks :, :] = jnp.zeros((8, LANES), jnp.float32)


def comparators(count):
    pairs, p = [], 1
    while p < count:
        k = p
        while k >= 1:
            for j in range(k % p, count - k, 2 * k):
                for i in range(min(k, count - j - k)):
                    if (i + j) // (2 * p) == (i + j + k) // (2 * p):
                        pairs.append((i + j, i + j + k))
            k //= 2
        p *= 2
    return pairs


def sort_network(values):
    for a, b in comparators(len(values)):
        values[a], values[b] = jnp.minimum(values[a], values[b]), jnp.maximum(values[a], values[b])
    return values


def sorted_tiles(keys):
    shape = keys.shape
    sub = lax.broadcasted_iota(jnp.int32, shape, 1)
    lane = lax.broadcasted_iota(jnp.int32, shape, 2)
    at = sub * LANES + lane
    size = 2
    while size <= CHUNK:
        distance = size // 2
        while distance >= 1:
            axis, by, extent = (2, distance, LANES) if distance < LANES else (1, distance // LANES, 8)
            lower = (at & distance) == 0
            partner = jnp.where(
                lower, pltpu.roll(keys, extent - by, axis), pltpu.roll(keys, by, axis)
            )
            ascending = (at & size) == 0
            keys = jnp.where(
                lower == ascending, jnp.minimum(keys, partner), jnp.maximum(keys, partner)
            )
            distance //= 2
        size *= 2
    return keys


def plan_kernel(first, after, nbr_ref, deg_ref, after_ref, ids_ref, order_ref, class_ref):
    slots = nbr_ref.shape[0]
    chunks = deg_ref.shape[0] // 8
    at = lax.broadcasted_iota(jnp.int32, (8, LANES), 0) * LANES + lax.broadcasted_iota(
        jnp.int32, (8, LANES), 1
    )
    keys = []
    for c in range(chunks):
        rows = slice(8 * c, 8 * c + 8)
        degree = deg_ref[rows, :]
        ids = []
        count = jnp.zeros((8, LANES), jnp.int32)
        for j in range(slots):
            nbr = nbr_ref[j, rows, :]
            inside = (degree > j) & ((nbr < after) if first == 0 else (nbr >= first))
            ids.append(jnp.where(inside, nbr, after) - first)
            count = count + inside.astype(jnp.int32)
        for j, sorted_ids in enumerate(sort_network(ids)):
            ids_ref[c, j] = sorted_ids
        keys.append(count * CHUNK + at)
    keys = sorted_tiles(jnp.stack(keys))
    order_ref[...] = keys & (CHUNK - 1)
    class_ref[...] = keys >> 10


def scale_kernel(deg_ref, after_ref, scale_ref):
    half = CHUNK // LANES // 2
    inverse = 1.0 / (deg_ref[...] + 1).astype(jnp.float32)
    for c in range(scale_ref.shape[0]):
        for t in range(half):
            a = inverse[8 * c + t : 8 * c + t + 1, :]
            b = inverse[8 * c + half + t : 8 * c + half + t + 1, :]
            both = jnp.concatenate(
                [jnp.broadcast_to(row, (LANES // 2, LANES)) for row in (a, b)], axis=0
            )
            scale_ref[c, LANES * t : LANES * (t + 1), :] = both.T


def halo_kernel(x_ref, after_ref, low_ref, high_ref):
    half = low_ref.shape[1]
    low_ref[...] = x_ref[:, half:]
    high_ref[...] = x_ref[:, :half]


def add_tree(parts):
    while len(parts) > 1:
        tail = [parts[-1]] if len(parts) % 2 else []
        parts = [parts[i] + parts[i + 1] for i in range(0, len(parts) - 1, 2)] + tail
    return parts[0]


def load_plan(slots, chunk, ids_ref, order_ref, class_ref, slot_ids, order, classes, sem):
    rows = pl.ds(chunk * CHUNK, CHUNK)
    first = [
        pltpu.make_async_copy(order_ref.at[rows], order, sem.at[slots]),
        pltpu.make_async_copy(class_ref.at[rows], classes.at[pl.ds(0, CHUNK)], sem.at[slots + 1]),
    ]
    by_slot = [
        pltpu.make_async_copy(
            ids_ref.at[pl.ds((chunk * slots + j) * CHUNK, CHUNK)],
            slot_ids.at[pl.ds(j * CHUNK, CHUNK)],
            sem.at[j],
        )
        for j in range(slots)
    ]
    for copy in first + by_slot:
        copy.start()
    return first, by_slot


def sum_slots(slots, by_slot, slot_ids, order, classes, frame_ref, total_ref):
    last = GROUP - 1
    classes[CHUNK + last] = slots + 1
    of_slot = [slot_ids.at[pl.ds(j * CHUNK, CHUNK)] for j in range(slots)]

    def body(count, carry):
        g, _ = carry
        base = g * GROUP
        for k in range(GROUP):
            node = order[base + k]
            total_ref[pl.ds(node, 1), :] = add_tree(
                [frame_ref[pl.ds(of_slot[j][node], 1), :] for j in range(count)]
            )
        return g + 1, classes[base + GROUP + last]

    def skip(carry):
        g, _ = carry
        return g + 1, classes[g * GROUP + GROUP + last]

    carry = (jnp.int32(0), classes[last])
    carry = lax.while_loop(lambda carry: carry[1] == 0, skip, carry)
    for count in range(1, slots + 1):
        by_slot[count - 1].wait()
        carry = lax.while_loop(
            lambda carry, count=count: carry[1] == count, functools.partial(body, count), carry
        )


def near_kernel(slots, chunk, own, ids_ref, order_ref, class_ref, frame_ref, after_ref, total_ref, *plan):
    first, by_slot = load_plan(slots, chunk, ids_ref, order_ref, class_ref, *plan)
    total_ref[...] = jnp.zeros_like(total_ref)
    for copy in first:
        copy.wait()
    sum_slots(slots, by_slot, *plan[:3], frame_ref, total_ref)
    total_ref[...] = total_ref[...] + frame_ref[pl.ds(own + chunk * CHUNK, CHUNK), :]


def far_kernel(slots, chunk, ids_ref, order_ref, class_ref, frame_ref, near_ref, scale_ref, after_ref, out_ref, total_ref, *plan):
    first, by_slot = load_plan(slots, chunk, ids_ref, order_ref, class_ref, *plan)
    total_ref[...] = jnp.zeros_like(total_ref)
    for copy in first:
        copy.wait()
    sum_slots(slots, by_slot, *plan[:3], frame_ref, total_ref)
    pairs = out_ref.shape[0]
    step = 64
    lane = lax.broadcasted_iota(jnp.int32, (step, LANES), 1)
    for at in range(0, pairs, step):
        a, b = slice(at, at + step), slice(pairs + at, pairs + at + step)
        total = jnp.where(
            lane < LANES // 2, total_ref[a, :] + near_ref[a, :], total_ref[b, :] + near_ref[b, :]
        )
        out_ref[a, :] = (total * scale_ref[chunk, a, :]).astype(jnp.bfloat16)


def join_kernel(near_ref, far_ref, after_ref, out_ref):
    rows = near_ref.shape[0]
    out_ref[:rows] = near_ref[...]
    out_ref[rows:] = far_ref[...]


def layer_kernel(chunks, weight_ref, bias_ref, *refs):
    mine, theirs, out_ref = refs[:chunks], refs[chunks : 2 * chunks], refs[2 * chunks]
    pairs = mine[0].shape[0]
    chans = out_ref.shape[0]
    first = lax.axis_index("feat") == 0
    by_out = weight_ref[...].astype(jnp.float32).T
    by_out = jnp.where(first, by_out[:chans], by_out[chans:]).astype(jnp.bfloat16)
    own = jnp.where(first, by_out[:, :chans], by_out[:, chans:])
    far = jnp.where(first, by_out[:, chans:], by_out[:, :chans])
    none = jnp.zeros_like(own)
    weights = [
        jnp.concatenate([own, none, far, none], axis=1),
        jnp.concatenate([none, own, none, far], axis=1),
    ]
    row = lax.broadcasted_iota(jnp.int32, (chans, 2 * chans), 0) + jnp.where(first, 0, chans)
    lane = lax.broadcasted_iota(jnp.int32, (chans, 2 * chans), 1)
    bias = jnp.sum(jnp.where(row == lane, bias_ref[...], 0.0), axis=1, keepdims=True)
    for c in range(chunks):
        rows = jnp.concatenate([mine[c][...], theirs[c][...]], axis=1)
        for h in range(2):
            product = lax.dot_general(
                weights[h], rows, (((1,), (1,)), ((), ())), preferred_element_type=jnp.float32
            )
            out_ref[:, pl.ds((2 * c + h) * pairs, pairs)] = jnp.maximum(product + bias, 0.0).astype(
                jnp.bfloat16
            )


def pallas(kernel, out_shape, in_specs, scratch=(), us=1.0):
    return pl.pallas_call(
        kernel,
        out_shape=out_shape,
        in_specs=in_specs,
        out_specs=jax.tree.map(lambda _: IN_VMEM, out_shape),
        scratch_shapes=list(scratch),
        compiler_params=pltpu.CompilerParams(vmem_limit_bytes=6 * 2**20),
        cost_estimate=pl.CostEstimate(flops=0, bytes_accessed=int(us * 3_000_000), transcendentals=0),
    )


IN_VMEM = pl.BlockSpec(memory_space=VMEM)
ANYWHERE = pl.BlockSpec(memory_space=pl.ANY)


def local(node_feats, neighbours, degrees, hub_rows, weight, bias_terms):
    chans, nodes = node_feats.shape
    slots = neighbours.shape[0]
    hubs = hub_rows.shape[0]
    slabs = lax.axis_size("slab")
    half = nodes // 2
    chunks = nodes // CHUNK
    pairs = CHUNK // 2

    block = pallas(
        hub_pick_kernel, jax.ShapeDtypeStruct((hubs // 2, 2 * chans), jnp.bfloat16), [IN_VMEM] * 2
    )(hub_rows[None, :], node_feats)

    def stage(block, bit):
        return lax.ppermute(block, "slab", [(i, i ^ bit) for i in range(slabs)])

    table = jax.ShapeDtypeStruct((chunks, slots, 8, LANES), jnp.int32)
    tiles = jax.ShapeDtypeStruct((chunks, 8, LANES), jnp.int32)
    frame_rows, hub_count = 2 * half + nodes, slabs * hubs
    nbr_tiles = neighbours.reshape(slots, nodes // LANES, LANES)
    deg_tiles = degrees.reshape(nodes // LANES, LANES)

    def plan(first, after, behind):
        return pallas(
            functools.partial(plan_kernel, first, after),
            (table, tiles, tiles),
            [IN_VMEM, IN_VMEM, ANYWHERE],
            us=3.0,
        )(nbr_tiles, deg_tiles, behind)

    near_plan = plan(0, frame_rows, block)

    plan_scratch = [
        SMEM((slots * CHUNK,), jnp.int32),
        SMEM((CHUNK,), jnp.int32),
        SMEM((CHUNK + GROUP,), jnp.int32),
        pltpu.SemaphoreType.DMA((slots + 2,)),
    ]
    totals = jax.ShapeDtypeStruct((CHUNK, LANES), jnp.float32)
    beside = [near_plan[1]]
    near = []
    for k, bit in enumerate(STAGES):
        arrived = stage(block, bit)
        if k == len(STAGES) - 1:
            break
        if k == 1:
            halo = jax.ShapeDtypeStruct((chans, half), jnp.bfloat16)
            low, high = pallas(halo_kernel, (halo, halo), [IN_VMEM, ANYWHERE], us=0.3)(node_feats, block)
            low = lax.ppermute(low, "slab", [(i, i + 1) for i in range(slabs - 1)])
            high = lax.ppermute(high, "slab", [(i + 1, i) for i in range(slabs - 1)])
            far_plan = plan(frame_rows, frame_rows + hub_count, block)
            scale = pallas(
                scale_kernel,
                jax.ShapeDtypeStruct((chunks, pairs, LANES), jnp.float32),
                [IN_VMEM, ANYWHERE],
            )(deg_tiles, far_plan[1])
            frame = pallas(
                frame_kernel,
                jax.ShapeDtypeStruct((frame_rows + 8, LANES), jnp.float32),
                [IN_VMEM] * 3 + [ANYWHERE],
                us=2.0,
            )(low, node_feats, high, scale)
            beside.append(frame)
        if k >= 2:
            near.append(
                pallas(
                    functools.partial(near_kernel, slots, k - 2, half),
                    totals,
                    [ANYWHERE] * 3 + [IN_VMEM, ANYWHERE],
                    plan_scratch,
                    us=6.0,
                )(*(a.reshape(-1) for a in near_plan), frame, block)
            )
            beside.append(near[-1])
        rows = block.shape[0]
        block = pallas(
            join_kernel,
            jax.ShapeDtypeStruct((2 * rows, 2 * chans), jnp.bfloat16),
            [IN_VMEM, IN_VMEM, ANYWHERE],
            us=0.5,
        )(block, arrived, beside[k])

    hub_frame = pallas(
        hub_frame_kernel, jax.ShapeDtypeStruct((hub_count + 8, LANES), jnp.float32), [IN_VMEM, IN_VMEM]
    )(block, arrived)

    swap = [(0, 1), (1, 0)]
    mine, theirs = [], []
    for c in range(chunks):
        after = theirs[c - 2] if c >= 2 else hub_rows
        rows = pallas(
            functools.partial(far_kernel, slots, c),
            jax.ShapeDtypeStruct((pairs, 2 * chans), jnp.bfloat16),
            [ANYWHERE] * 3 + [IN_VMEM] * 3 + [ANYWHERE],
            [VMEM((CHUNK, LANES), jnp.float32)] + plan_scratch,
            us=3.0,
        )(*(a.reshape(-1) for a in far_plan), hub_frame, near[c], scale, after)
        mine.append(rows)
        theirs.append(lax.ppermute(rows, "feat", swap))

    return pallas(
        functools.partial(layer_kernel, chunks),
        jax.ShapeDtypeStruct((chans, nodes), jnp.bfloat16),
        [IN_VMEM] * (2 + 2 * chunks),
    )(weight, bias_terms[None, :], *mine, *theirs)


def solution(mesh):
    in_specs = (P("feat", "slab"), P(None, "slab"), P("slab"), P("slab"), P(), P())
    return jax.shard_map(local, mesh=mesh, in_specs=in_specs, out_specs=P("feat", "slab"), check_vma=False)
```

```python
import functools

import jax
import jax.numpy as jnp
from jax import lax
from jax.experimental import pallas as pl
from jax.experimental.pallas import tpu as pltpu
from jax.sharding import PartitionSpec as P

VMEM = pltpu.VMEM
SMEM = pltpu.SMEM
LANES = 128
CHUNK = 1024
GROUP = 16
STAGES = ((32,), (8, 16, 24), (64,), (2, 4, 6), (1,))


def hub_pick_kernel(rows_ref, x_hbm, out_ref, x_ref, sem):
    hubs, nodes = rows_ref.shape[1], x_ref.shape[1]
    parts = sem.shape[0]
    copies = [
        pltpu.make_async_copy(x_hbm.at[:, part], x_ref.at[:, part], sem.at[i])
        for i in range(parts)
        for part in [pl.ds(i * (nodes // parts), nodes // parts)]
    ]
    for copy in copies:
        copy.start()
    diagonal = lax.broadcasted_iota(jnp.int32, (hubs, hubs), 0) == lax.broadcasted_iota(
        jnp.int32, (hubs, hubs), 1
    )
    rows = jnp.sum(jnp.where(diagonal, rows_ref[...], 0), axis=1, keepdims=True)
    onehot = (lax.broadcasted_iota(jnp.int32, (hubs, nodes), 1) == rows).astype(jnp.bfloat16)
    for copy in copies:
        copy.wait()
    picked = lax.dot_general(
        onehot, x_ref[...], (((1,), (1,)), ((), ())), preferred_element_type=jnp.float32
    ).astype(jnp.bfloat16)
    out_ref[...] = jnp.concatenate([picked[: hubs // 2], picked[hubs // 2 :]], axis=1)


def join_kernel(*refs):
    blocks, out_ref = refs[:-2], refs[-1]
    rows = blocks[0].shape[0]
    for i, ref in enumerate(blocks):
        out_ref[i * rows : (i + 1) * rows] = ref[...]


def join_feat_kernel(mine_ref, other_ref, after_ref, out_ref):
    first = lax.axis_index("feat") == 0
    lane = lax.broadcasted_iota(jnp.int32, (16, LANES), 1)
    for i in range(mine_ref.shape[0] // 16):
        mine = mine_ref[16 * i : 16 * i + 16, :].astype(jnp.float32)
        other = other_ref[16 * i : 16 * i + 16, :].astype(jnp.float32)
        low = jnp.where(first, mine, other)
        high = jnp.where(first, other, mine)
        row = jnp.where(lane < LANES // 2, low, pltpu.roll(high, LANES // 2, 1))
        out_ref[32 * i : 32 * i + 16, :] = row.astype(jnp.bfloat16)
        row = jnp.where(lane < LANES // 2, pltpu.roll(low, LANES // 2, 1), high)
        out_ref[32 * i + 16 : 32 * i + 32, :] = row.astype(jnp.bfloat16)


def halves_kernel(x_ref, other_ref, after_ref, outer_ref, inner_ref):
    feat = lax.axis_index("feat")
    odd = lax.axis_index("slab") & 1
    chans, half = x_ref.shape[0], outer_ref.shape[1]
    for ref, channels in ((x_ref, feat), (other_ref, 1 - feat)):
        rows = pl.ds(pl.multiple_of(channels * chans, chans), chans)
        outer_ref[rows, :] = ref[:, pl.ds(pl.multiple_of(odd * half, half), half)]
        inner_ref[rows, :] = ref[:, pl.ds(pl.multiple_of((1 - odd) * half, half), half)]


def frame_kernel(outer_halo_ref, outer_ref, inner_ref, inner_halo_ref, after_ref, frame_ref):
    odd = lax.axis_index("slab") & 1
    half = outer_ref.shape[1]
    step = 256
    unit = (
        lax.broadcasted_iota(jnp.int32, (step, step), 0)
        == lax.broadcasted_iota(jnp.int32, (step, step), 1)
    ).astype(jnp.bfloat16)
    for place, ref in enumerate((outer_halo_ref, outer_ref, inner_ref, inner_halo_ref)):
        first = (place + odd * (3 - 2 * place)) * half
        for at in range(0, half, step):
            frame_ref[pl.ds(pl.multiple_of(first + at, step), step), :] = lax.dot_general(
                unit,
                ref[:, at : at + step],
                (((1,), (1,)), ((), ())),
                preferred_element_type=jnp.float32,
            )
    rows = frame_ref.shape[0]
    frame_ref[rows - 8 :, :] = jnp.zeros((8, LANES), jnp.float32)


def origins():
    differs = [0]
    for bits in STAGES:
        differs = [d ^ bit for bit in (0,) + bits for d in differs]
    return differs


def hub_frame_kernel(first, hubs, frame_in, near_ref, far_ref, after_ref, frame_ref):
    blocks = near_ref.shape[0] // hubs
    me = lax.axis_index("slab")
    for p, differs in enumerate(origins()):
        ref, i = (near_ref, p) if p < blocks else (far_ref, p - blocks)
        at = pl.multiple_of(first + (me ^ differs) * hubs, hubs)
        frame_ref[pl.ds(at, hubs), :] = ref[hubs * i : hubs * (i + 1), :].astype(jnp.float32)


def comparators(count):
    pairs, p = [], 1
    while p < count:
        k = p
        while k >= 1:
            for j in range(k % p, count - k, 2 * k):
                for i in range(min(k, count - j - k)):
                    if (i + j) // (2 * p) == (i + j + k) // (2 * p):
                        pairs.append((i + j, i + j + k))
            k //= 2
        p *= 2
    return pairs


def sort_network(values):
    for a, b in comparators(len(values)):
        values[a], values[b] = jnp.minimum(values[a], values[b]), jnp.maximum(values[a], values[b])
    return values


def sorted_tiles(keys, halved):
    shape = keys.shape
    apart = lax.broadcasted_iota(jnp.int32, shape, 0) == halved
    sub = lax.broadcasted_iota(jnp.int32, shape, 1)
    lane = lax.broadcasted_iota(jnp.int32, shape, 2)
    at = sub * LANES + lane
    size = 2
    while size <= CHUNK:
        distance = size // 2
        while distance >= 1:
            axis, by, extent = (2, distance, LANES) if distance < LANES else (1, distance // LANES, 8)
            lower = (at & distance) == 0
            partner = jnp.where(
                lower, pltpu.roll(keys, extent - by, axis), pltpu.roll(keys, by, axis)
            )
            ascending = (at & size) == 0
            if 2 * size == CHUNK:
                ascending = ascending | apart
            merged = jnp.where(
                lower == ascending, jnp.minimum(keys, partner), jnp.maximum(keys, partner)
            )
            keys = jnp.where(apart, keys, merged) if size == CHUNK else merged
            distance //= 2
        size *= 2
    return keys


def plan_kernel(frame_rows, all_rows, nbr_ref, deg_ref, after_ref, near_ids, near_order, near_class, far_ids, far_order, far_class, full_ids, full_order, full_class):
    slots = nbr_ref.shape[0]
    first = lax.axis_index("feat") * 16
    at = lax.broadcasted_iota(jnp.int32, (8, LANES), 0) * LANES + lax.broadcasted_iota(
        jnp.int32, (8, LANES), 1
    )
    rows = pl.ds(pl.multiple_of(first, 8), 8)
    degree = deg_ref[rows, :]
    near, far = [], []
    near_count = jnp.zeros((8, LANES), jnp.int32)
    for j in range(slots):
        nbr = nbr_ref[j, rows, :]
        used = degree > j
        is_near = used & (nbr < frame_rows)
        near.append(jnp.where(is_near, nbr, all_rows))
        far.append(jnp.where(used & (nbr >= frame_rows), nbr, all_rows))
        near_count = near_count + is_near.astype(jnp.int32)
    for j, ids in enumerate(sort_network(near)):
        near_ids[j] = ids
    for j, ids in enumerate(sort_network(far)):
        far_ids[j] = ids
    rows = pl.ds(pl.multiple_of(first + 8, 8), 8)
    full_degree = deg_ref[rows, :]
    for j in range(slots):
        full_ids[j] = jnp.where(full_degree > j, nbr_ref[j, rows, :], all_rows)
    counts = (near_count, degree - near_count, full_degree)
    keys = sorted_tiles(jnp.stack([count * CHUNK + at for count in counts]), 2)
    for i, order in enumerate((near_order, far_order)):
        order[...] = keys[i] & (CHUNK - 1)
    full_order[...] = keys[2] & (CHUNK // 2 - 1)
    for i, classes in enumerate((near_class, far_class, full_class)):
        classes[...] = keys[i] >> 10


def constants_kernel(deg_ref, weight_ref, bias_ref, after_ref, scale_ref, weight_out, bias_out):
    tiles = scale_ref.shape[0] // LANES
    first = pl.multiple_of(lax.axis_index("feat") * tiles, tiles)
    inverse = 1.0 / (deg_ref[pl.ds(first, tiles), :] + 1).astype(jnp.float32)
    for t in range(tiles):
        scale_ref[LANES * t : LANES * (t + 1), :] = jnp.broadcast_to(
            inverse[t : t + 1, :], (LANES, LANES)
        ).T
    weight_out[...] = weight_ref[...].astype(jnp.float32).T.astype(jnp.bfloat16)
    bias_out[...] = jnp.broadcast_to(bias_ref[...], (LANES, LANES)).T


def add_tree(parts):
    while len(parts) > 1:
        tail = [parts[-1]] if len(parts) % 2 else []
        parts = [parts[i] + parts[i + 1] for i in range(0, len(parts) - 1, 2)] + tail
    return parts[0]


def load_plan(slots, start, ids_ref, order_ref, class_ref, slot_ids, order, classes, sem):
    size = order.shape[0]
    rows = pl.ds(start, size)
    first = [
        pltpu.make_async_copy(order_ref.at[rows], order, sem.at[slots]),
        pltpu.make_async_copy(class_ref.at[rows], classes.at[pl.ds(0, size)], sem.at[slots + 1]),
    ]
    by_slot = [
        pltpu.make_async_copy(
            ids_ref.at[pl.ds(j * CHUNK + start, size)], slot_ids.at[pl.ds(j * size, size)], sem.at[j]
        )
        for j in range(slots)
    ]
    for copy in first + by_slot:
        copy.start()
    return first, by_slot


def sum_slots(slots, start, part, parts, plan_refs, frame_ref, total_ref, slot_ids, order, classes, sem):
    size = order.shape[0]
    first, by_slot = load_plan(slots, start, *plan_refs, slot_ids, order, classes, sem)
    total_ref[...] = jnp.zeros_like(total_ref)
    for copy in first:
        copy.wait()
    last = GROUP - 1
    classes[size + part * GROUP + last] = slots + 1
    of_slot = [slot_ids.at[pl.ds(j * size, size)] for j in range(slots)]

    def body(count, carry):
        base, _ = carry
        for k in range(GROUP):
            node = order[base + k]
            total_ref[pl.ds(node, 1), :] = add_tree(
                [frame_ref[pl.ds(of_slot[j][node], 1), :] for j in range(count)]
            )
        return base + parts * GROUP, classes[base + parts * GROUP + last]

    def skip(carry):
        base, _ = carry
        return base + parts * GROUP, classes[base + parts * GROUP + last]

    carry = (jnp.int32(part * GROUP), classes[part * GROUP + last])
    carry = lax.while_loop(lambda carry: carry[1] == 0, skip, carry)
    for count in range(1, slots + 1):
        by_slot[count - 1].wait()
        carry = lax.while_loop(
            lambda carry, count=count: carry[1] == count, functools.partial(body, count), carry
        )


def near_kernel(slots, part, parts, ids_ref, order_ref, class_ref, frame_ref, after_ref, total_ref, *plan):
    sum_slots(slots, 0, part, parts, (ids_ref, order_ref, class_ref), frame_ref, total_ref, *plan)


def layer_kernel(slots, first, start, parts, own, ids_ref, order_ref, class_ref, frame_ref, scale_ref, weight_ref, bias_ref, after_ref, *refs):
    near, (keep_ref, send_ref, total_ref), plan = refs[:parts], refs[parts : parts + 3], refs[parts + 3 :]
    sum_slots(slots, start, 0, 1, (ids_ref, order_ref, class_ref), frame_ref, total_ref, *plan)
    chans, size = keep_ref.shape
    feat = lax.axis_index("feat")
    step = 256
    for at in range(0, size, step):
        rows = slice(at, at + step)
        own_at = pl.multiple_of(own + feat * own + first + at, step)
        total = total_ref[rows, :] + frame_ref[pl.ds(own_at, step), :]
        for ref in near:
            total = total + ref[rows, :]
        product = lax.dot_general(
            weight_ref[...],
            (total * scale_ref[first + at : first + at + step, :]).astype(jnp.bfloat16),
            (((1,), (1,)), ((), ())),
            preferred_element_type=jnp.float32,
        )
        bias = jnp.concatenate([bias_ref[...]] * (step // LANES), axis=1)
        result = jnp.maximum(product + bias, 0.0)
        low, high = result[:chans], result[chans:]
        keep_ref[:, rows] = jnp.where(feat == 0, low, high).astype(jnp.bfloat16)
        if send_ref.shape[0] == chans:
            result = jnp.where(feat == 0, high, low)
        send_ref[:, rows] = result.astype(jnp.bfloat16)


def output_kernel(*refs):
    out_ref = refs[-1]
    count = len(refs) // 2
    feat = lax.axis_index("feat")
    chans = out_ref.shape[0]
    for refs, part in ((refs[:count], feat), (refs[count:-1], 1 - feat)):
        at = part * (out_ref.shape[1] // 2)
        for ref in refs:
            size = ref.shape[1]
            rows = pl.ds(pl.multiple_of(feat * chans, chans), chans) if ref.shape[0] > chans else slice(None)
            out_ref[:, pl.ds(pl.multiple_of(at, size), size)] = ref[rows, :]
            at = at + size


def pallas(kernel, out_shape, in_specs, scratch=(), us=1.0, aliases=None):
    return pl.pallas_call(
        kernel,
        out_shape=out_shape,
        in_specs=in_specs,
        out_specs=jax.tree.map(lambda _: IN_VMEM, out_shape),
        scratch_shapes=list(scratch),
        input_output_aliases=aliases or {},
        compiler_params=pltpu.CompilerParams(vmem_limit_bytes=6 * 2**20),
        cost_estimate=pl.CostEstimate(flops=0, bytes_accessed=int(us * 3_000_000), transcendentals=0),
    )


IN_VMEM = pl.BlockSpec(memory_space=VMEM)
ANYWHERE = pl.BlockSpec(memory_space=pl.ANY)


def local(node_feats, neighbours, degrees, hub_rows, weight, bias_terms):
    chans, nodes = node_feats.shape
    slots = neighbours.shape[0]
    hubs = hub_rows.shape[0]
    slabs = lax.axis_size("slab")
    half = nodes // 2
    chunks = half // CHUNK
    frame_rows, hub_count = 2 * half + nodes, slabs * hubs
    swap = [(0, 1), (1, 0)]

    def bf16(*shape):
        return jax.ShapeDtypeStruct(shape, jnp.bfloat16)

    def f32(*shape):
        return jax.ShapeDtypeStruct(shape, jnp.float32)

    def i32(*shape):
        return jax.ShapeDtypeStruct(shape, jnp.int32)

    block = pallas(
        hub_pick_kernel,
        bf16(hubs // 2, 2 * chans),
        [IN_VMEM, ANYWHERE],
        [VMEM((chans, nodes), jnp.bfloat16), pltpu.SemaphoreType.DMA((4,))],
    )(hub_rows[None, :], node_feats)
    arrived = None

    def stage(block, bits):
        return [lax.ppermute(block, "slab", [(i, i ^ bit) for i in range(slabs)]) for bit in bits]

    def join(block, arrived, after):
        rows = block.shape[0] * (1 + len(arrived))
        specs = [IN_VMEM] * (1 + len(arrived)) + [ANYWHERE]
        return pallas(join_kernel, bf16(rows, 2 * chans), specs, us=0.5)(block, *arrived, after)

    arrived = stage(block, STAGES[0])
    deg_tiles = degrees.reshape(nodes // LANES, LANES)
    scale, by_out, bias = pallas(
        constants_kernel,
        (f32(half, LANES), bf16(2 * chans, 2 * chans), f32(LANES, LANES)),
        [IN_VMEM] * 3 + [ANYWHERE],
        us=1.0,
    )(deg_tiles, weight, bias_terms[None, :], block)
    other = lax.ppermute(node_feats, "feat", swap)

    block = join(block, arrived, scale)
    arrived = stage(block, STAGES[1])
    block = join(block, arrived, scale)
    arrived = lax.ppermute(block, "feat", swap)
    outer, inner = pallas(
        halves_kernel, (bf16(2 * chans, half),) * 2, [IN_VMEM, IN_VMEM, ANYWHERE], us=0.5
    )(node_feats, other, block)
    block = pallas(
        join_feat_kernel, bf16(2 * block.shape[0], 2 * chans), [IN_VMEM, IN_VMEM, ANYWHERE], us=0.5
    )(block, arrived, outer)
    arrived = stage(block, STAGES[2])
    inner_halo = lax.ppermute(inner, "slab", [(i, i ^ 1) for i in range(slabs)])
    outer_halo = lax.ppermute(
        outer, "slab", [(i, j) for i in range(slabs) for j in [i + 2 * (i & 1) - 1] if 0 <= j < slabs]
    )
    table, tile = i32(slots, 8, LANES), i32(8, LANES)
    plan = pallas(
        functools.partial(plan_kernel, frame_rows, frame_rows + hub_count),
        (table, tile, tile) * 3,
        [IN_VMEM, IN_VMEM, ANYWHERE],
        us=4.0,
    )(neighbours.reshape(slots, nodes // LANES, LANES), deg_tiles, block)
    plan = [a.reshape(-1) for a in plan]
    near_plan, far_plan, full_plan = plan[:3], plan[3:6], plan[6:]
    frame = pallas(
        frame_kernel,
        f32(frame_rows + hub_count + 8, LANES),
        [IN_VMEM] * 4 + [ANYWHERE],
        us=2.0,
    )(outer_halo, outer, inner, inner_halo, near_plan[1])

    def plan_scratch(size):
        return [
            SMEM((slots * size,), jnp.int32),
            SMEM((size,), jnp.int32),
            SMEM((size + 2 * GROUP,), jnp.int32),
            pltpu.SemaphoreType.DMA((slots + 2,)),
        ]

    def near_sum(part, after):
        return pallas(
            functools.partial(near_kernel, slots, part, 2),
            f32(CHUNK, LANES),
            [ANYWHERE] * 3 + [IN_VMEM, ANYWHERE],
            plan_scratch(CHUNK),
            us=4.0,
        )(*near_plan, frame, after)

    near = [near_sum(0, block)]
    block = join(block, arrived, near[0])
    arrived = stage(block, STAGES[3])
    near.append(near_sum(1, block))
    block = join(block, arrived, near[1])
    arrived = stage(block, STAGES[4])
    frame = pallas(
        functools.partial(hub_frame_kernel, frame_rows, hubs),
        f32(*frame.shape),
        [IN_VMEM] * 3 + [ANYWHERE],
        us=0.5,
        aliases={0: 0},
    )(frame, block, arrived[0], near[1])

    def layer(plan, first, start, size, sent_chans, near, after, us):
        return pallas(
            functools.partial(layer_kernel, slots, first, start, len(near), half),
            (bf16(chans, size), bf16(sent_chans, size)),
            [ANYWHERE] * 3 + [IN_VMEM] * 4 + [ANYWHERE] + [IN_VMEM] * len(near),
            [VMEM((size, LANES), jnp.float32)] + plan_scratch(size),
            us=us,
        )(*plan, frame, scale, by_out, bias, after, *near)

    keep, received = [hub_rows], []
    for plan, first, start, size, sent_chans, near, us in (
        (far_plan, 0, 0, CHUNK, 2 * chans, near, 3.0),
        (full_plan, CHUNK, 0, CHUNK // 2, 2 * chans, [], 4.0),
        (full_plan, CHUNK + CHUNK // 2, CHUNK // 2, CHUNK // 2, chans, [], 4.0),
    ):
        kept, sent = layer(plan, first, start, size, sent_chans, near, keep[-1], us)
        keep.append(kept)
        received.append(lax.ppermute(sent, "feat", swap))
    pieces = keep[1:] + received
    return pallas(output_kernel, bf16(chans, nodes), [IN_VMEM] * len(pieces), us=0.5)(*pieces)


def solution(mesh):
    in_specs = (P("feat", "slab"), P(None, "slab"), P("slab"), P("slab"), P(), P())
    return jax.shard_map(local, mesh=mesh, in_specs=in_specs, out_specs=P("feat", "slab"), check_vma=False)
```

```python
import functools

import jax
import jax.numpy as jnp
from jax import lax
from jax.experimental import pallas as pl
from jax.experimental.pallas import tpu as pltpu
from jax.sharding import PartitionSpec as P

VMEM = pltpu.VMEM
SMEM = pltpu.SMEM
LANES = 128
CHUNK = 1024
GROUP = 16
STAGES = ((32,), (8, 16, 24), (64,), (2, 4, 6), (1,))


def hub_pick_kernel(rows_ref, x_hbm, out_ref, x_ref, sem):
    hubs, nodes = rows_ref.shape[1], x_ref.shape[1]
    parts = sem.shape[0]
    copies = [
        pltpu.make_async_copy(x_hbm.at[:, part], x_ref.at[:, part], sem.at[i])
        for i in range(parts)
        for part in [pl.ds(i * (nodes // parts), nodes // parts)]
    ]
    for copy in copies:
        copy.start()
    diagonal = lax.broadcasted_iota(jnp.int32, (hubs, hubs), 0) == lax.broadcasted_iota(
        jnp.int32, (hubs, hubs), 1
    )
    rows = jnp.sum(jnp.where(diagonal, rows_ref[...], 0), axis=1, keepdims=True)
    onehot = (lax.broadcasted_iota(jnp.int32, (hubs, nodes), 1) == rows).astype(jnp.bfloat16)
    for copy in copies:
        copy.wait()
    picked = lax.dot_general(
        onehot, x_ref[...], (((1,), (1,)), ((), ())), preferred_element_type=jnp.float32
    ).astype(jnp.bfloat16)
    out_ref[...] = jnp.concatenate([picked[: hubs // 2], picked[hubs // 2 :]], axis=1)


def join_kernel(*refs):
    blocks, out_ref = refs[:-2], refs[-1]
    rows = blocks[0].shape[0]
    for i, ref in enumerate(blocks):
        out_ref[i * rows : (i + 1) * rows] = ref[...]


def join_feat_kernel(mine_ref, other_ref, out_ref):
    first = lax.axis_index("feat") == 0
    lane = lax.broadcasted_iota(jnp.int32, (16, LANES), 1)
    for i in range(mine_ref.shape[0] // 16):
        mine = mine_ref[16 * i : 16 * i + 16, :].astype(jnp.float32)
        other = other_ref[16 * i : 16 * i + 16, :].astype(jnp.float32)
        low = jnp.where(first, mine, other)
        high = jnp.where(first, other, mine)
        row = jnp.where(lane < LANES // 2, low, pltpu.roll(high, LANES // 2, 1))
        out_ref[32 * i : 32 * i + 16, :] = row.astype(jnp.bfloat16)
        row = jnp.where(lane < LANES // 2, pltpu.roll(low, LANES // 2, 1), high)
        out_ref[32 * i + 16 : 32 * i + 32, :] = row.astype(jnp.bfloat16)


def halves_kernel(x_ref, other_ref, after_ref, outer_ref, inner_ref, sem):
    feat = lax.axis_index("feat")
    odd = lax.axis_index("slab") & 1
    chans, half = x_ref.shape[0], outer_ref.shape[1]
    copies = []
    for ref, channels in ((x_ref, feat), (other_ref, 1 - feat)):
        rows = pl.ds(pl.multiple_of(channels * chans, chans), chans)
        for out_ref, part in ((outer_ref, odd), (inner_ref, 1 - odd)):
            cols = pl.ds(pl.multiple_of(part * half, half), half)
            copies.append(
                pltpu.make_async_copy(ref.at[:, cols], out_ref.at[rows, :], sem.at[len(copies)])
            )
    for copy in copies:
        copy.start()
    for copy in copies:
        copy.wait()


def frame_kernel(outer_halo_ref, outer_ref, inner_ref, inner_halo_ref, after_ref, frame_ref):
    odd = lax.axis_index("slab") & 1
    half = outer_ref.shape[1]
    step = 256
    unit = (
        lax.broadcasted_iota(jnp.int32, (step, step), 0)
        == lax.broadcasted_iota(jnp.int32, (step, step), 1)
    ).astype(jnp.bfloat16)
    for place, ref in enumerate((outer_halo_ref, outer_ref, inner_ref, inner_halo_ref)):
        first = (place + odd * (3 - 2 * place)) * half
        for at in range(0, half, step):
            frame_ref[pl.ds(pl.multiple_of(first + at, step), step), :] = lax.dot_general(
                unit,
                ref[:, at : at + step],
                (((1,), (1,)), ((), ())),
                preferred_element_type=jnp.float32,
            )
    rows = frame_ref.shape[0]
    frame_ref[rows - 8 :, :] = jnp.zeros((8, LANES), jnp.float32)


def origins():
    differs = [0]
    for bits in STAGES:
        differs = [d ^ bit for bit in (0,) + bits for d in differs]
    return differs


def hub_frame_kernel(first, hubs, frame_in, near_ref, far_ref, after_ref, frame_ref):
    blocks = near_ref.shape[0] // hubs
    me = lax.axis_index("slab")
    for p, differs in enumerate(origins()):
        ref, i = (near_ref, p) if p < blocks else (far_ref, p - blocks)
        at = pl.multiple_of(first + (me ^ differs) * hubs, hubs)
        frame_ref[pl.ds(at, hubs), :] = ref[hubs * i : hubs * (i + 1), :].astype(jnp.float32)


def comparators(count):
    pairs, p = [], 1
    while p < count:
        k = p
        while k >= 1:
            for j in range(k % p, count - k, 2 * k):
                for i in range(min(k, count - j - k)):
                    if (i + j) // (2 * p) == (i + j + k) // (2 * p):
                        pairs.append((i + j, i + j + k))
            k //= 2
        p *= 2
    return pairs


def sort_network(values):
    for a, b in comparators(len(values)):
        values[a], values[b] = jnp.minimum(values[a], values[b]), jnp.maximum(values[a], values[b])
    return values


def sorted_tiles(keys, halved):
    shape = keys.shape
    apart = lax.broadcasted_iota(jnp.int32, shape, 0) == halved
    sub = lax.broadcasted_iota(jnp.int32, shape, 1)
    lane = lax.broadcasted_iota(jnp.int32, shape, 2)
    at = sub * LANES + lane
    size = 2
    while size <= CHUNK:
        distance = size // 2
        while distance >= 1:
            axis, by, extent = (2, distance, LANES) if distance < LANES else (1, distance // LANES, 8)
            lower = (at & distance) == 0
            partner = jnp.where(
                lower, pltpu.roll(keys, extent - by, axis), pltpu.roll(keys, by, axis)
            )
            ascending = (at & size) == 0
            if 2 * size == CHUNK:
                ascending = ascending | apart
            merged = jnp.where(
                lower == ascending, jnp.minimum(keys, partner), jnp.maximum(keys, partner)
            )
            keys = jnp.where(apart, keys, merged) if size == CHUNK else merged
            distance //= 2
        size *= 2
    return keys


def plan_kernel(frame_rows, all_rows, nbr_ref, deg_ref, after_ref, near_ids, near_order, near_class, far_ids, far_order, far_class, full_ids, full_order, full_class):
    slots = nbr_ref.shape[0]
    first = lax.axis_index("feat") * 16
    at = lax.broadcasted_iota(jnp.int32, (8, LANES), 0) * LANES + lax.broadcasted_iota(
        jnp.int32, (8, LANES), 1
    )
    rows = pl.ds(pl.multiple_of(first, 8), 8)
    degree = deg_ref[rows, :]
    near, far = [], []
    near_count = jnp.zeros((8, LANES), jnp.int32)
    for j in range(slots):
        nbr = nbr_ref[j, rows, :]
        used = degree > j
        is_near = used & (nbr < frame_rows)
        near.append(jnp.where(is_near, nbr, all_rows))
        far.append(jnp.where(used & (nbr >= frame_rows), nbr, all_rows))
        near_count = near_count + is_near.astype(jnp.int32)
    for j, ids in enumerate(sort_network(near)):
        near_ids[j] = ids
    for j, ids in enumerate(sort_network(far)):
        far_ids[j] = ids
    rows = pl.ds(pl.multiple_of(first + 8, 8), 8)
    full_degree = deg_ref[rows, :]
    for j in range(slots):
        full_ids[j] = jnp.where(full_degree > j, nbr_ref[j, rows, :], all_rows)
    counts = (near_count, degree - near_count, full_degree)
    keys = sorted_tiles(jnp.stack([count * CHUNK + at for count in counts]), 2)
    for i, order in enumerate((near_order, far_order)):
        order[...] = keys[i] & (CHUNK - 1)
    full_order[...] = keys[2] & (CHUNK // 2 - 1)
    for i, classes in enumerate((near_class, far_class, full_class)):
        classes[...] = keys[i] >> 10


def constants_kernel(deg_ref, weight_ref, bias_ref, after_ref, scale_ref, weight_out, bias_out):
    tiles = scale_ref.shape[0] // LANES
    first = pl.multiple_of(lax.axis_index("feat") * tiles, tiles)
    inverse = 1.0 / (deg_ref[pl.ds(first, tiles), :] + 1).astype(jnp.float32)
    for t in range(tiles):
        scale_ref[LANES * t : LANES * (t + 1), :] = jnp.broadcast_to(
            inverse[t : t + 1, :], (LANES, LANES)
        ).T
    weight_out[...] = weight_ref[...].astype(jnp.float32).T.astype(jnp.bfloat16)
    bias_out[...] = jnp.broadcast_to(bias_ref[...], (LANES, LANES)).T


def add_tree(parts):
    while len(parts) > 1:
        tail = [parts[-1]] if len(parts) % 2 else []
        parts = [parts[i] + parts[i + 1] for i in range(0, len(parts) - 1, 2)] + tail
    return parts[0]


def load_plan(slots, start, ids_ref, order_ref, class_ref, slot_ids, order, classes, sem):
    size = order.shape[0]
    rows = pl.ds(start, size)
    first = [
        pltpu.make_async_copy(order_ref.at[rows], order, sem.at[slots]),
        pltpu.make_async_copy(class_ref.at[rows], classes.at[pl.ds(0, size)], sem.at[slots + 1]),
    ]
    by_slot = [
        pltpu.make_async_copy(
            ids_ref.at[pl.ds(j * CHUNK + start, size)], slot_ids.at[pl.ds(j * size, size)], sem.at[j]
        )
        for j in range(slots)
    ]
    for copy in first + by_slot:
        copy.start()
    return first, by_slot


def sum_slots(slots, start, part, parts, plan_refs, frame_ref, total_ref, slot_ids, order, classes, sem):
    size = order.shape[0]
    first, by_slot = load_plan(slots, start, *plan_refs, slot_ids, order, classes, sem)
    total_ref[...] = jnp.zeros_like(total_ref)
    for copy in first:
        copy.wait()
    last = GROUP - 1
    classes[size + part * GROUP + last] = slots + 1
    of_slot = [slot_ids.at[pl.ds(j * size, size)] for j in range(slots)]

    def body(count, carry):
        base, _ = carry
        for k in range(GROUP):
            node = order[base + k]
            total_ref[pl.ds(node, 1), :] = add_tree(
                [frame_ref[pl.ds(of_slot[j][node], 1), :] for j in range(count)]
            )
        return base + parts * GROUP, classes[base + parts * GROUP + last]

    def skip(carry):
        base, _ = carry
        return base + parts * GROUP, classes[base + parts * GROUP + last]

    carry = (jnp.int32(part * GROUP), classes[part * GROUP + last])
    carry = lax.while_loop(lambda carry: carry[1] == 0, skip, carry)
    for count in range(1, slots + 1):
        by_slot[count - 1].wait()
        carry = lax.while_loop(
            lambda carry, count=count: carry[1] == count, functools.partial(body, count), carry
        )


def near_kernel(slots, part, parts, ids_ref, order_ref, class_ref, frame_ref, after_ref, total_ref, *plan):
    sum_slots(slots, 0, part, parts, (ids_ref, order_ref, class_ref), frame_ref, total_ref, *plan)


def layer_kernel(slots, first, start, parts, own, ids_ref, order_ref, class_ref, frame_ref, scale_ref, weight_ref, bias_ref, after_ref, *refs):
    near, (keep_ref, send_ref, total_ref), plan = refs[:parts], refs[parts : parts + 3], refs[parts + 3 :]
    sum_slots(slots, start, 0, 1, (ids_ref, order_ref, class_ref), frame_ref, total_ref, *plan)
    chans, size = keep_ref.shape
    feat = lax.axis_index("feat")
    step = 256
    for at in range(0, size, step):
        rows = slice(at, at + step)
        own_at = pl.multiple_of(own + feat * own + first + at, step)
        total = total_ref[rows, :] + frame_ref[pl.ds(own_at, step), :]
        for ref in near:
            total = total + ref[rows, :]
        product = lax.dot_general(
            weight_ref[...],
            (total * scale_ref[first + at : first + at + step, :]).astype(jnp.bfloat16),
            (((1,), (1,)), ((), ())),
            preferred_element_type=jnp.float32,
        )
        bias = jnp.concatenate([bias_ref[...]] * (step // LANES), axis=1)
        result = jnp.maximum(product + bias, 0.0)
        low, high = result[:chans], result[chans:]
        keep_ref[:, rows] = jnp.where(feat == 0, low, high).astype(jnp.bfloat16)
        if send_ref.shape[0] == chans:
            result = jnp.where(feat == 0, high, low)
        send_ref[:, rows] = result.astype(jnp.bfloat16)


def output_kernel(*refs):
    out_ref = refs[-1]
    count = len(refs) // 2
    feat = lax.axis_index("feat")
    chans = out_ref.shape[0]
    for refs, part in ((refs[:count], feat), (refs[count:-1], 1 - feat)):
        at = part * (out_ref.shape[1] // 2)
        for ref in refs:
            size = ref.shape[1]
            rows = pl.ds(pl.multiple_of(feat * chans, chans), chans) if ref.shape[0] > chans else slice(None)
            out_ref[:, pl.ds(pl.multiple_of(at, size), size)] = ref[rows, :]
            at = at + size


def pallas(kernel, out_shape, in_specs, scratch=(), us=1.0, aliases=None):
    return pl.pallas_call(
        kernel,
        out_shape=out_shape,
        in_specs=in_specs,
        out_specs=jax.tree.map(lambda _: IN_VMEM, out_shape),
        scratch_shapes=list(scratch),
        input_output_aliases=aliases or {},
        compiler_params=pltpu.CompilerParams(vmem_limit_bytes=6 * 2**20),
        cost_estimate=pl.CostEstimate(flops=0, bytes_accessed=int(us * 3_000_000), transcendentals=0),
    )


IN_VMEM = pl.BlockSpec(memory_space=VMEM)
ANYWHERE = pl.BlockSpec(memory_space=pl.ANY)
IN_HBM = pl.BlockSpec(memory_space=pltpu.HBM)


def local(node_feats, neighbours, degrees, hub_rows, weight, bias_terms):
    chans, nodes = node_feats.shape
    slots = neighbours.shape[0]
    hubs = hub_rows.shape[0]
    slabs = lax.axis_size("slab")
    half = nodes // 2
    chunks = half // CHUNK
    frame_rows, hub_count = 2 * half + nodes, slabs * hubs
    swap = [(0, 1), (1, 0)]

    def bf16(*shape):
        return jax.ShapeDtypeStruct(shape, jnp.bfloat16)

    def f32(*shape):
        return jax.ShapeDtypeStruct(shape, jnp.float32)

    def i32(*shape):
        return jax.ShapeDtypeStruct(shape, jnp.int32)

    block = pallas(
        hub_pick_kernel,
        bf16(hubs // 2, 2 * chans),
        [IN_VMEM, IN_HBM],
        [VMEM((chans, nodes), jnp.bfloat16), pltpu.SemaphoreType.DMA((4,))],
    )(hub_rows[None, :], node_feats)
    arrived = None

    def stage(block, bits):
        return [lax.ppermute(block, "slab", [(i, i ^ bit) for i in range(slabs)]) for bit in bits]

    def join(block, arrived, after):
        rows = block.shape[0] * (1 + len(arrived))
        specs = [IN_VMEM] * (1 + len(arrived)) + [ANYWHERE]
        return pallas(join_kernel, bf16(rows, 2 * chans), specs, us=0.5)(block, *arrived, after)

    arrived = stage(block, STAGES[0])
    deg_tiles = degrees.reshape(nodes // LANES, LANES)
    table, tile = i32(slots, 8, LANES), i32(8, LANES)
    plan = pallas(
        functools.partial(plan_kernel, frame_rows, frame_rows + hub_count),
        (table, tile, tile) * 3,
        [IN_VMEM, IN_VMEM, ANYWHERE],
        us=4.0,
    )(neighbours.reshape(slots, nodes // LANES, LANES), deg_tiles, block)
    plan = [a.reshape(-1) for a in plan]
    near_plan, far_plan, full_plan = plan[:3], plan[3:6], plan[6:]
    other = lax.ppermute(node_feats, "feat", swap)

    block = join(block, arrived, near_plan[1])
    arrived = stage(block, STAGES[1])
    scale, by_out, bias = pallas(
        constants_kernel,
        (f32(half, LANES), bf16(2 * chans, 2 * chans), f32(LANES, LANES)),
        [IN_VMEM] * 3 + [ANYWHERE],
        us=1.0,
    )(deg_tiles, weight, bias_terms[None, :], block)

    block = join(block, arrived, scale)
    arrived = lax.ppermute(block, "feat", swap)
    block = pallas(
        join_feat_kernel, bf16(2 * block.shape[0], 2 * chans), [IN_VMEM] * 2, us=0.5
    )(block, arrived)
    arrived = stage(block, STAGES[2])
    outer, inner = pallas(
        halves_kernel,
        (bf16(2 * chans, half),) * 2,
        [IN_HBM, ANYWHERE, ANYWHERE],
        [pltpu.SemaphoreType.DMA((4,))],
        us=0.5,
    )(node_feats, other, block)
    inner_halo = lax.ppermute(inner, "slab", [(i, i ^ 1) for i in range(slabs)])
    outer_halo = lax.ppermute(
        outer, "slab", [(i, j) for i in range(slabs) for j in [i + 2 * (i & 1) - 1] if 0 <= j < slabs]
    )
    block = join(block, arrived, outer)
    arrived = stage(block, STAGES[3])
    frame = pallas(
        frame_kernel,
        f32(frame_rows + hub_count + 8, LANES),
        [IN_VMEM] * 4 + [ANYWHERE],
        us=2.0,
    )(outer_halo, outer, inner, inner_halo, block)

    def plan_scratch(size):
        return [
            SMEM((slots * size,), jnp.int32),
            SMEM((size,), jnp.int32),
            SMEM((size + 2 * GROUP,), jnp.int32),
            pltpu.SemaphoreType.DMA((slots + 2,)),
        ]

    def near_sum(part, after):
        return pallas(
            functools.partial(near_kernel, slots, part, 2),
            f32(CHUNK, LANES),
            [ANYWHERE] * 3 + [IN_VMEM, ANYWHERE],
            plan_scratch(CHUNK),
            us=4.0,
        )(*near_plan, frame, after)

    near = [near_sum(0, block)]
    block = join(block, arrived, near[0])
    arrived = stage(block, STAGES[4])
    near.append(near_sum(1, block))
    frame = pallas(
        functools.partial(hub_frame_kernel, frame_rows, hubs),
        f32(*frame.shape),
        [IN_VMEM] * 3 + [ANYWHERE],
        us=0.5,
        aliases={0: 0},
    )(frame, block, arrived[0], near[1])

    def layer(plan, first, start, size, sent_chans, near, after, us):
        return pallas(
            functools.partial(layer_kernel, slots, first, start, len(near), half),
            (bf16(chans, size), bf16(sent_chans, size)),
            [ANYWHERE] * 3 + [IN_VMEM] * 4 + [ANYWHERE] + [IN_VMEM] * len(near),
            [VMEM((size, LANES), jnp.float32)] + plan_scratch(size),
            us=us,
        )(*plan, frame, scale, by_out, bias, after, *near)

    keep, received = [hub_rows], []
    for plan, first, start, size, sent_chans, near, us in (
        (far_plan, 0, 0, CHUNK, 2 * chans, near, 3.0),
        (full_plan, CHUNK, 0, CHUNK // 2, 2 * chans, [], 4.0),
        (full_plan, CHUNK + CHUNK // 2, CHUNK // 2, CHUNK // 2, chans, [], 4.0),
    ):
        kept, sent = layer(plan, first, start, size, sent_chans, near, keep[-1], us)
        keep.append(kept)
        received.append(lax.ppermute(sent, "feat", swap))
    pieces = keep[1:] + received
    return pallas(output_kernel, bf16(chans, nodes), [IN_VMEM] * len(pieces), us=0.5)(*pieces)


def solution(mesh):
    in_specs = (P("feat", "slab"), P(None, "slab"), P("slab"), P("slab"), P(), P())
    return jax.shard_map(local, mesh=mesh, in_specs=in_specs, out_specs=P("feat", "slab"), check_vma=False)
```

```python
import functools

import jax
import jax.numpy as jnp
from jax import lax
from jax.experimental import pallas as pl
from jax.experimental.pallas import tpu as pltpu
from jax.sharding import PartitionSpec as P

VMEM = pltpu.VMEM
SMEM = pltpu.SMEM
LANES = 128
CHUNK = 1024
GROUP = 16
STAGES = ((32,), (8, 16, 24), (64,), (2, 4, 6), (1,))


def hub_pick_kernel(rows_ref, x_hbm, out_ref, x_ref, sem):
    hubs, nodes = rows_ref.shape[1], x_ref.shape[1]
    parts = sem.shape[0]
    copies = [
        pltpu.make_async_copy(x_hbm.at[:, part], x_ref.at[:, part], sem.at[i])
        for i in range(parts)
        for part in [pl.ds(i * (nodes // parts), nodes // parts)]
    ]
    for copy in copies:
        copy.start()
    diagonal = lax.broadcasted_iota(jnp.int32, (hubs, hubs), 0) == lax.broadcasted_iota(
        jnp.int32, (hubs, hubs), 1
    )
    rows = jnp.sum(jnp.where(diagonal, rows_ref[...], 0), axis=1, keepdims=True)
    onehot = (lax.broadcasted_iota(jnp.int32, (hubs, nodes), 1) == rows).astype(jnp.bfloat16)
    for copy in copies:
        copy.wait()
    picked = lax.dot_general(
        onehot, x_ref[...], (((1,), (1,)), ((), ())), preferred_element_type=jnp.float32
    ).astype(jnp.bfloat16)
    out_ref[...] = jnp.concatenate([picked[: hubs // 2], picked[hubs // 2 :]], axis=1)


def join_kernel(count, *refs):
    blocks, out_ref = refs[:count], refs[-1]
    rows = blocks[0].shape[0]
    for i, ref in enumerate(blocks):
        out_ref[i * rows : (i + 1) * rows] = ref[...]


def join_feat_kernel(mine_ref, other_ref, after_ref, out_ref):
    first = lax.axis_index("feat") == 0
    lane = lax.broadcasted_iota(jnp.int32, (16, LANES), 1)
    for i in range(mine_ref.shape[0] // 16):
        mine = mine_ref[16 * i : 16 * i + 16, :].astype(jnp.float32)
        other = other_ref[16 * i : 16 * i + 16, :].astype(jnp.float32)
        low = jnp.where(first, mine, other)
        high = jnp.where(first, other, mine)
        row = jnp.where(lane < LANES // 2, low, pltpu.roll(high, LANES // 2, 1))
        out_ref[32 * i : 32 * i + 16, :] = row.astype(jnp.bfloat16)
        row = jnp.where(lane < LANES // 2, pltpu.roll(low, LANES // 2, 1), high)
        out_ref[32 * i + 16 : 32 * i + 32, :] = row.astype(jnp.bfloat16)


def outer_half_kernel(x_ref, after_ref, outer_ref, sem):
    half = outer_ref.shape[1]
    part = lax.axis_index("slab") & 1
    copy = pltpu.make_async_copy(
        x_ref.at[:, pl.ds(pl.multiple_of(part * half, half), half)], outer_ref, sem
    )
    copy.start()
    copy.wait()


def inner_half_kernel(x_ref, other_ref, after_ref, inner_ref, sem):
    feat = lax.axis_index("feat")
    part = 1 - (lax.axis_index("slab") & 1)
    chans, half = x_ref.shape[0], inner_ref.shape[1]
    copies = [
        pltpu.make_async_copy(
            ref.at[:, pl.ds(pl.multiple_of(part * half, half), half)],
            inner_ref.at[pl.ds(pl.multiple_of(channels * chans, chans), chans), :],
            sem.at[i],
        )
        for i, (ref, channels) in enumerate(((x_ref, feat), (other_ref, 1 - feat)))
    ]
    for copy in copies:
        copy.start()
    for copy in copies:
        copy.wait()


def frame_kernel(x_ref, outer_ref, other_x_ref, other_outer_ref, inner_ref, after_ref, frame_ref):
    odd = lax.axis_index("slab") & 1
    first = lax.axis_index("feat") == 0
    half, nodes = outer_ref.shape[1], x_ref.shape[1]
    step = 256
    unit = (
        lax.broadcasted_iota(jnp.int32, (step, step), 0)
        == lax.broadcasted_iota(jnp.int32, (step, step), 1)
    ).astype(jnp.bfloat16)

    def fill(place, *refs):
        for at in range(0, refs[0].shape[1], step):
            columns = refs[0][:, at : at + step]
            if len(refs) == 2:
                other = refs[1][:, at : at + step]
                columns = jnp.concatenate(
                    [jnp.where(first, columns, other), jnp.where(first, other, columns)], axis=0
                )
            frame_ref[pl.ds(pl.multiple_of(place + at, step), step), :] = lax.dot_general(
                unit, columns, (((1,), (1,)), ((), ())), preferred_element_type=jnp.float32
            )

    fill(odd * (half + nodes), outer_ref, other_outer_ref)
    fill(half, x_ref, other_x_ref)
    fill((1 - odd) * (half + nodes), inner_ref)
    rows = frame_ref.shape[0]
    frame_ref[rows - 8 :, :] = jnp.zeros((8, LANES), jnp.float32)


def origins():
    differs = [0]
    for bits in STAGES:
        differs = [d ^ bit for bit in (0,) + bits for d in differs]
    return differs


def hub_frame_kernel(first, hubs, frame_in, near_ref, far_ref, after_ref, frame_ref):
    blocks = near_ref.shape[0] // hubs
    me = lax.axis_index("slab")
    for p, differs in enumerate(origins()):
        ref, i = (near_ref, p) if p < blocks else (far_ref, p - blocks)
        at = pl.multiple_of(first + (me ^ differs) * hubs, hubs)
        frame_ref[pl.ds(at, hubs), :] = ref[hubs * i : hubs * (i + 1), :].astype(jnp.float32)


def comparators(count):
    pairs, p = [], 1
    while p < count:
        k = p
        while k >= 1:
            for j in range(k % p, count - k, 2 * k):
                for i in range(min(k, count - j - k)):
                    if (i + j) // (2 * p) == (i + j + k) // (2 * p):
                        pairs.append((i + j, i + j + k))
            k //= 2
        p *= 2
    return pairs


def sort_network(values):
    for a, b in comparators(len(values)):
        values[a], values[b] = jnp.minimum(values[a], values[b]), jnp.maximum(values[a], values[b])
    return values


def sorted_tiles(keys, halved):
    shape = keys.shape
    apart = lax.broadcasted_iota(jnp.int32, shape, 0) == halved
    sub = lax.broadcasted_iota(jnp.int32, shape, 1)
    lane = lax.broadcasted_iota(jnp.int32, shape, 2)
    at = sub * LANES + lane
    size = 2
    while size <= CHUNK:
        distance = size // 2
        while distance >= 1:
            axis, by, extent = (2, distance, LANES) if distance < LANES else (1, distance // LANES, 8)
            lower = (at & distance) == 0
            partner = jnp.where(
                lower, pltpu.roll(keys, extent - by, axis), pltpu.roll(keys, by, axis)
            )
            ascending = (at & size) == 0
            if 2 * size == CHUNK:
                ascending = ascending | apart
            merged = jnp.where(
                lower == ascending, jnp.minimum(keys, partner), jnp.maximum(keys, partner)
            )
            keys = jnp.where(apart, keys, merged) if size == CHUNK else merged
            distance //= 2
        size *= 2
    return keys


def plan_kernel(frame_rows, all_rows, nbr_ref, deg_ref, after_ref, near_ids, near_order, near_class, far_ids, far_order, far_class, full_ids, full_order, full_class):
    slots = nbr_ref.shape[0]
    first = lax.axis_index("feat") * 16
    at = lax.broadcasted_iota(jnp.int32, (8, LANES), 0) * LANES + lax.broadcasted_iota(
        jnp.int32, (8, LANES), 1
    )
    rows = pl.ds(pl.multiple_of(first, 8), 8)
    degree = deg_ref[rows, :]
    near, far = [], []
    near_count = jnp.zeros((8, LANES), jnp.int32)
    for j in range(slots):
        nbr = nbr_ref[j, rows, :]
        used = degree > j
        is_near = used & (nbr < frame_rows)
        near.append(jnp.where(is_near, nbr, all_rows))
        far.append(jnp.where(used & (nbr >= frame_rows), nbr, all_rows))
        near_count = near_count + is_near.astype(jnp.int32)
    for j, ids in enumerate(sort_network(near)):
        near_ids[j] = ids
    for j, ids in enumerate(sort_network(far)):
        far_ids[j] = ids
    rows = pl.ds(pl.multiple_of(first + 8, 8), 8)
    full_degree = deg_ref[rows, :]
    for j in range(slots):
        full_ids[j] = jnp.where(full_degree > j, nbr_ref[j, rows, :], all_rows)
    counts = (near_count, degree - near_count, full_degree)
    keys = sorted_tiles(jnp.stack([count * CHUNK + at for count in counts]), 2)
    for i, order in enumerate((near_order, far_order)):
        order[...] = keys[i] & (CHUNK - 1)
    full_order[...] = keys[2] & (CHUNK // 2 - 1)
    for i, classes in enumerate((near_class, far_class, full_class)):
        classes[...] = keys[i] >> 10


def constants_kernel(deg_ref, weight_ref, bias_ref, after_ref, scale_ref, weight_out, bias_out):
    tiles = scale_ref.shape[0] // LANES
    first = pl.multiple_of(lax.axis_index("feat") * tiles, tiles)
    inverse = 1.0 / (deg_ref[pl.ds(first, tiles), :] + 1).astype(jnp.float32)
    for t in range(tiles):
        scale_ref[LANES * t : LANES * (t + 1), :] = jnp.broadcast_to(
            inverse[t : t + 1, :], (LANES, LANES)
        ).T
    weight_out[...] = weight_ref[...].astype(jnp.float32).T.astype(jnp.bfloat16)
    bias_out[...] = jnp.broadcast_to(bias_ref[...], (LANES, LANES)).T


def add_tree(parts):
    while len(parts) > 1:
        tail = [parts[-1]] if len(parts) % 2 else []
        parts = [parts[i] + parts[i + 1] for i in range(0, len(parts) - 1, 2)] + tail
    return parts[0]


def load_plan(slots, start, ids_ref, order_ref, class_ref, slot_ids, order, classes, sem):
    size = order.shape[0]
    rows = pl.ds(start, size)
    first = [
        pltpu.make_async_copy(order_ref.at[rows], order, sem.at[slots]),
        pltpu.make_async_copy(class_ref.at[rows], classes.at[pl.ds(0, size)], sem.at[slots + 1]),
    ]
    by_slot = [
        pltpu.make_async_copy(
            ids_ref.at[pl.ds(j * CHUNK + start, size)], slot_ids.at[pl.ds(j * size, size)], sem.at[j]
        )
        for j in range(slots)
    ]
    for copy in first + by_slot:
        copy.start()
    return first, by_slot


def sum_slots(slots, start, part, parts, plan_refs, frame_ref, total_ref, slot_ids, order, classes, sem):
    size = order.shape[0]
    first, by_slot = load_plan(slots, start, *plan_refs, slot_ids, order, classes, sem)
    total_ref[...] = jnp.zeros_like(total_ref)
    for copy in first:
        copy.wait()
    last = GROUP - 1
    classes[size + part * GROUP + last] = slots + 1
    of_slot = [slot_ids.at[pl.ds(j * size, size)] for j in range(slots)]

    def body(count, carry):
        base, _ = carry
        for k in range(GROUP):
            node = order[base + k]
            total_ref[pl.ds(node, 1), :] = add_tree(
                [frame_ref[pl.ds(of_slot[j][node], 1), :] for j in range(count)]
            )
        return base + parts * GROUP, classes[base + parts * GROUP + last]

    def skip(carry):
        base, _ = carry
        return base + parts * GROUP, classes[base + parts * GROUP + last]

    carry = (jnp.int32(part * GROUP), classes[part * GROUP + last])
    carry = lax.while_loop(lambda carry: carry[1] == 0, skip, carry)
    for count in range(1, slots + 1):
        by_slot[count - 1].wait()
        carry = lax.while_loop(
            lambda carry, count=count: carry[1] == count, functools.partial(body, count), carry
        )


def near_kernel(slots, part, parts, ids_ref, order_ref, class_ref, frame_ref, after_ref, total_ref, *plan):
    sum_slots(slots, 0, part, parts, (ids_ref, order_ref, class_ref), frame_ref, total_ref, *plan)


def layer_kernel(slots, first, start, parts, own, ids_ref, order_ref, class_ref, frame_ref, scale_ref, weight_ref, bias_ref, after_ref, *refs):
    near, (keep_ref, send_ref, total_ref), plan = refs[:parts], refs[parts : parts + 3], refs[parts + 3 :]
    sum_slots(slots, start, 0, 1, (ids_ref, order_ref, class_ref), frame_ref, total_ref, *plan)
    chans, size = keep_ref.shape
    feat = lax.axis_index("feat")
    step = 256
    for at in range(0, size, step):
        rows = slice(at, at + step)
        own_at = pl.multiple_of(own + feat * own + first + at, step)
        total = total_ref[rows, :] + frame_ref[pl.ds(own_at, step), :]
        for ref in near:
            total = total + ref[rows, :]
        product = lax.dot_general(
            weight_ref[...],
            (total * scale_ref[first + at : first + at + step, :]).astype(jnp.bfloat16),
            (((1,), (1,)), ((), ())),
            preferred_element_type=jnp.float32,
        )
        bias = jnp.concatenate([bias_ref[...]] * (step // LANES), axis=1)
        result = jnp.maximum(product + bias, 0.0)
        low, high = result[:chans], result[chans:]
        keep_ref[:, rows] = jnp.where(feat == 0, low, high).astype(jnp.bfloat16)
        if send_ref.shape[0] == chans:
            result = jnp.where(feat == 0, high, low)
        send_ref[:, rows] = result.astype(jnp.bfloat16)


def output_kernel(*refs):
    out_ref = refs[-1]
    count = len(refs) // 2
    feat = lax.axis_index("feat")
    chans = out_ref.shape[0]
    for refs, part in ((refs[:count], feat), (refs[count:-1], 1 - feat)):
        at = part * (out_ref.shape[1] // 2)
        for ref in refs:
            size = ref.shape[1]
            rows = pl.ds(pl.multiple_of(feat * chans, chans), chans) if ref.shape[0] > chans else slice(None)
            out_ref[:, pl.ds(pl.multiple_of(at, size), size)] = ref[rows, :]
            at = at + size


def pallas(kernel, out_shape, in_specs, scratch=(), us=1.0, aliases=None):
    return pl.pallas_call(
        kernel,
        out_shape=out_shape,
        in_specs=in_specs,
        out_specs=jax.tree.map(lambda _: IN_VMEM, out_shape),
        scratch_shapes=list(scratch),
        input_output_aliases=aliases or {},
        compiler_params=pltpu.CompilerParams(vmem_limit_bytes=6 * 2**20),
        cost_estimate=pl.CostEstimate(flops=0, bytes_accessed=int(us * 3_000_000), transcendentals=0),
    )


IN_VMEM = pl.BlockSpec(memory_space=VMEM)
ANYWHERE = pl.BlockSpec(memory_space=pl.ANY)


def local(node_feats, neighbours, degrees, hub_rows, weight, bias_terms):
    chans, nodes = node_feats.shape
    slots = neighbours.shape[0]
    hubs = hub_rows.shape[0]
    slabs = lax.axis_size("slab")
    half = nodes // 2
    chunks = half // CHUNK
    frame_rows, hub_count = 2 * half + nodes, slabs * hubs
    swap = [(0, 1), (1, 0)]

    def bf16(*shape):
        return jax.ShapeDtypeStruct(shape, jnp.bfloat16)

    def f32(*shape):
        return jax.ShapeDtypeStruct(shape, jnp.float32)

    def i32(*shape):
        return jax.ShapeDtypeStruct(shape, jnp.int32)

    block = pallas(
        hub_pick_kernel,
        bf16(hubs // 2, 2 * chans),
        [IN_VMEM, ANYWHERE],
        [VMEM((chans, nodes), jnp.bfloat16), pltpu.SemaphoreType.DMA((4,))],
    )(hub_rows[None, :], node_feats)
    arrived = None

    def stage(block, bits):
        return [lax.ppermute(block, "slab", [(i, i ^ bit) for i in range(slabs)]) for bit in bits]

    def join(block, arrived, *after):
        blocks = 1 + len(arrived)
        return pallas(
            functools.partial(join_kernel, blocks),
            bf16(blocks * block.shape[0], 2 * chans),
            [IN_VMEM] * blocks + [ANYWHERE] * len(after),
            us=0.1,
        )(block, *arrived, *after)

    arrived = stage(block, STAGES[0])
    other = lax.ppermute(node_feats, "feat", swap)
    outer = pallas(
        outer_half_kernel, bf16(chans, half), [ANYWHERE] * 2, [pltpu.SemaphoreType.DMA], us=0.1
    )(node_feats, block)
    pairs = [(i, j) for i in range(slabs) for j in [i + 2 * (i & 1) - 1] if 0 <= j < slabs]
    outer_halo = lax.ppermute(outer, "slab", pairs)
    other_outer = lax.ppermute(
        outer, ("slab", "feat"), [(2 * i + f, 2 * j + 1 - f) for i, j in pairs for f in range(2)]
    )
    deg_tiles = degrees.reshape(nodes // LANES, LANES)
    table, tile = i32(slots, 8, LANES), i32(8, LANES)
    plan = pallas(
        functools.partial(plan_kernel, frame_rows, frame_rows + hub_count),
        (table, tile, tile) * 3,
        [IN_VMEM, IN_VMEM, ANYWHERE],
        us=0.1,
    )(neighbours.reshape(slots, nodes // LANES, LANES), deg_tiles, outer)
    plan = [a.reshape(-1) for a in plan]
    near_plan, far_plan, full_plan = plan[:3], plan[3:6], plan[6:]

    block = join(block, arrived, near_plan[1])
    arrived = stage(block, STAGES[1])
    scale, by_out, bias = pallas(
        constants_kernel,
        (f32(half, LANES), bf16(2 * chans, 2 * chans), f32(LANES, LANES)),
        [IN_VMEM] * 3 + [ANYWHERE],
        us=0.1,
    )(deg_tiles, weight, bias_terms[None, :], block)

    block = join(block, arrived, scale, outer_halo)
    arrived = lax.ppermute(block, "feat", swap)
    block = pallas(
        join_feat_kernel, bf16(2 * block.shape[0], 2 * chans), [IN_VMEM] * 2 + [ANYWHERE], us=0.1
    )(block, arrived, other_outer)
    arrived = stage(block, STAGES[2])
    inner = pallas(
        inner_half_kernel,
        bf16(2 * chans, half),
        [ANYWHERE] * 3,
        [pltpu.SemaphoreType.DMA((2,))],
        us=0.1,
    )(node_feats, other, block)
    inner_halo = lax.ppermute(inner, "slab", [(i, i ^ 1) for i in range(slabs)])
    frame = pallas(
        frame_kernel,
        f32(frame_rows + hub_count + 8, LANES),
        [IN_VMEM] * 5 + [ANYWHERE],
        us=2.0,
    )(node_feats, outer_halo, other, other_outer, inner_halo, block)

    def plan_scratch(size):
        return [
            SMEM((slots * size,), jnp.int32),
            SMEM((size,), jnp.int32),
            SMEM((size + 2 * GROUP,), jnp.int32),
            pltpu.SemaphoreType.DMA((slots + 2,)),
        ]

    def near_sum(part, after):
        return pallas(
            functools.partial(near_kernel, slots, part, 2),
            f32(CHUNK, LANES),
            [ANYWHERE] * 3 + [IN_VMEM, ANYWHERE],
            plan_scratch(CHUNK),
            us=4.0,
        )(*near_plan, frame, after)

    near = [near_sum(0, block)]
    block = join(block, arrived, near[0])
    arrived = stage(block, STAGES[3])
    near.append(near_sum(1, block))
    block = join(block, arrived, near[1])
    arrived = stage(block, STAGES[4])
    frame = pallas(
        functools.partial(hub_frame_kernel, frame_rows, hubs),
        f32(*frame.shape),
        [IN_VMEM] * 3 + [ANYWHERE],
        us=0.5,
        aliases={0: 0},
    )(frame, block, arrived[0], near[1])

    def layer(plan, first, start, size, sent_chans, near, after, us):
        return pallas(
            functools.partial(layer_kernel, slots, first, start, len(near), half),
            (bf16(chans, size), bf16(sent_chans, size)),
            [ANYWHERE] * 3 + [IN_VMEM] * 4 + [ANYWHERE] + [IN_VMEM] * len(near),
            [VMEM((size, LANES), jnp.float32)] + plan_scratch(size),
            us=us,
        )(*plan, frame, scale, by_out, bias, after, *near)

    keep, received = [hub_rows], []
    for plan, first, start, size, sent_chans, near, us in (
        (far_plan, 0, 0, CHUNK, 2 * chans, near, 3.0),
        (full_plan, CHUNK, 0, CHUNK // 2, 2 * chans, [], 4.0),
        (full_plan, CHUNK + CHUNK // 2, CHUNK // 2, CHUNK // 2, chans, [], 4.0),
    ):
        kept, sent = layer(plan, first, start, size, sent_chans, near, keep[-1], us)
        keep.append(kept)
        received.append(lax.ppermute(sent, "feat", swap))
    pieces = keep[1:] + received
    return pallas(output_kernel, bf16(chans, nodes), [IN_VMEM] * len(pieces), us=0.5)(*pieces)


def solution(mesh):
    in_specs = (P("feat", "slab"), P(None, "slab"), P("slab"), P("slab"), P(), P())
    return jax.shard_map(local, mesh=mesh, in_specs=in_specs, out_specs=P("feat", "slab"), check_vma=False)
```

```python
import functools

import jax
import jax.numpy as jnp
from jax import lax
from jax.experimental import pallas as pl
from jax.experimental.pallas import tpu as pltpu
from jax.sharding import PartitionSpec as P

VMEM = pltpu.VMEM
SMEM = pltpu.SMEM
LANES = 128
CHUNK = 1024
GROUP = 16
STAGES = ((32,), (64,), (8, 16, 24), (2, 4, 6), (1,))


def hub_pick_kernel(rows_ref, x_hbm, out_ref, x_ref, sem):
    hubs, nodes = rows_ref.shape[1], x_ref.shape[1]
    parts = sem.shape[0]
    copies = [
        pltpu.make_async_copy(x_hbm.at[:, part], x_ref.at[:, part], sem.at[i])
        for i in range(parts)
        for part in [pl.ds(i * (nodes // parts), nodes // parts)]
    ]
    for copy in copies:
        copy.start()
    diagonal = lax.broadcasted_iota(jnp.int32, (hubs, hubs), 0) == lax.broadcasted_iota(
        jnp.int32, (hubs, hubs), 1
    )
    rows = jnp.sum(jnp.where(diagonal, rows_ref[...], 0), axis=1, keepdims=True)
    onehot = (lax.broadcasted_iota(jnp.int32, (hubs, nodes), 1) == rows).astype(jnp.bfloat16)
    for copy in copies:
        copy.wait()
    picked = lax.dot_general(
        onehot, x_ref[...], (((1,), (1,)), ((), ())), preferred_element_type=jnp.float32
    ).astype(jnp.bfloat16)
    out_ref[...] = jnp.concatenate([picked[: hubs // 2], picked[hubs // 2 :]], axis=1)


def join_kernel(*refs):
    blocks, out_ref = refs[:-2], refs[-1]
    rows = blocks[0].shape[0]
    for i, ref in enumerate(blocks):
        out_ref[i * rows : (i + 1) * rows] = ref[...]


def join_feat_kernel(mine_ref, other_ref, out_ref):
    first = lax.axis_index("feat") == 0
    lane = lax.broadcasted_iota(jnp.int32, (16, LANES), 1)
    for i in range(mine_ref.shape[0] // 16):
        mine = mine_ref[16 * i : 16 * i + 16, :].astype(jnp.float32)
        other = other_ref[16 * i : 16 * i + 16, :].astype(jnp.float32)
        low = jnp.where(first, mine, other)
        high = jnp.where(first, other, mine)
        row = jnp.where(lane < LANES // 2, low, pltpu.roll(high, LANES // 2, 1))
        out_ref[32 * i : 32 * i + 16, :] = row.astype(jnp.bfloat16)
        row = jnp.where(lane < LANES // 2, pltpu.roll(low, LANES // 2, 1), high)
        out_ref[32 * i + 16 : 32 * i + 32, :] = row.astype(jnp.bfloat16)


def halves_kernel(x_ref, other_ref, after_ref, outer_ref, inner_ref, sem):
    feat = lax.axis_index("feat")
    odd = lax.axis_index("slab") & 1
    chans, half = x_ref.shape[0], outer_ref.shape[1]
    copies = []
    for ref, channels in ((x_ref, feat), (other_ref, 1 - feat)):
        rows = pl.ds(pl.multiple_of(channels * chans, chans), chans)
        for out_ref, part in ((outer_ref, odd), (inner_ref, 1 - odd)):
            cols = pl.ds(pl.multiple_of(part * half, half), half)
            copies.append(
                pltpu.make_async_copy(ref.at[:, cols], out_ref.at[rows, :], sem.at[len(copies)])
            )
    for copy in copies:
        copy.start()
    for copy in copies:
        copy.wait()


def frame_kernel(outer_halo_ref, outer_ref, inner_ref, inner_halo_ref, after_ref, frame_ref):
    odd = lax.axis_index("slab") & 1
    half = outer_ref.shape[1]
    step = 256
    unit = (
        lax.broadcasted_iota(jnp.int32, (step, step), 0)
        == lax.broadcasted_iota(jnp.int32, (step, step), 1)
    ).astype(jnp.bfloat16)
    for place, ref in enumerate((outer_halo_ref, outer_ref, inner_ref, inner_halo_ref)):
        first = (place + odd * (3 - 2 * place)) * half
        for at in range(0, half, step):
            frame_ref[pl.ds(pl.multiple_of(first + at, step), step), :] = lax.dot_general(
                unit,
                ref[:, at : at + step],
                (((1,), (1,)), ((), ())),
                preferred_element_type=jnp.float32,
            )
    rows = frame_ref.shape[0]
    frame_ref[rows - 8 :, :] = jnp.zeros((8, LANES), jnp.float32)


def origins():
    differs = [0]
    for bits in STAGES:
        differs = [d ^ bit for bit in (0,) + bits for d in differs]
    return differs


def hub_frame_kernel(first, hubs, frame_in, near_ref, far_ref, after_ref, frame_ref):
    blocks = near_ref.shape[0] // hubs
    me = lax.axis_index("slab")
    for p, differs in enumerate(origins()):
        ref, i = (near_ref, p) if p < blocks else (far_ref, p - blocks)
        at = pl.multiple_of(first + (me ^ differs) * hubs, hubs)
        frame_ref[pl.ds(at, hubs), :] = ref[hubs * i : hubs * (i + 1), :].astype(jnp.float32)


def comparators(count):
    pairs, p = [], 1
    while p < count:
        k = p
        while k >= 1:
            for j in range(k % p, count - k, 2 * k):
                for i in range(min(k, count - j - k)):
                    if (i + j) // (2 * p) == (i + j + k) // (2 * p):
                        pairs.append((i + j, i + j + k))
            k //= 2
        p *= 2
    return pairs


def sort_network(values):
    for a, b in comparators(len(values)):
        values[a], values[b] = jnp.minimum(values[a], values[b]), jnp.maximum(values[a], values[b])
    return values


def sorted_tiles(keys, halved):
    shape = keys.shape
    apart = lax.broadcasted_iota(jnp.int32, shape, 0) == halved
    sub = lax.broadcasted_iota(jnp.int32, shape, 1)
    lane = lax.broadcasted_iota(jnp.int32, shape, 2)
    at = sub * LANES + lane
    size = 2
    while size <= CHUNK:
        distance = size // 2
        while distance >= 1:
            axis, by, extent = (2, distance, LANES) if distance < LANES else (1, distance // LANES, 8)
            lower = (at & distance) == 0
            partner = jnp.where(
                lower, pltpu.roll(keys, extent - by, axis), pltpu.roll(keys, by, axis)
            )
            ascending = (at & size) == 0
            if 2 * size == CHUNK:
                ascending = ascending | apart
            merged = jnp.where(
                lower == ascending, jnp.minimum(keys, partner), jnp.maximum(keys, partner)
            )
            keys = jnp.where(apart, keys, merged) if size == CHUNK else merged
            distance //= 2
        size *= 2
    return keys


def slots_kernel(frame_rows, all_rows, nbr_ref, deg_ref, after_ref, near_ids, far_ids, full_ids, counts_ref):
    slots = nbr_ref.shape[0]
    first = lax.axis_index("feat") * 16
    rows = pl.ds(pl.multiple_of(first, 8), 8)
    degree = deg_ref[rows, :]
    near, far = [], []
    near_count = jnp.zeros((8, LANES), jnp.int32)
    for j in range(slots):
        nbr = nbr_ref[j, rows, :]
        used = degree > j
        is_near = used & (nbr < frame_rows)
        near.append(jnp.where(is_near, nbr, all_rows))
        far.append(jnp.where(used & (nbr >= frame_rows), nbr, all_rows))
        near_count = near_count + is_near.astype(jnp.int32)
    for j, ids in enumerate(sort_network(near)):
        near_ids[j] = ids
    for j, ids in enumerate(sort_network(far)):
        far_ids[j] = ids
    counts_ref[0] = near_count
    counts_ref[1] = degree - near_count
    rows = pl.ds(pl.multiple_of(first + 8, 8), 8)
    degree = deg_ref[rows, :]
    for j in range(slots):
        full_ids[j] = jnp.where(degree > j, nbr_ref[j, rows, :], all_rows)
    counts_ref[2] = degree


def order_kernel(counts_ref, after_ref, *refs):
    orders, classes = refs[:3], refs[3:]
    at = lax.broadcasted_iota(jnp.int32, (8, LANES), 0) * LANES + lax.broadcasted_iota(
        jnp.int32, (8, LANES), 1
    )
    keys = sorted_tiles(counts_ref[...] * CHUNK + at[None], 2)
    for i in range(3):
        orders[i][...] = keys[i] & ((CHUNK if i < 2 else CHUNK // 2) - 1)
        classes[i][...] = keys[i] >> 10


def constants_kernel(deg_ref, weight_ref, bias_ref, after_ref, scale_ref, weight_out, bias_out):
    tiles = scale_ref.shape[0] // LANES
    first = pl.multiple_of(lax.axis_index("feat") * tiles, tiles)
    inverse = 1.0 / (deg_ref[pl.ds(first, tiles), :] + 1).astype(jnp.float32)
    for t in range(tiles):
        scale_ref[LANES * t : LANES * (t + 1), :] = jnp.broadcast_to(
            inverse[t : t + 1, :], (LANES, LANES)
        ).T
    weight_out[...] = weight_ref[...].astype(jnp.float32).T.astype(jnp.bfloat16)
    bias_out[...] = jnp.broadcast_to(bias_ref[...], (LANES, LANES)).T


def add_tree(parts):
    while len(parts) > 1:
        tail = [parts[-1]] if len(parts) % 2 else []
        parts = [parts[i] + parts[i + 1] for i in range(0, len(parts) - 1, 2)] + tail
    return parts[0]


def load_plan(slots, start, ids_ref, order_ref, class_ref, slot_ids, order, classes, sem):
    size = order.shape[0]
    rows = pl.ds(start, size)
    first = [
        pltpu.make_async_copy(order_ref.at[rows], order, sem.at[slots]),
        pltpu.make_async_copy(class_ref.at[rows], classes.at[pl.ds(0, size)], sem.at[slots + 1]),
    ]
    by_slot = [
        pltpu.make_async_copy(
            ids_ref.at[pl.ds(j * CHUNK + start, size)], slot_ids.at[pl.ds(j * size, size)], sem.at[j]
        )
        for j in range(slots)
    ]
    for copy in first + by_slot:
        copy.start()
    return first, by_slot


def sum_slots(slots, start, part, parts, plan_refs, frame_ref, total_ref, slot_ids, order, classes, sem):
    size = order.shape[0]
    first, by_slot = load_plan(slots, start, *plan_refs, slot_ids, order, classes, sem)
    total_ref[...] = jnp.zeros_like(total_ref)
    for copy in first:
        copy.wait()
    last = GROUP - 1
    classes[size + part * GROUP + last] = slots + 1
    of_slot = [slot_ids.at[pl.ds(j * size, size)] for j in range(slots)]

    def body(count, carry):
        base, _ = carry
        for k in range(GROUP):
            node = order[base + k]
            total_ref[pl.ds(node, 1), :] = add_tree(
                [frame_ref[pl.ds(of_slot[j][node], 1), :] for j in range(count)]
            )
        return base + parts * GROUP, classes[base + parts * GROUP + last]

    def skip(carry):
        base, _ = carry
        return base + parts * GROUP, classes[base + parts * GROUP + last]

    carry = (jnp.int32(part * GROUP), classes[part * GROUP + last])
    carry = lax.while_loop(lambda carry: carry[1] == 0, skip, carry)
    for count in range(1, slots + 1):
        by_slot[count - 1].wait()
        carry = lax.while_loop(
            lambda carry, count=count: carry[1] == count, functools.partial(body, count), carry
        )


def near_kernel(slots, part, parts, ids_ref, order_ref, class_ref, frame_ref, after_ref, total_ref, *plan):
    sum_slots(slots, 0, part, parts, (ids_ref, order_ref, class_ref), frame_ref, total_ref, *plan)


def layer_kernel(slots, first, start, parts, own, ids_ref, order_ref, class_ref, frame_ref, scale_ref, weight_ref, bias_ref, after_ref, *refs):
    near, (keep_ref, send_ref, total_ref), plan = refs[:parts], refs[parts : parts + 3], refs[parts + 3 :]
    sum_slots(slots, start, 0, 1, (ids_ref, order_ref, class_ref), frame_ref, total_ref, *plan)
    chans, size = keep_ref.shape
    feat = lax.axis_index("feat")
    step = 256
    for at in range(0, size, step):
        rows = slice(at, at + step)
        own_at = pl.multiple_of(own + feat * own + first + at, step)
        total = total_ref[rows, :] + frame_ref[pl.ds(own_at, step), :]
        for ref in near:
            total = total + ref[rows, :]
        product = lax.dot_general(
            weight_ref[...],
            (total * scale_ref[first + at : first + at + step, :]).astype(jnp.bfloat16),
            (((1,), (1,)), ((), ())),
            preferred_element_type=jnp.float32,
        )
        bias = jnp.concatenate([bias_ref[...]] * (step // LANES), axis=1)
        result = jnp.maximum(product + bias, 0.0)
        low, high = result[:chans], result[chans:]
        keep_ref[:, rows] = jnp.where(feat == 0, low, high).astype(jnp.bfloat16)
        if send_ref.shape[0] == chans:
            result = jnp.where(feat == 0, high, low)
        send_ref[:, rows] = result.astype(jnp.bfloat16)


def output_kernel(*refs):
    out_ref = refs[-1]
    count = len(refs) // 2
    feat = lax.axis_index("feat")
    chans = out_ref.shape[0]
    for refs, part in ((refs[:count], feat), (refs[count:-1], 1 - feat)):
        at = part * (out_ref.shape[1] // 2)
        for ref in refs:
            size = ref.shape[1]
            rows = pl.ds(pl.multiple_of(feat * chans, chans), chans) if ref.shape[0] > chans else slice(None)
            out_ref[:, pl.ds(pl.multiple_of(at, size), size)] = ref[rows, :]
            at = at + size


def pallas(kernel, out_shape, in_specs, scratch=(), us=1.0, aliases=None):
    return pl.pallas_call(
        kernel,
        out_shape=out_shape,
        in_specs=in_specs,
        out_specs=jax.tree.map(lambda _: IN_VMEM, out_shape),
        scratch_shapes=list(scratch),
        input_output_aliases=aliases or {},
        compiler_params=pltpu.CompilerParams(vmem_limit_bytes=6 * 2**20),
        cost_estimate=pl.CostEstimate(flops=0, bytes_accessed=int(us * 3_000_000), transcendentals=0),
    )


IN_VMEM = pl.BlockSpec(memory_space=VMEM)
ANYWHERE = pl.BlockSpec(memory_space=pl.ANY)


def local(node_feats, neighbours, degrees, hub_rows, weight, bias_terms):
    chans, nodes = node_feats.shape
    slots = neighbours.shape[0]
    hubs = hub_rows.shape[0]
    slabs = lax.axis_size("slab")
    half = nodes // 2
    chunks = half // CHUNK
    frame_rows, hub_count = 2 * half + nodes, slabs * hubs
    swap = [(0, 1), (1, 0)]

    def bf16(*shape):
        return jax.ShapeDtypeStruct(shape, jnp.bfloat16)

    def f32(*shape):
        return jax.ShapeDtypeStruct(shape, jnp.float32)

    def i32(*shape):
        return jax.ShapeDtypeStruct(shape, jnp.int32)

    block = pallas(
        hub_pick_kernel,
        bf16(hubs // 2, 2 * chans),
        [IN_VMEM, ANYWHERE],
        [VMEM((chans, nodes), jnp.bfloat16), pltpu.SemaphoreType.DMA((4,))],
    )(hub_rows[None, :], node_feats)
    arrived = None

    def stage(block, bits):
        return [lax.ppermute(block, "slab", [(i, i ^ bit) for i in range(slabs)]) for bit in bits]

    def join(block, arrived, after):
        rows = block.shape[0] * (1 + len(arrived))
        specs = [IN_VMEM] * (1 + len(arrived)) + [ANYWHERE]
        return pallas(join_kernel, bf16(rows, 2 * chans), specs, us=0.5)(block, *arrived, after)

    arrived = stage(block, STAGES[0])
    deg_tiles = degrees.reshape(nodes // LANES, LANES)
    table, tile = i32(slots, 8, LANES), i32(8, LANES)
    *ids, counts = pallas(
        functools.partial(slots_kernel, frame_rows, frame_rows + hub_count),
        (table, table, table, i32(3, 8, LANES)),
        [IN_VMEM, IN_VMEM, ANYWHERE],
        us=1.0,
    )(neighbours.reshape(slots, nodes // LANES, LANES), deg_tiles, block)
    other = lax.ppermute(node_feats, "feat", swap)

    block = join(block, arrived, counts)
    arrived = stage(block, STAGES[1])
    order = pallas(order_kernel, (tile,) * 6, [IN_VMEM, ANYWHERE], us=3.0)(counts, block)
    near_plan, far_plan, full_plan = (
        [a.reshape(-1) for a in (ids[i], order[i], order[3 + i])] for i in range(3)
    )

    block = join(block, arrived, order[0])
    arrived = stage(block, STAGES[2])
    scale, by_out, bias = pallas(
        constants_kernel,
        (f32(half, LANES), bf16(2 * chans, 2 * chans), f32(LANES, LANES)),
        [IN_VMEM] * 3 + [ANYWHERE],
        us=1.0,
    )(deg_tiles, weight, bias_terms[None, :], block)

    block = join(block, arrived, scale)
    arrived = lax.ppermute(block, "feat", swap)
    block = pallas(
        join_feat_kernel, bf16(2 * block.shape[0], 2 * chans), [IN_VMEM] * 2, us=0.5
    )(block, arrived)
    arrived = stage(block, STAGES[3])
    outer, inner = pallas(
        halves_kernel,
        (bf16(2 * chans, half),) * 2,
        [ANYWHERE] * 3,
        [pltpu.SemaphoreType.DMA((4,))],
        us=0.5,
    )(node_feats, other, block)
    inner_halo = lax.ppermute(inner, "slab", [(i, i ^ 1) for i in range(slabs)])
    outer_halo = lax.ppermute(
        outer, "slab", [(i, j) for i in range(slabs) for j in [i + 2 * (i & 1) - 1] if 0 <= j < slabs]
    )
    frame = pallas(
        frame_kernel,
        f32(frame_rows + hub_count + 8, LANES),
        [IN_VMEM] * 4 + [ANYWHERE],
        us=2.0,
    )(outer_halo, outer, inner, inner_halo, block)

    def plan_scratch(size):
        return [
            SMEM((slots * size,), jnp.int32),
            SMEM((size,), jnp.int32),
            SMEM((size + 2 * GROUP,), jnp.int32),
            pltpu.SemaphoreType.DMA((slots + 2,)),
        ]

    def near_sum(part, after):
        return pallas(
            functools.partial(near_kernel, slots, part, 2),
            f32(CHUNK, LANES),
            [ANYWHERE] * 3 + [IN_VMEM, ANYWHERE],
            plan_scratch(CHUNK),
            us=4.0,
        )(*near_plan, frame, after)

    near = [near_sum(0, block)]
    block = join(block, arrived, near[0])
    arrived = stage(block, STAGES[4])
    near.append(near_sum(1, block))
    frame = pallas(
        functools.partial(hub_frame_kernel, frame_rows, hubs),
        f32(*frame.shape),
        [IN_VMEM] * 3 + [ANYWHERE],
        us=0.5,
        aliases={0: 0},
    )(frame, block, arrived[0], near[1])

    def layer(plan, first, start, size, sent_chans, near, after, us):
        return pallas(
            functools.partial(layer_kernel, slots, first, start, len(near), half),
            (bf16(chans, size), bf16(sent_chans, size)),
            [ANYWHERE] * 3 + [IN_VMEM] * 4 + [ANYWHERE] + [IN_VMEM] * len(near),
            [VMEM((size, LANES), jnp.float32)] + plan_scratch(size),
            us=us,
        )(*plan, frame, scale, by_out, bias, after, *near)

    keep, received = [hub_rows], []
    for plan, first, start, size, sent_chans, near, us in (
        (far_plan, 0, 0, CHUNK, 2 * chans, near, 3.0),
        (full_plan, CHUNK, 0, CHUNK // 2, 2 * chans, [], 4.0),
        (full_plan, CHUNK + CHUNK // 2, CHUNK // 2, CHUNK // 2, chans, [], 4.0),
    ):
        kept, sent = layer(plan, first, start, size, sent_chans, near, keep[-1], us)
        keep.append(kept)
        received.append(lax.ppermute(sent, "feat", swap))
    pieces = keep[1:] + received
    return pallas(output_kernel, bf16(chans, nodes), [IN_VMEM] * len(pieces), us=0.5)(*pieces)


def solution(mesh):
    in_specs = (P("feat", "slab"), P(None, "slab"), P("slab"), P("slab"), P(), P())
    return jax.shard_map(local, mesh=mesh, in_specs=in_specs, out_specs=P("feat", "slab"), check_vma=False)
```

```python
import functools

import jax
import jax.numpy as jnp
from jax import lax
from jax.experimental import pallas as pl
from jax.experimental.pallas import tpu as pltpu
from jax.sharding import PartitionSpec as P

VMEM = pltpu.VMEM
SMEM = pltpu.SMEM
LANES = 128
CHUNK = 1024
GROUP = 16
STAGES = ((32,), (64,), (8, 16, 24), (2, 4, 6), (1,))


def hub_pick_kernel(rows_ref, x_hbm, out_ref, x_ref, sem):
    hubs, nodes = rows_ref.shape[1], x_ref.shape[1]
    parts = sem.shape[0]
    copies = [
        pltpu.make_async_copy(x_hbm.at[:, part], x_ref.at[:, part], sem.at[i])
        for i in range(parts)
        for part in [pl.ds(i * (nodes // parts), nodes // parts)]
    ]
    for copy in copies:
        copy.start()
    diagonal = lax.broadcasted_iota(jnp.int32, (hubs, hubs), 0) == lax.broadcasted_iota(
        jnp.int32, (hubs, hubs), 1
    )
    rows = jnp.sum(jnp.where(diagonal, rows_ref[...], 0), axis=1, keepdims=True)
    onehot = (lax.broadcasted_iota(jnp.int32, (hubs, nodes), 1) == rows).astype(jnp.bfloat16)
    for copy in copies:
        copy.wait()
    picked = lax.dot_general(
        onehot, x_ref[...], (((1,), (1,)), ((), ())), preferred_element_type=jnp.float32
    ).astype(jnp.bfloat16)
    out_ref[...] = jnp.concatenate([picked[: hubs // 2], picked[hubs // 2 :]], axis=1)


def join_kernel(*refs):
    blocks, out_ref = refs[:-2], refs[-1]
    rows = blocks[0].shape[0]
    for i, ref in enumerate(blocks):
        out_ref[i * rows : (i + 1) * rows] = ref[...]


def join_feat_kernel(mine_ref, other_ref, after_ref, out_ref):
    first = lax.axis_index("feat") == 0
    lane = lax.broadcasted_iota(jnp.int32, (16, LANES), 1)
    for i in range(mine_ref.shape[0] // 16):
        mine = mine_ref[16 * i : 16 * i + 16, :].astype(jnp.float32)
        other = other_ref[16 * i : 16 * i + 16, :].astype(jnp.float32)
        low = jnp.where(first, mine, other)
        high = jnp.where(first, other, mine)
        row = jnp.where(lane < LANES // 2, low, pltpu.roll(high, LANES // 2, 1))
        out_ref[32 * i : 32 * i + 16, :] = row.astype(jnp.bfloat16)
        row = jnp.where(lane < LANES // 2, pltpu.roll(low, LANES // 2, 1), high)
        out_ref[32 * i + 16 : 32 * i + 32, :] = row.astype(jnp.bfloat16)


def halves_kernel(x_ref, other_ref, after_ref, outer_ref, inner_ref, sem):
    feat = lax.axis_index("feat")
    odd = lax.axis_index("slab") & 1
    chans, half = x_ref.shape[0], outer_ref.shape[1]
    copies = []
    for ref, channels in ((x_ref, feat), (other_ref, 1 - feat)):
        rows = pl.ds(pl.multiple_of(channels * chans, chans), chans)
        for out_ref, part in ((outer_ref, odd), (inner_ref, 1 - odd)):
            cols = pl.ds(pl.multiple_of(part * half, half), half)
            copies.append(
                pltpu.make_async_copy(ref.at[:, cols], out_ref.at[rows, :], sem.at[len(copies)])
            )
    for copy in copies:
        copy.start()
    for copy in copies:
        copy.wait()


def frame_kernel(outer_halo_ref, outer_ref, inner_ref, inner_halo_ref, after_ref, frame_ref):
    odd = lax.axis_index("slab") & 1
    half = outer_ref.shape[1]
    step = 256
    unit = (
        lax.broadcasted_iota(jnp.int32, (step, step), 0)
        == lax.broadcasted_iota(jnp.int32, (step, step), 1)
    ).astype(jnp.bfloat16)
    for place, ref in enumerate((outer_halo_ref, outer_ref, inner_ref, inner_halo_ref)):
        first = (place + odd * (3 - 2 * place)) * half
        for at in range(0, half, step):
            frame_ref[pl.ds(pl.multiple_of(first + at, step), step), :] = lax.dot_general(
                unit,
                ref[:, at : at + step],
                (((1,), (1,)), ((), ())),
                preferred_element_type=jnp.float32,
            )
    rows = frame_ref.shape[0]
    frame_ref[rows - 8 :, :] = jnp.zeros((8, LANES), jnp.float32)


def origins():
    differs = [0]
    for bits in STAGES:
        differs = [d ^ bit for bit in (0,) + bits for d in differs]
    return differs


def hub_frame_kernel(first, hubs, frame_in, near_ref, far_ref, after_ref, frame_ref):
    blocks = near_ref.shape[0] // hubs
    me = lax.axis_index("slab")
    for p, differs in enumerate(origins()):
        ref, i = (near_ref, p) if p < blocks else (far_ref, p - blocks)
        at = pl.multiple_of(first + (me ^ differs) * hubs, hubs)
        frame_ref[pl.ds(at, hubs), :] = ref[hubs * i : hubs * (i + 1), :].astype(jnp.float32)


def comparators(count):
    pairs, p = [], 1
    while p < count:
        k = p
        while k >= 1:
            for j in range(k % p, count - k, 2 * k):
                for i in range(min(k, count - j - k)):
                    if (i + j) // (2 * p) == (i + j + k) // (2 * p):
                        pairs.append((i + j, i + j + k))
            k //= 2
        p *= 2
    return pairs


def sort_network(values):
    for a, b in comparators(len(values)):
        values[a], values[b] = jnp.minimum(values[a], values[b]), jnp.maximum(values[a], values[b])
    return values


def sorted_tiles(keys, halved):
    shape = keys.shape
    apart = lax.broadcasted_iota(jnp.int32, shape, 0) == halved
    sub = lax.broadcasted_iota(jnp.int32, shape, 1)
    lane = lax.broadcasted_iota(jnp.int32, shape, 2)
    at = sub * LANES + lane
    size = 2
    while size <= CHUNK:
        distance = size // 2
        while distance >= 1:
            axis, by, extent = (2, distance, LANES) if distance < LANES else (1, distance // LANES, 8)
            lower = (at & distance) == 0
            partner = jnp.where(
                lower, pltpu.roll(keys, extent - by, axis), pltpu.roll(keys, by, axis)
            )
            ascending = (at & size) == 0
            if 2 * size == CHUNK:
                ascending = ascending | apart
            merged = jnp.where(
                lower == ascending, jnp.minimum(keys, partner), jnp.maximum(keys, partner)
            )
            keys = jnp.where(apart, keys, merged) if size == CHUNK else merged
            distance //= 2
        size *= 2
    return keys


def slots_kernel(frame_rows, all_rows, nbr_ref, deg_ref, after_ref, near_ids, far_ids, full_ids, counts_ref):
    slots = nbr_ref.shape[0]
    first = lax.axis_index("feat") * 16
    rows = pl.ds(pl.multiple_of(first, 8), 8)
    degree = deg_ref[rows, :]
    near, far = [], []
    near_count = jnp.zeros((8, LANES), jnp.int32)
    for j in range(slots):
        nbr = nbr_ref[j, rows, :]
        used = degree > j
        is_near = used & (nbr < frame_rows)
        near.append(jnp.where(is_near, nbr, all_rows))
        far.append(jnp.where(used & (nbr >= frame_rows), nbr, all_rows))
        near_count = near_count + is_near.astype(jnp.int32)
    for j, ids in enumerate(sort_network(near)):
        near_ids[j] = ids
    for j, ids in enumerate(sort_network(far)):
        far_ids[j] = ids
    counts_ref[0] = near_count
    counts_ref[1] = degree - near_count
    rows = pl.ds(pl.multiple_of(first + 8, 8), 8)
    degree = deg_ref[rows, :]
    for j in range(slots):
        full_ids[j] = jnp.where(degree > j, nbr_ref[j, rows, :], all_rows)
    counts_ref[2] = degree


def order_kernel(counts_ref, after_ref, *refs):
    orders, classes = refs[:3], refs[3:]
    at = lax.broadcasted_iota(jnp.int32, (8, LANES), 0) * LANES + lax.broadcasted_iota(
        jnp.int32, (8, LANES), 1
    )
    keys = sorted_tiles(counts_ref[...] * CHUNK + at[None], 2)
    for i in range(3):
        orders[i][...] = keys[i] & ((CHUNK if i < 2 else CHUNK // 2) - 1)
        classes[i][...] = keys[i] >> 10


def constants_kernel(deg_ref, weight_ref, bias_ref, after_ref, scale_ref, weight_out, bias_out):
    tiles = scale_ref.shape[0] // LANES
    first = pl.multiple_of(lax.axis_index("feat") * tiles, tiles)
    inverse = 1.0 / (deg_ref[pl.ds(first, tiles), :] + 1).astype(jnp.float32)
    for t in range(tiles):
        scale_ref[LANES * t : LANES * (t + 1), :] = jnp.broadcast_to(
            inverse[t : t + 1, :], (LANES, LANES)
        ).T
    weight_out[...] = weight_ref[...].astype(jnp.float32).T.astype(jnp.bfloat16)
    bias_out[...] = jnp.broadcast_to(bias_ref[...], (LANES, LANES)).T


def add_tree(parts):
    while len(parts) > 1:
        tail = [parts[-1]] if len(parts) % 2 else []
        parts = [parts[i] + parts[i + 1] for i in range(0, len(parts) - 1, 2)] + tail
    return parts[0]


def load_plan(slots, start, ids_ref, order_ref, class_ref, slot_ids, order, classes, sem):
    size = order.shape[0]
    rows = pl.ds(start, size)
    first = [
        pltpu.make_async_copy(order_ref.at[rows], order, sem.at[slots]),
        pltpu.make_async_copy(class_ref.at[rows], classes.at[pl.ds(0, size)], sem.at[slots + 1]),
    ]
    by_slot = [
        pltpu.make_async_copy(
            ids_ref.at[pl.ds(j * CHUNK + start, size)], slot_ids.at[pl.ds(j * size, size)], sem.at[j]
        )
        for j in range(slots)
    ]
    for copy in first + by_slot:
        copy.start()
    return first, by_slot


def sum_slots(slots, start, part, parts, plan_refs, frame_ref, total_ref, slot_ids, order, classes, sem):
    size = order.shape[0]
    first, by_slot = load_plan(slots, start, *plan_refs, slot_ids, order, classes, sem)
    total_ref[...] = jnp.zeros_like(total_ref)
    for copy in first:
        copy.wait()
    last = GROUP - 1
    classes[size + part * GROUP + last] = slots + 1
    of_slot = [slot_ids.at[pl.ds(j * size, size)] for j in range(slots)]

    def body(count, carry):
        base, _ = carry
        for k in range(GROUP):
            node = order[base + k]
            total_ref[pl.ds(node, 1), :] = add_tree(
                [frame_ref[pl.ds(of_slot[j][node], 1), :] for j in range(count)]
            )
        return base + parts * GROUP, classes[base + parts * GROUP + last]

    def skip(carry):
        base, _ = carry
        return base + parts * GROUP, classes[base + parts * GROUP + last]

    carry = (jnp.int32(part * GROUP), classes[part * GROUP + last])
    carry = lax.while_loop(lambda carry: carry[1] == 0, skip, carry)
    for count in range(1, slots + 1):
        by_slot[count - 1].wait()
        carry = lax.while_loop(
            lambda carry, count=count: carry[1] == count, functools.partial(body, count), carry
        )


def near_kernel(slots, part, parts, ids_ref, order_ref, class_ref, frame_ref, after_ref, total_ref, *plan):
    sum_slots(slots, 0, part, parts, (ids_ref, order_ref, class_ref), frame_ref, total_ref, *plan)


def layer_kernel(slots, first, start, parts, own, ids_ref, order_ref, class_ref, frame_ref, scale_ref, weight_ref, bias_ref, after_ref, *refs):
    near, (keep_ref, send_ref, total_ref), plan = refs[:parts], refs[parts : parts + 3], refs[parts + 3 :]
    sum_slots(slots, start, 0, 1, (ids_ref, order_ref, class_ref), frame_ref, total_ref, *plan)
    chans, size = keep_ref.shape
    feat = lax.axis_index("feat")
    step = 256
    for at in range(0, size, step):
        rows = slice(at, at + step)
        own_at = pl.multiple_of(own + feat * own + first + at, step)
        total = total_ref[rows, :] + frame_ref[pl.ds(own_at, step), :]
        for ref in near:
            total = total + ref[rows, :]
        product = lax.dot_general(
            weight_ref[...],
            (total * scale_ref[first + at : first + at + step, :]).astype(jnp.bfloat16),
            (((1,), (1,)), ((), ())),
            preferred_element_type=jnp.float32,
        )
        bias = jnp.concatenate([bias_ref[...]] * (step // LANES), axis=1)
        result = jnp.maximum(product + bias, 0.0)
        low, high = result[:chans], result[chans:]
        keep_ref[:, rows] = jnp.where(feat == 0, low, high).astype(jnp.bfloat16)
        if send_ref.shape[0] == chans:
            result = jnp.where(feat == 0, high, low)
        send_ref[:, rows] = result.astype(jnp.bfloat16)


def output_kernel(*refs):
    out_ref = refs[-1]
    count = len(refs) // 2
    feat = lax.axis_index("feat")
    chans = out_ref.shape[0]
    for refs, part in ((refs[:count], feat), (refs[count:-1], 1 - feat)):
        at = part * (out_ref.shape[1] // 2)
        for ref in refs:
            size = ref.shape[1]
            rows = pl.ds(pl.multiple_of(feat * chans, chans), chans) if ref.shape[0] > chans else slice(None)
            out_ref[:, pl.ds(pl.multiple_of(at, size), size)] = ref[rows, :]
            at = at + size


def pallas(kernel, out_shape, in_specs, scratch=(), us=1.0, aliases=None):
    return pl.pallas_call(
        kernel,
        out_shape=out_shape,
        in_specs=in_specs,
        out_specs=jax.tree.map(lambda _: IN_VMEM, out_shape),
        scratch_shapes=list(scratch),
        input_output_aliases=aliases or {},
        compiler_params=pltpu.CompilerParams(vmem_limit_bytes=6 * 2**20),
        cost_estimate=pl.CostEstimate(flops=0, bytes_accessed=int(us * 3_000_000), transcendentals=0),
    )


IN_VMEM = pl.BlockSpec(memory_space=VMEM)
ANYWHERE = pl.BlockSpec(memory_space=pl.ANY)


def local(node_feats, neighbours, degrees, hub_rows, weight, bias_terms):
    chans, nodes = node_feats.shape
    slots = neighbours.shape[0]
    hubs = hub_rows.shape[0]
    slabs = lax.axis_size("slab")
    half = nodes // 2
    chunks = half // CHUNK
    frame_rows, hub_count = 2 * half + nodes, slabs * hubs
    swap = [(0, 1), (1, 0)]

    def bf16(*shape):
        return jax.ShapeDtypeStruct(shape, jnp.bfloat16)

    def f32(*shape):
        return jax.ShapeDtypeStruct(shape, jnp.float32)

    def i32(*shape):
        return jax.ShapeDtypeStruct(shape, jnp.int32)

    block = pallas(
        hub_pick_kernel,
        bf16(hubs // 2, 2 * chans),
        [IN_VMEM, ANYWHERE],
        [VMEM((chans, nodes), jnp.bfloat16), pltpu.SemaphoreType.DMA((4,))],
    )(hub_rows[None, :], node_feats)
    arrived = None

    def stage(block, bits):
        return [lax.ppermute(block, "slab", [(i, i ^ bit) for i in range(slabs)]) for bit in bits]

    def join(block, arrived, after):
        rows = block.shape[0] * (1 + len(arrived))
        specs = [IN_VMEM] * (1 + len(arrived)) + [ANYWHERE]
        return pallas(join_kernel, bf16(rows, 2 * chans), specs, us=0.5)(block, *arrived, after)

    arrived = stage(block, STAGES[0])
    deg_tiles = degrees.reshape(nodes // LANES, LANES)
    table, tile = i32(slots, 8, LANES), i32(8, LANES)
    *ids, counts = pallas(
        functools.partial(slots_kernel, frame_rows, frame_rows + hub_count),
        (table, table, table, i32(3, 8, LANES)),
        [IN_VMEM, IN_VMEM, ANYWHERE],
        us=1.0,
    )(neighbours.reshape(slots, nodes // LANES, LANES), deg_tiles, block)
    other = lax.ppermute(node_feats, "feat", swap)

    block = join(block, arrived, counts)
    arrived = stage(block, STAGES[1])
    order = pallas(order_kernel, (tile,) * 6, [IN_VMEM, ANYWHERE], us=3.0)(counts, block)
    near_plan, far_plan, full_plan = (
        [a.reshape(-1) for a in (ids[i], order[i], order[3 + i])] for i in range(3)
    )

    block = join(block, arrived, order[0])
    outer, inner = pallas(
        halves_kernel,
        (bf16(2 * chans, half),) * 2,
        [ANYWHERE] * 3,
        [pltpu.SemaphoreType.DMA((4,))],
        us=0.5,
    )(node_feats, other, block)
    inner_halo = lax.ppermute(inner, "slab", [(i, i ^ 1) for i in range(slabs)])
    outer_halo = lax.ppermute(
        outer, "slab", [(i, j) for i in range(slabs) for j in [i + 2 * (i & 1) - 1] if 0 <= j < slabs]
    )
    arrived = stage(block, STAGES[2])

    block = join(block, arrived, outer)
    arrived = lax.ppermute(block, "feat", swap)
    scale, by_out, bias = pallas(
        constants_kernel,
        (f32(half, LANES), bf16(2 * chans, 2 * chans), f32(LANES, LANES)),
        [IN_VMEM] * 3 + [ANYWHERE],
        us=1.0,
    )(deg_tiles, weight, bias_terms[None, :], block)
    block = pallas(
        join_feat_kernel, bf16(2 * block.shape[0], 2 * chans), [IN_VMEM] * 2 + [ANYWHERE], us=0.5
    )(block, arrived, scale)
    arrived = stage(block, STAGES[3])
    frame = pallas(
        frame_kernel,
        f32(frame_rows + hub_count + 8, LANES),
        [IN_VMEM] * 4 + [ANYWHERE],
        us=2.0,
    )(outer_halo, outer, inner, inner_halo, block)

    def plan_scratch(size):
        return [
            SMEM((slots * size,), jnp.int32),
            SMEM((size,), jnp.int32),
            SMEM((size + 2 * GROUP,), jnp.int32),
            pltpu.SemaphoreType.DMA((slots + 2,)),
        ]

    def near_sum(part, after):
        return pallas(
            functools.partial(near_kernel, slots, part, 2),
            f32(CHUNK, LANES),
            [ANYWHERE] * 3 + [IN_VMEM, ANYWHERE],
            plan_scratch(CHUNK),
            us=4.0,
        )(*near_plan, frame, after)

    near = [near_sum(0, block)]
    block = join(block, arrived, near[0])
    arrived = stage(block, STAGES[4])
    near.append(near_sum(1, block))
    frame = pallas(
        functools.partial(hub_frame_kernel, frame_rows, hubs),
        f32(*frame.shape),
        [IN_VMEM] * 3 + [ANYWHERE],
        us=0.5,
        aliases={0: 0},
    )(frame, block, arrived[0], near[1])

    def layer(plan, first, start, size, sent_chans, near, after, us):
        return pallas(
            functools.partial(layer_kernel, slots, first, start, len(near), half),
            (bf16(chans, size), bf16(sent_chans, size)),
            [ANYWHERE] * 3 + [IN_VMEM] * 4 + [ANYWHERE] + [IN_VMEM] * len(near),
            [VMEM((size, LANES), jnp.float32)] + plan_scratch(size),
            us=us,
        )(*plan, frame, scale, by_out, bias, after, *near)

    keep, received = [hub_rows], []
    for plan, first, start, size, sent_chans, near, us in (
        (far_plan, 0, 0, CHUNK, 2 * chans, near, 3.0),
        (full_plan, CHUNK, 0, CHUNK // 2, 2 * chans, [], 4.0),
        (full_plan, CHUNK + CHUNK // 2, CHUNK // 2, CHUNK // 2, chans, [], 4.0),
    ):
        kept, sent = layer(plan, first, start, size, sent_chans, near, keep[-1], us)
        keep.append(kept)
        received.append(lax.ppermute(sent, "feat", swap))
    pieces = keep[1:] + received
    return pallas(output_kernel, bf16(chans, nodes), [IN_VMEM] * len(pieces), us=0.5)(*pieces)


def solution(mesh):
    in_specs = (P("feat", "slab"), P(None, "slab"), P("slab"), P("slab"), P(), P())
    return jax.shard_map(local, mesh=mesh, in_specs=in_specs, out_specs=P("feat", "slab"), check_vma=False)
```

```python
import functools

import jax
import jax.numpy as jnp
from jax import lax
from jax.experimental import pallas as pl
from jax.experimental.pallas import tpu as pltpu
from jax.sharding import PartitionSpec as P

VMEM = pltpu.VMEM
SMEM = pltpu.SMEM
LANES = 128
CHUNK = 1024
GROUP = 16
STAGES = ((32,), (64,), (8, 16, 24), (2, 4, 6), (1,))


def hub_pick_kernel(rows_ref, x_hbm, out_ref, x_ref, sem):
    hubs, nodes = rows_ref.shape[1], x_ref.shape[1]
    parts = sem.shape[0]
    copies = [
        pltpu.make_async_copy(x_hbm.at[:, part], x_ref.at[:, part], sem.at[i])
        for i in range(parts)
        for part in [pl.ds(i * (nodes // parts), nodes // parts)]
    ]
    for copy in copies:
        copy.start()
    diagonal = lax.broadcasted_iota(jnp.int32, (hubs, hubs), 0) == lax.broadcasted_iota(
        jnp.int32, (hubs, hubs), 1
    )
    rows = jnp.sum(jnp.where(diagonal, rows_ref[...], 0), axis=1, keepdims=True)
    onehot = (lax.broadcasted_iota(jnp.int32, (hubs, nodes), 1) == rows).astype(jnp.bfloat16)
    for copy in copies:
        copy.wait()
    picked = lax.dot_general(
        onehot, x_ref[...], (((1,), (1,)), ((), ())), preferred_element_type=jnp.float32
    ).astype(jnp.bfloat16)
    out_ref[...] = jnp.concatenate([picked[: hubs // 2], picked[hubs // 2 :]], axis=1)


def join_kernel(*refs):
    blocks, out_ref = refs[:-2], refs[-1]
    rows = blocks[0].shape[0]
    for i, ref in enumerate(blocks):
        out_ref[i * rows : (i + 1) * rows] = ref[...]


def join_feat_kernel(mine_ref, other_ref, after_ref, out_ref):
    first = lax.axis_index("feat") == 0
    lane = lax.broadcasted_iota(jnp.int32, (16, LANES), 1)
    for i in range(mine_ref.shape[0] // 16):
        mine = mine_ref[16 * i : 16 * i + 16, :].astype(jnp.float32)
        other = other_ref[16 * i : 16 * i + 16, :].astype(jnp.float32)
        low = jnp.where(first, mine, other)
        high = jnp.where(first, other, mine)
        row = jnp.where(lane < LANES // 2, low, pltpu.roll(high, LANES // 2, 1))
        out_ref[32 * i : 32 * i + 16, :] = row.astype(jnp.bfloat16)
        row = jnp.where(lane < LANES // 2, pltpu.roll(low, LANES // 2, 1), high)
        out_ref[32 * i + 16 : 32 * i + 32, :] = row.astype(jnp.bfloat16)


def halves_kernel(x_ref, other_ref, after_ref, outer_ref, inner_ref, sem):
    feat = lax.axis_index("feat")
    odd = lax.axis_index("slab") & 1
    chans, half = x_ref.shape[0], outer_ref.shape[1]
    copies = []
    for ref, channels in ((x_ref, feat), (other_ref, 1 - feat)):
        rows = pl.ds(pl.multiple_of(channels * chans, chans), chans)
        for out_ref, part in ((outer_ref, odd), (inner_ref, 1 - odd)):
            cols = pl.ds(pl.multiple_of(part * half, half), half)
            copies.append(
                pltpu.make_async_copy(ref.at[:, cols], out_ref.at[rows, :], sem.at[len(copies)])
            )
    for copy in copies:
        copy.start()
    for copy in copies:
        copy.wait()


def frame_kernel(outer_halo_ref, outer_ref, inner_ref, inner_halo_ref, after_ref, frame_ref):
    odd = lax.axis_index("slab") & 1
    half = outer_ref.shape[1]
    step = 256
    unit = (
        lax.broadcasted_iota(jnp.int32, (step, step), 0)
        == lax.broadcasted_iota(jnp.int32, (step, step), 1)
    ).astype(jnp.bfloat16)
    for place, ref in enumerate((outer_halo_ref, outer_ref, inner_ref, inner_halo_ref)):
        first = (place + odd * (3 - 2 * place)) * half
        for at in range(0, half, step):
            frame_ref[pl.ds(pl.multiple_of(first + at, step), step), :] = lax.dot_general(
                unit,
                ref[:, at : at + step],
                (((1,), (1,)), ((), ())),
                preferred_element_type=jnp.float32,
            )
    rows = frame_ref.shape[0]
    frame_ref[rows - 8 :, :] = jnp.zeros((8, LANES), jnp.float32)


def origins():
    differs = [0]
    for bits in STAGES:
        differs = [d ^ bit for bit in (0,) + bits for d in differs]
    return differs


def hub_frame_kernel(first, hubs, frame_in, near_ref, far_ref, after_ref, frame_ref):
    blocks = near_ref.shape[0] // hubs
    me = lax.axis_index("slab")
    for p, differs in enumerate(origins()):
        ref, i = (near_ref, p) if p < blocks else (far_ref, p - blocks)
        at = pl.multiple_of(first + (me ^ differs) * hubs, hubs)
        frame_ref[pl.ds(at, hubs), :] = ref[hubs * i : hubs * (i + 1), :].astype(jnp.float32)


def comparators(count):
    pairs, p = [], 1
    while p < count:
        k = p
        while k >= 1:
            for j in range(k % p, count - k, 2 * k):
                for i in range(min(k, count - j - k)):
                    if (i + j) // (2 * p) == (i + j + k) // (2 * p):
                        pairs.append((i + j, i + j + k))
            k //= 2
        p *= 2
    return pairs


def sort_network(values):
    for a, b in comparators(len(values)):
        values[a], values[b] = jnp.minimum(values[a], values[b]), jnp.maximum(values[a], values[b])
    return values


def sorted_tiles(keys):
    shape = keys.shape
    sub = lax.broadcasted_iota(jnp.int32, shape, 1)
    lane = lax.broadcasted_iota(jnp.int32, shape, 2)
    at = sub * LANES + lane
    size = 2
    while size <= CHUNK:
        distance = size // 2
        while distance >= 1:
            axis, by, extent = (2, distance, LANES) if distance < LANES else (1, distance // LANES, 8)
            lower = (at & distance) == 0
            partner = jnp.where(
                lower, pltpu.roll(keys, extent - by, axis), pltpu.roll(keys, by, axis)
            )
            ascending = (at & size) == 0
            keys = jnp.where(
                lower == ascending, jnp.minimum(keys, partner), jnp.maximum(keys, partner)
            )
            distance //= 2
        size *= 2
    return keys


def slots_kernel(frame_rows, all_rows, nbr_ref, deg_ref, after_ref, near_ids, far_ids, full_ids, counts_ref):
    slots = nbr_ref.shape[0]
    first = lax.axis_index("feat") * 16
    rows = pl.ds(pl.multiple_of(first, 8), 8)
    degree = deg_ref[rows, :]
    near, far = [], []
    near_count = jnp.zeros((8, LANES), jnp.int32)
    for j in range(slots):
        nbr = nbr_ref[j, rows, :]
        used = degree > j
        is_near = used & (nbr < frame_rows)
        near.append(jnp.where(is_near, nbr, all_rows))
        far.append(jnp.where(used & (nbr >= frame_rows), nbr, all_rows))
        near_count = near_count + is_near.astype(jnp.int32)
    for j, ids in enumerate(sort_network(near)):
        near_ids[j] = ids
    for j, ids in enumerate(sort_network(far)):
        far_ids[j] = ids
    counts_ref[0] = near_count
    counts_ref[1] = degree - near_count
    rows = pl.ds(pl.multiple_of(first + 8, 8), 8)
    degree = deg_ref[rows, :]
    for j in range(slots):
        full_ids[j] = jnp.where(degree > j, nbr_ref[j, rows, :], all_rows)
    counts_ref[2] = degree


def order_kernel(counts_ref, after_ref, *refs):
    orders, classes = refs[:3], refs[3:]
    at = lax.broadcasted_iota(jnp.int32, (8, LANES), 0) * LANES + lax.broadcasted_iota(
        jnp.int32, (8, LANES), 1
    )
    keys = sorted_tiles(counts_ref[...] * CHUNK + at[None])
    for i in range(3):
        orders[i][...] = keys[i] & (CHUNK - 1)
        classes[i][...] = keys[i] >> 10


def constants_kernel(deg_ref, weight_ref, bias_ref, after_ref, scale_ref, weight_out, bias_out):
    tiles = scale_ref.shape[0] // LANES
    first = pl.multiple_of(lax.axis_index("feat") * tiles, tiles)
    inverse = 1.0 / (deg_ref[pl.ds(first, tiles), :] + 1).astype(jnp.float32)
    for t in range(tiles):
        scale_ref[LANES * t : LANES * (t + 1), :] = jnp.broadcast_to(
            inverse[t : t + 1, :], (LANES, LANES)
        ).T
    weight_out[...] = weight_ref[...].astype(jnp.float32).T.astype(jnp.bfloat16)
    bias_out[...] = jnp.broadcast_to(bias_ref[...], (LANES, LANES)).T


def add_tree(parts):
    while len(parts) > 1:
        tail = [parts[-1]] if len(parts) % 2 else []
        parts = [parts[i] + parts[i + 1] for i in range(0, len(parts) - 1, 2)] + tail
    return parts[0]


def load_plan(slots, start, ids_ref, order_ref, class_ref, slot_ids, order, classes, sem):
    size = order.shape[0]
    rows = pl.ds(start, size)
    first = [
        pltpu.make_async_copy(order_ref.at[rows], order, sem.at[slots]),
        pltpu.make_async_copy(class_ref.at[rows], classes.at[pl.ds(0, size)], sem.at[slots + 1]),
    ]
    by_slot = [
        pltpu.make_async_copy(
            ids_ref.at[pl.ds(j * CHUNK + start, size)], slot_ids.at[pl.ds(j * size, size)], sem.at[j]
        )
        for j in range(slots)
    ]
    for copy in first + by_slot:
        copy.start()
    return first, by_slot


def sum_slots(slots, start, part, parts, plan_refs, frame_ref, total_ref, slot_ids, order, classes, sem):
    size = order.shape[0]
    first, by_slot = load_plan(slots, start, *plan_refs, slot_ids, order, classes, sem)
    total_ref[...] = jnp.zeros_like(total_ref)
    for copy in first:
        copy.wait()
    last = GROUP - 1
    classes[size + part * GROUP + last] = slots + 1
    of_slot = [slot_ids.at[pl.ds(j * size, size)] for j in range(slots)]

    def body(count, carry):
        base, _ = carry
        for k in range(GROUP):
            node = order[base + k]
            total_ref[pl.ds(node, 1), :] = add_tree(
                [frame_ref[pl.ds(of_slot[j][node], 1), :] for j in range(count)]
            )
        return base + parts * GROUP, classes[base + parts * GROUP + last]

    def skip(carry):
        base, _ = carry
        return base + parts * GROUP, classes[base + parts * GROUP + last]

    carry = (jnp.int32(part * GROUP), classes[part * GROUP + last])
    carry = lax.while_loop(lambda carry: carry[1] == 0, skip, carry)
    for count in range(1, slots + 1):
        by_slot[count - 1].wait()
        carry = lax.while_loop(
            lambda carry, count=count: carry[1] == count, functools.partial(body, count), carry
        )


def near_kernel(slots, part, parts, ids_ref, order_ref, class_ref, frame_ref, after_ref, total_ref, *plan):
    sum_slots(slots, 0, part, parts, (ids_ref, order_ref, class_ref), frame_ref, total_ref, *plan)


def layer_kernel(slots, first, start, parts, own, ids_ref, order_ref, class_ref, frame_ref, scale_ref, weight_ref, bias_ref, after_ref, *refs):
    near, (keep_ref, send_ref, total_ref), plan = refs[:parts], refs[parts : parts + 3], refs[parts + 3 :]
    sum_slots(slots, start, 0, 1, (ids_ref, order_ref, class_ref), frame_ref, total_ref, *plan)
    chans, size = keep_ref.shape
    feat = lax.axis_index("feat")
    step = 256
    for at in range(0, size, step):
        rows = slice(at, at + step)
        own_at = pl.multiple_of(own + feat * own + first + at, step)
        total = total_ref[rows, :] + frame_ref[pl.ds(own_at, step), :]
        for ref in near:
            total = total + ref[rows, :]
        product = lax.dot_general(
            weight_ref[...],
            (total * scale_ref[first + at : first + at + step, :]).astype(jnp.bfloat16),
            (((1,), (1,)), ((), ())),
            preferred_element_type=jnp.float32,
        )
        bias = jnp.concatenate([bias_ref[...]] * (step // LANES), axis=1)
        result = jnp.maximum(product + bias, 0.0)
        low, high = result[:chans], result[chans:]
        keep_ref[:, rows] = jnp.where(feat == 0, low, high).astype(jnp.bfloat16)
        if send_ref.shape[0] == chans:
            result = jnp.where(feat == 0, high, low)
        send_ref[:, rows] = result.astype(jnp.bfloat16)


def output_kernel(*refs):
    out_ref = refs[-1]
    count = len(refs) // 2
    feat = lax.axis_index("feat")
    chans = out_ref.shape[0]
    for refs, part in ((refs[:count], feat), (refs[count:-1], 1 - feat)):
        at = part * (out_ref.shape[1] // 2)
        for ref in refs:
            size = ref.shape[1]
            rows = pl.ds(pl.multiple_of(feat * chans, chans), chans) if ref.shape[0] > chans else slice(None)
            out_ref[:, pl.ds(pl.multiple_of(at, size), size)] = ref[rows, :]
            at = at + size


def pallas(kernel, out_shape, in_specs, scratch=(), us=1.0, aliases=None):
    return pl.pallas_call(
        kernel,
        out_shape=out_shape,
        in_specs=in_specs,
        out_specs=jax.tree.map(lambda _: IN_VMEM, out_shape),
        scratch_shapes=list(scratch),
        input_output_aliases=aliases or {},
        compiler_params=pltpu.CompilerParams(vmem_limit_bytes=6 * 2**20),
        cost_estimate=pl.CostEstimate(flops=0, bytes_accessed=int(us * 3_000_000), transcendentals=0),
    )


IN_VMEM = pl.BlockSpec(memory_space=VMEM)
ANYWHERE = pl.BlockSpec(memory_space=pl.ANY)


def local(node_feats, neighbours, degrees, hub_rows, weight, bias_terms):
    chans, nodes = node_feats.shape
    slots = neighbours.shape[0]
    hubs = hub_rows.shape[0]
    slabs = lax.axis_size("slab")
    half = nodes // 2
    chunks = half // CHUNK
    frame_rows, hub_count = 2 * half + nodes, slabs * hubs
    swap = [(0, 1), (1, 0)]

    def bf16(*shape):
        return jax.ShapeDtypeStruct(shape, jnp.bfloat16)

    def f32(*shape):
        return jax.ShapeDtypeStruct(shape, jnp.float32)

    def i32(*shape):
        return jax.ShapeDtypeStruct(shape, jnp.int32)

    block = pallas(
        hub_pick_kernel,
        bf16(hubs // 2, 2 * chans),
        [IN_VMEM, ANYWHERE],
        [VMEM((chans, nodes), jnp.bfloat16), pltpu.SemaphoreType.DMA((4,))],
    )(hub_rows[None, :], node_feats)
    arrived = None

    def stage(block, bits):
        return [lax.ppermute(block, "slab", [(i, i ^ bit) for i in range(slabs)]) for bit in bits]

    def join(block, arrived, after):
        rows = block.shape[0] * (1 + len(arrived))
        specs = [IN_VMEM] * (1 + len(arrived)) + [ANYWHERE]
        return pallas(join_kernel, bf16(rows, 2 * chans), specs, us=0.5)(block, *arrived, after)

    arrived = stage(block, STAGES[0])
    deg_tiles = degrees.reshape(nodes // LANES, LANES)
    table, tile = i32(slots, 8, LANES), i32(8, LANES)
    *ids, counts = pallas(
        functools.partial(slots_kernel, frame_rows, frame_rows + hub_count),
        (table, table, table, i32(3, 8, LANES)),
        [IN_VMEM, IN_VMEM, ANYWHERE],
        us=1.0,
    )(neighbours.reshape(slots, nodes // LANES, LANES), deg_tiles, block)
    other = lax.ppermute(node_feats, "feat", swap)

    block = join(block, arrived, counts)
    arrived = stage(block, STAGES[1])
    order = pallas(order_kernel, (tile,) * 6, [IN_VMEM, ANYWHERE], us=3.0)(counts, block)
    near_plan, far_plan, full_plan = (
        [a.reshape(-1) for a in (ids[i], order[i], order[3 + i])] for i in range(3)
    )

    block = join(block, arrived, order[0])
    arrived = stage(block, STAGES[2])

    block = join(block, arrived, order[0])
    outer, inner = pallas(
        halves_kernel,
        (bf16(2 * chans, half),) * 2,
        [ANYWHERE] * 3,
        [pltpu.SemaphoreType.DMA((4,))],
        us=0.1,
    )(node_feats, other, block)
    inner_halo = lax.ppermute(inner, "slab", [(i, i ^ 1) for i in range(slabs)])
    outer_halo = lax.ppermute(
        outer, "slab", [(i, j) for i in range(slabs) for j in [i + 2 * (i & 1) - 1] if 0 <= j < slabs]
    )

    arrived = lax.ppermute(block, "feat", swap)
    scale, by_out, bias = pallas(
        constants_kernel,
        (f32(half, LANES), bf16(2 * chans, 2 * chans), f32(LANES, LANES)),
        [IN_VMEM] * 3 + [ANYWHERE],
        us=0.1,
    )(deg_tiles, weight, bias_terms[None, :], outer)
    block = pallas(
        join_feat_kernel, bf16(2 * block.shape[0], 2 * chans), [IN_VMEM] * 2 + [ANYWHERE], us=0.1
    )(block, arrived, scale)
    arrived = stage(block, STAGES[3])
    frame = pallas(
        frame_kernel,
        f32(frame_rows + hub_count + 8, LANES),
        [IN_VMEM] * 4 + [ANYWHERE],
        us=2.0,
    )(outer_halo, outer, inner, inner_halo, block)

    def plan_scratch(size):
        return [
            SMEM((slots * size,), jnp.int32),
            SMEM((size,), jnp.int32),
            SMEM((size + 2 * GROUP,), jnp.int32),
            pltpu.SemaphoreType.DMA((slots + 2,)),
        ]

    def near_sum(part, after):
        return pallas(
            functools.partial(near_kernel, slots, part, 2),
            f32(CHUNK, LANES),
            [ANYWHERE] * 3 + [IN_VMEM, ANYWHERE],
            plan_scratch(CHUNK),
            us=4.0,
        )(*near_plan, frame, after)

    near = [near_sum(0, block)]
    block = join(block, arrived, near[0])
    arrived = stage(block, STAGES[4])
    near.append(near_sum(1, block))
    frame = pallas(
        functools.partial(hub_frame_kernel, frame_rows, hubs),
        f32(*frame.shape),
        [IN_VMEM] * 3 + [ANYWHERE],
        us=0.5,
        aliases={0: 0},
    )(frame, block, arrived[0], near[1])

    def layer(plan, first, start, size, sent_chans, near, after, us):
        return pallas(
            functools.partial(layer_kernel, slots, first, start, len(near), half),
            (bf16(chans, size), bf16(sent_chans, size)),
            [ANYWHERE] * 3 + [IN_VMEM] * 4 + [ANYWHERE] + [IN_VMEM] * len(near),
            [VMEM((size, LANES), jnp.float32)] + plan_scratch(size),
            us=us,
        )(*plan, frame, scale, by_out, bias, after, *near)

    keep, received = [near[1]], []
    for plan, first, start, size, sent_chans, near, us in (
        (far_plan, 0, 0, CHUNK, 2 * chans, near, 3.0),
        (full_plan, CHUNK, 0, CHUNK, chans, [], 8.0),
    ):
        kept, sent = layer(plan, first, start, size, sent_chans, near, keep[-1], us)
        keep.append(kept)
        received.append(lax.ppermute(sent, "feat", swap))
    pieces = keep[1:] + received
    return pallas(output_kernel, bf16(chans, nodes), [IN_VMEM] * len(pieces), us=0.5)(*pieces)


def solution(mesh):
    in_specs = (P("feat", "slab"), P(None, "slab"), P("slab"), P("slab"), P(), P())
    return jax.shard_map(local, mesh=mesh, in_specs=in_specs, out_specs=P("feat", "slab"), check_vma=False)
```

```python
import functools

import jax
import jax.numpy as jnp
from jax import lax
from jax.experimental import pallas as pl
from jax.experimental.pallas import tpu as pltpu
from jax.sharding import PartitionSpec as P

VMEM = pltpu.VMEM
SMEM = pltpu.SMEM
LANES = 128
CHUNK = 1024
GROUP = 16
STAGES = ((32,), (64,), (8, 16, 24), (2, 4, 6), (1,))


def hub_pick_kernel(rows_ref, x_ref, out_ref, x_out_ref):
    hubs, nodes = rows_ref.shape[1], x_ref.shape[1]
    diagonal = lax.broadcasted_iota(jnp.int32, (hubs, hubs), 0) == lax.broadcasted_iota(
        jnp.int32, (hubs, hubs), 1
    )
    rows = jnp.sum(jnp.where(diagonal, rows_ref[...], 0), axis=1, keepdims=True)
    onehot = (lax.broadcasted_iota(jnp.int32, (hubs, nodes), 1) == rows).astype(jnp.bfloat16)
    picked = lax.dot_general(
        onehot, x_ref[...], (((1,), (1,)), ((), ())), preferred_element_type=jnp.float32
    ).astype(jnp.bfloat16)
    out_ref[...] = jnp.concatenate([picked[: hubs // 2], picked[hubs // 2 :]], axis=1)
    x_out_ref[...] = x_ref[...]


def join_kernel(*refs):
    blocks, out_ref = refs[:-2], refs[-1]
    rows = blocks[0].shape[0]
    for i, ref in enumerate(blocks):
        out_ref[i * rows : (i + 1) * rows] = ref[...]


def join_feat_kernel(mine_ref, other_ref, after_ref, out_ref):
    first = lax.axis_index("feat") == 0
    lane = lax.broadcasted_iota(jnp.int32, (16, LANES), 1)
    for i in range(mine_ref.shape[0] // 16):
        mine = mine_ref[16 * i : 16 * i + 16, :].astype(jnp.float32)
        other = other_ref[16 * i : 16 * i + 16, :].astype(jnp.float32)
        low = jnp.where(first, mine, other)
        high = jnp.where(first, other, mine)
        row = jnp.where(lane < LANES // 2, low, pltpu.roll(high, LANES // 2, 1))
        out_ref[32 * i : 32 * i + 16, :] = row.astype(jnp.bfloat16)
        row = jnp.where(lane < LANES // 2, pltpu.roll(low, LANES // 2, 1), high)
        out_ref[32 * i + 16 : 32 * i + 32, :] = row.astype(jnp.bfloat16)


def halves_kernel(x_ref, other_ref, after_ref, outer_ref, inner_ref, sem):
    feat = lax.axis_index("feat")
    odd = lax.axis_index("slab") & 1
    chans, half = x_ref.shape[0], outer_ref.shape[1]
    copies = []
    for ref, channels in ((x_ref, feat), (other_ref, 1 - feat)):
        rows = pl.ds(pl.multiple_of(channels * chans, chans), chans)
        for out_ref, part in ((outer_ref, odd), (inner_ref, 1 - odd)):
            cols = pl.ds(pl.multiple_of(part * half, half), half)
            copies.append(
                pltpu.make_async_copy(ref.at[:, cols], out_ref.at[rows, :], sem.at[len(copies)])
            )
    for copy in copies:
        copy.start()
    for copy in copies:
        copy.wait()


def frame_kernel(outer_halo_ref, outer_ref, inner_ref, inner_halo_ref, after_ref, frame_ref):
    odd = lax.axis_index("slab") & 1
    half = outer_ref.shape[1]
    step = 256
    unit = (
        lax.broadcasted_iota(jnp.int32, (step, step), 0)
        == lax.broadcasted_iota(jnp.int32, (step, step), 1)
    ).astype(jnp.bfloat16)
    for place, ref in enumerate((outer_halo_ref, outer_ref, inner_ref, inner_halo_ref)):
        first = (place + odd * (3 - 2 * place)) * half
        for at in range(0, half, step):
            frame_ref[pl.ds(pl.multiple_of(first + at, step), step), :] = lax.dot_general(
                unit,
                ref[:, at : at + step],
                (((1,), (1,)), ((), ())),
                preferred_element_type=jnp.float32,
            )
    rows = frame_ref.shape[0]
    frame_ref[rows - 8 :, :] = jnp.zeros((8, LANES), jnp.float32)


def origins():
    differs = [0]
    for bits in STAGES:
        differs = [d ^ bit for bit in (0,) + bits for d in differs]
    return differs


def hub_frame_kernel(first, hubs, frame_in, near_ref, far_ref, after_ref, frame_ref):
    blocks = near_ref.shape[0] // hubs
    me = lax.axis_index("slab")
    for p, differs in enumerate(origins()):
        ref, i = (near_ref, p) if p < blocks else (far_ref, p - blocks)
        at = pl.multiple_of(first + (me ^ differs) * hubs, hubs)
        frame_ref[pl.ds(at, hubs), :] = ref[hubs * i : hubs * (i + 1), :].astype(jnp.float32)


def comparators(count):
    pairs, p = [], 1
    while p < count:
        k = p
        while k >= 1:
            for j in range(k % p, count - k, 2 * k):
                for i in range(min(k, count - j - k)):
                    if (i + j) // (2 * p) == (i + j + k) // (2 * p):
                        pairs.append((i + j, i + j + k))
            k //= 2
        p *= 2
    return pairs


def sort_network(values):
    for a, b in comparators(len(values)):
        values[a], values[b] = jnp.minimum(values[a], values[b]), jnp.maximum(values[a], values[b])
    return values


def sorted_tiles(keys):
    shape = keys.shape
    sub = lax.broadcasted_iota(jnp.int32, shape, 1)
    lane = lax.broadcasted_iota(jnp.int32, shape, 2)
    at = sub * LANES + lane
    size = 2
    while size <= CHUNK:
        distance = size // 2
        while distance >= 1:
            axis, by, extent = (2, distance, LANES) if distance < LANES else (1, distance // LANES, 8)
            lower = (at & distance) == 0
            partner = jnp.where(
                lower, pltpu.roll(keys, extent - by, axis), pltpu.roll(keys, by, axis)
            )
            ascending = (at & size) == 0
            keys = jnp.where(
                lower == ascending, jnp.minimum(keys, partner), jnp.maximum(keys, partner)
            )
            distance //= 2
        size *= 2
    return keys


def slots_kernel(frame_rows, all_rows, nbr_ref, deg_ref, after_ref, near_ids, far_ids, full_ids, counts_ref):
    slots = nbr_ref.shape[0]
    first = lax.axis_index("feat") * 16
    rows = pl.ds(pl.multiple_of(first, 8), 8)
    degree = deg_ref[rows, :]
    near, far = [], []
    near_count = jnp.zeros((8, LANES), jnp.int32)
    for j in range(slots):
        nbr = nbr_ref[j, rows, :]
        used = degree > j
        is_near = used & (nbr < frame_rows)
        near.append(jnp.where(is_near, nbr, all_rows))
        far.append(jnp.where(used & (nbr >= frame_rows), nbr, all_rows))
        near_count = near_count + is_near.astype(jnp.int32)
    for j, ids in enumerate(sort_network(near)):
        near_ids[j] = ids
    for j, ids in enumerate(sort_network(far)):
        far_ids[j] = ids
    counts_ref[0] = near_count
    counts_ref[1] = degree - near_count
    rows = pl.ds(pl.multiple_of(first + 8, 8), 8)
    degree = deg_ref[rows, :]
    for j in range(slots):
        full_ids[j] = jnp.where(degree > j, nbr_ref[j, rows, :], all_rows)
    counts_ref[2] = degree


def order_kernel(counts_ref, after_ref, *refs):
    orders, classes = refs[:3], refs[3:]
    at = lax.broadcasted_iota(jnp.int32, (8, LANES), 0) * LANES + lax.broadcasted_iota(
        jnp.int32, (8, LANES), 1
    )
    keys = sorted_tiles(counts_ref[...] * CHUNK + at[None])
    for i in range(3):
        orders[i][...] = keys[i] & (CHUNK - 1)
        classes[i][...] = keys[i] >> 10


def constants_kernel(deg_ref, weight_ref, bias_ref, after_ref, scale_ref, weight_out, bias_out):
    tiles = scale_ref.shape[0] // LANES
    first = pl.multiple_of(lax.axis_index("feat") * tiles, tiles)
    inverse = 1.0 / (deg_ref[pl.ds(first, tiles), :] + 1).astype(jnp.float32)
    for t in range(tiles):
        scale_ref[LANES * t : LANES * (t + 1), :] = jnp.broadcast_to(
            inverse[t : t + 1, :], (LANES, LANES)
        ).T
    weight_out[...] = weight_ref[...].astype(jnp.float32).T.astype(jnp.bfloat16)
    bias_out[...] = jnp.broadcast_to(bias_ref[...], (LANES, LANES)).T


def add_tree(parts):
    while len(parts) > 1:
        tail = [parts[-1]] if len(parts) % 2 else []
        parts = [parts[i] + parts[i + 1] for i in range(0, len(parts) - 1, 2)] + tail
    return parts[0]


def load_plan(slots, start, ids_ref, order_ref, class_ref, slot_ids, order, classes, sem):
    size = order.shape[0]
    rows = pl.ds(start, size)
    first = [
        pltpu.make_async_copy(order_ref.at[rows], order, sem.at[slots]),
        pltpu.make_async_copy(class_ref.at[rows], classes.at[pl.ds(0, size)], sem.at[slots + 1]),
    ]
    by_slot = [
        pltpu.make_async_copy(
            ids_ref.at[pl.ds(j * CHUNK + start, size)], slot_ids.at[pl.ds(j * size, size)], sem.at[j]
        )
        for j in range(slots)
    ]
    for copy in first + by_slot:
        copy.start()
    return first, by_slot


def sum_slots(slots, start, part, parts, plan_refs, frame_ref, total_ref, slot_ids, order, classes, sem):
    size = order.shape[0]
    first, by_slot = load_plan(slots, start, *plan_refs, slot_ids, order, classes, sem)
    total_ref[...] = jnp.zeros_like(total_ref)
    for copy in first:
        copy.wait()
    last = GROUP - 1
    classes[size + part * GROUP + last] = slots + 1
    of_slot = [slot_ids.at[pl.ds(j * size, size)] for j in range(slots)]

    def body(count, carry):
        base, _ = carry
        for k in range(GROUP):
            node = order[base + k]
            total_ref[pl.ds(node, 1), :] = add_tree(
                [frame_ref[pl.ds(of_slot[j][node], 1), :] for j in range(count)]
            )
        return base + parts * GROUP, classes[base + parts * GROUP + last]

    def skip(carry):
        base, _ = carry
        return base + parts * GROUP, classes[base + parts * GROUP + last]

    carry = (jnp.int32(part * GROUP), classes[part * GROUP + last])
    carry = lax.while_loop(lambda carry: carry[1] == 0, skip, carry)
    for count in range(1, slots + 1):
        by_slot[count - 1].wait()
        carry = lax.while_loop(
            lambda carry, count=count: carry[1] == count, functools.partial(body, count), carry
        )


def near_kernel(slots, part, parts, ids_ref, order_ref, class_ref, frame_ref, after_ref, total_ref, *plan):
    sum_slots(slots, 0, part, parts, (ids_ref, order_ref, class_ref), frame_ref, total_ref, *plan)


def layer_kernel(slots, first, start, parts, own, ids_ref, order_ref, class_ref, frame_ref, scale_ref, weight_ref, bias_ref, after_ref, *refs):
    near, (keep_ref, send_ref, total_ref), plan = refs[:parts], refs[parts : parts + 3], refs[parts + 3 :]
    sum_slots(slots, start, 0, 1, (ids_ref, order_ref, class_ref), frame_ref, total_ref, *plan)
    chans, size = keep_ref.shape
    feat = lax.axis_index("feat")
    step = 256
    for at in range(0, size, step):
        rows = slice(at, at + step)
        own_at = pl.multiple_of(own + feat * own + first + at, step)
        total = total_ref[rows, :] + frame_ref[pl.ds(own_at, step), :]
        for ref in near:
            total = total + ref[rows, :]
        product = lax.dot_general(
            weight_ref[...],
            (total * scale_ref[first + at : first + at + step, :]).astype(jnp.bfloat16),
            (((1,), (1,)), ((), ())),
            preferred_element_type=jnp.float32,
        )
        bias = jnp.concatenate([bias_ref[...]] * (step // LANES), axis=1)
        result = jnp.maximum(product + bias, 0.0)
        low, high = result[:chans], result[chans:]
        keep_ref[:, rows] = jnp.where(feat == 0, low, high).astype(jnp.bfloat16)
        if send_ref.shape[0] == chans:
            result = jnp.where(feat == 0, high, low)
        send_ref[:, rows] = result.astype(jnp.bfloat16)


def output_kernel(*refs):
    out_ref = refs[-1]
    count = len(refs) // 2
    feat = lax.axis_index("feat")
    chans = out_ref.shape[0]
    for refs, part in ((refs[:count], feat), (refs[count:-1], 1 - feat)):
        at = part * (out_ref.shape[1] // 2)
        for ref in refs:
            size = ref.shape[1]
            rows = pl.ds(pl.multiple_of(feat * chans, chans), chans) if ref.shape[0] > chans else slice(None)
            out_ref[:, pl.ds(pl.multiple_of(at, size), size)] = ref[rows, :]
            at = at + size


def pallas(kernel, out_shape, in_specs, scratch=(), us=1.0, aliases=None):
    return pl.pallas_call(
        kernel,
        out_shape=out_shape,
        in_specs=in_specs,
        out_specs=jax.tree.map(lambda _: IN_VMEM, out_shape),
        scratch_shapes=list(scratch),
        input_output_aliases=aliases or {},
        compiler_params=pltpu.CompilerParams(vmem_limit_bytes=6 * 2**20),
        cost_estimate=pl.CostEstimate(flops=0, bytes_accessed=int(us * 3_000_000), transcendentals=0),
    )


IN_VMEM = pl.BlockSpec(memory_space=VMEM)
ANYWHERE = pl.BlockSpec(memory_space=pl.ANY)


def local(node_feats, neighbours, degrees, hub_rows, weight, bias_terms):
    chans, nodes = node_feats.shape
    slots = neighbours.shape[0]
    hubs = hub_rows.shape[0]
    slabs = lax.axis_size("slab")
    half = nodes // 2
    chunks = half // CHUNK
    frame_rows, hub_count = 2 * half + nodes, slabs * hubs
    swap = [(0, 1), (1, 0)]

    def bf16(*shape):
        return jax.ShapeDtypeStruct(shape, jnp.bfloat16)

    def f32(*shape):
        return jax.ShapeDtypeStruct(shape, jnp.float32)

    def i32(*shape):
        return jax.ShapeDtypeStruct(shape, jnp.int32)

    block, own_feats = pallas(
        hub_pick_kernel, (bf16(hubs // 2, 2 * chans), bf16(chans, nodes)), [IN_VMEM] * 2
    )(hub_rows[None, :], node_feats)
    arrived = None

    def stage(block, bits):
        return [lax.ppermute(block, "slab", [(i, i ^ bit) for i in range(slabs)]) for bit in bits]

    def join(block, arrived, after):
        rows = block.shape[0] * (1 + len(arrived))
        specs = [IN_VMEM] * (1 + len(arrived)) + [ANYWHERE]
        return pallas(join_kernel, bf16(rows, 2 * chans), specs, us=0.5)(block, *arrived, after)

    arrived = stage(block, STAGES[0])
    deg_tiles = degrees.reshape(nodes // LANES, LANES)
    table, tile = i32(slots, 8, LANES), i32(8, LANES)
    *ids, counts = pallas(
        functools.partial(slots_kernel, frame_rows, frame_rows + hub_count),
        (table, table, table, i32(3, 8, LANES)),
        [IN_VMEM, IN_VMEM, ANYWHERE],
        us=1.0,
    )(neighbours.reshape(slots, nodes // LANES, LANES), deg_tiles, block)
    other = lax.ppermute(node_feats, "feat", swap)

    block = join(block, arrived, counts)
    arrived = stage(block, STAGES[1])
    order = pallas(order_kernel, (tile,) * 6, [IN_VMEM, ANYWHERE], us=3.0)(counts, block)
    near_plan, far_plan, full_plan = (
        [a.reshape(-1) for a in (ids[i], order[i], order[3 + i])] for i in range(3)
    )

    block = join(block, arrived, order[0])
    arrived = lax.ppermute(block, "feat", swap)
    scale, by_out, bias = pallas(
        constants_kernel,
        (f32(half, LANES), bf16(2 * chans, 2 * chans), f32(LANES, LANES)),
        [IN_VMEM] * 3 + [ANYWHERE],
        us=0.1,
    )(deg_tiles, weight, bias_terms[None, :], block)
    block = pallas(
        join_feat_kernel, bf16(2 * block.shape[0], 2 * chans), [IN_VMEM] * 2 + [ANYWHERE], us=0.1
    )(block, arrived, scale)

    outer, inner = pallas(
        halves_kernel,
        (bf16(2 * chans, half),) * 2,
        [ANYWHERE] * 3,
        [pltpu.SemaphoreType.DMA((4,))],
        us=0.1,
    )(own_feats, other, block)
    inner_halo = lax.ppermute(inner, "slab", [(i, i ^ 1) for i in range(slabs)])
    outer_halo = lax.ppermute(
        outer, "slab", [(i, j) for i in range(slabs) for j in [i + 2 * (i & 1) - 1] if 0 <= j < slabs]
    )
    arrived = stage(block, STAGES[2])
    block = join(block, arrived, outer)
    arrived = stage(block, STAGES[3])
    frame = pallas(
        frame_kernel,
        f32(frame_rows + hub_count + 8, LANES),
        [IN_VMEM] * 4 + [ANYWHERE],
        us=2.0,
    )(outer_halo, outer, inner, inner_halo, block)

    def plan_scratch(size):
        return [
            SMEM((slots * size,), jnp.int32),
            SMEM((size,), jnp.int32),
            SMEM((size + 2 * GROUP,), jnp.int32),
            pltpu.SemaphoreType.DMA((slots + 2,)),
        ]

    def near_sum(part, after):
        return pallas(
            functools.partial(near_kernel, slots, part, 2),
            f32(CHUNK, LANES),
            [ANYWHERE] * 3 + [IN_VMEM, ANYWHERE],
            plan_scratch(CHUNK),
            us=4.0,
        )(*near_plan, frame, after)

    near = [near_sum(0, block)]
    block = join(block, arrived, near[0])
    arrived = stage(block, STAGES[4])
    near.append(near_sum(1, block))
    frame = pallas(
        functools.partial(hub_frame_kernel, frame_rows, hubs),
        f32(*frame.shape),
        [IN_VMEM] * 3 + [ANYWHERE],
        us=0.5,
        aliases={0: 0},
    )(frame, block, arrived[0], near[1])

    def layer(plan, first, start, size, sent_chans, near, after, us):
        return pallas(
            functools.partial(layer_kernel, slots, first, start, len(near), half),
            (bf16(chans, size), bf16(sent_chans, size)),
            [ANYWHERE] * 3 + [IN_VMEM] * 4 + [ANYWHERE] + [IN_VMEM] * len(near),
            [VMEM((size, LANES), jnp.float32)] + plan_scratch(size),
            us=us,
        )(*plan, frame, scale, by_out, bias, after, *near)

    keep, received = [near[1]], []
    for plan, first, start, size, sent_chans, near, us in (
        (far_plan, 0, 0, CHUNK, 2 * chans, near, 3.0),
        (full_plan, CHUNK, 0, CHUNK, chans, [], 8.0),
    ):
        kept, sent = layer(plan, first, start, size, sent_chans, near, keep[-1], us)
        keep.append(kept)
        received.append(lax.ppermute(sent, "feat", swap))
    pieces = keep[1:] + received
    return pallas(output_kernel, bf16(chans, nodes), [IN_VMEM] * len(pieces), us=0.5)(*pieces)


def solution(mesh):
    in_specs = (P("feat", "slab"), P(None, "slab"), P("slab"), P("slab"), P(), P())
    return jax.shard_map(local, mesh=mesh, in_specs=in_specs, out_specs=P("feat", "slab"), check_vma=False)
```

```python
import functools

import jax
import jax.numpy as jnp
from jax import lax
from jax.experimental import pallas as pl
from jax.experimental.pallas import tpu as pltpu
from jax.sharding import PartitionSpec as P

VMEM = pltpu.VMEM
SMEM = pltpu.SMEM
LANES = 128
CHUNK = 1024
GROUP = 16
STAGES = ((32,), (64,), (8, 16, 24), (4,), (2,), (1,))


def hub_pick_kernel(rows_ref, x_ref, out_ref, x_out_ref):
    hubs, nodes = rows_ref.shape[1], x_ref.shape[1]
    diagonal = lax.broadcasted_iota(jnp.int32, (hubs, hubs), 0) == lax.broadcasted_iota(
        jnp.int32, (hubs, hubs), 1
    )
    rows = jnp.sum(jnp.where(diagonal, rows_ref[...], 0), axis=1, keepdims=True)
    onehot = (lax.broadcasted_iota(jnp.int32, (hubs, nodes), 1) == rows).astype(jnp.bfloat16)
    picked = lax.dot_general(
        onehot, x_ref[...], (((1,), (1,)), ((), ())), preferred_element_type=jnp.float32
    ).astype(jnp.bfloat16)
    out_ref[...] = jnp.concatenate([picked[: hubs // 2], picked[hubs // 2 :]], axis=1)
    x_out_ref[...] = x_ref[...]


def join_kernel(*refs):
    blocks, out_ref = refs[:-2], refs[-1]
    rows = blocks[0].shape[0]
    for i, ref in enumerate(blocks):
        out_ref[i * rows : (i + 1) * rows] = ref[...]


def join_feat_kernel(mine_ref, other_ref, after_ref, out_ref):
    first = lax.axis_index("feat") == 0
    lane = lax.broadcasted_iota(jnp.int32, (16, LANES), 1)
    for i in range(mine_ref.shape[0] // 16):
        mine = mine_ref[16 * i : 16 * i + 16, :].astype(jnp.float32)
        other = other_ref[16 * i : 16 * i + 16, :].astype(jnp.float32)
        low = jnp.where(first, mine, other)
        high = jnp.where(first, other, mine)
        row = jnp.where(lane < LANES // 2, low, pltpu.roll(high, LANES // 2, 1))
        out_ref[32 * i : 32 * i + 16, :] = row.astype(jnp.bfloat16)
        row = jnp.where(lane < LANES // 2, pltpu.roll(low, LANES // 2, 1), high)
        out_ref[32 * i + 16 : 32 * i + 32, :] = row.astype(jnp.bfloat16)


def halves_kernel(x_ref, other_ref, after_ref, outer_ref, inner_ref, sem):
    feat = lax.axis_index("feat")
    odd = lax.axis_index("slab") & 1
    chans, half = x_ref.shape[0], outer_ref.shape[1]
    copies = []
    for ref, channels in ((x_ref, feat), (other_ref, 1 - feat)):
        rows = pl.ds(pl.multiple_of(channels * chans, chans), chans)
        for out_ref, part in ((outer_ref, odd), (inner_ref, 1 - odd)):
            cols = pl.ds(pl.multiple_of(part * half, half), half)
            copies.append(
                pltpu.make_async_copy(ref.at[:, cols], out_ref.at[rows, :], sem.at[len(copies)])
            )
    for copy in copies:
        copy.start()
    for copy in copies:
        copy.wait()


def frame_kernel(outer_halo_ref, outer_ref, inner_ref, inner_halo_ref, after_ref, frame_ref):
    odd = lax.axis_index("slab") & 1
    half = outer_ref.shape[1]
    step = 256
    unit = (
        lax.broadcasted_iota(jnp.int32, (step, step), 0)
        == lax.broadcasted_iota(jnp.int32, (step, step), 1)
    ).astype(jnp.bfloat16)
    for place, ref in enumerate((outer_halo_ref, outer_ref, inner_ref, inner_halo_ref)):
        first = (place + odd * (3 - 2 * place)) * half
        for at in range(0, half, step):
            frame_ref[pl.ds(pl.multiple_of(first + at, step), step), :] = lax.dot_general(
                unit,
                ref[:, at : at + step],
                (((1,), (1,)), ((), ())),
                preferred_element_type=jnp.float32,
            )
    rows = frame_ref.shape[0]
    frame_ref[rows - 8 :, :] = jnp.zeros((8, LANES), jnp.float32)


def origins():
    differs = [0]
    for bits in STAGES:
        differs = [d ^ bit for bit in (0,) + bits for d in differs]
    return differs


def hub_frame_kernel(first, hubs, frame_in, near_ref, far_ref, after_ref, frame_ref):
    blocks = near_ref.shape[0] // hubs
    me = lax.axis_index("slab")
    for p, differs in enumerate(origins()):
        ref, i = (near_ref, p) if p < blocks else (far_ref, p - blocks)
        at = pl.multiple_of(first + (me ^ differs) * hubs, hubs)
        frame_ref[pl.ds(at, hubs), :] = ref[hubs * i : hubs * (i + 1), :].astype(jnp.float32)


def comparators(count):
    pairs, p = [], 1
    while p < count:
        k = p
        while k >= 1:
            for j in range(k % p, count - k, 2 * k):
                for i in range(min(k, count - j - k)):
                    if (i + j) // (2 * p) == (i + j + k) // (2 * p):
                        pairs.append((i + j, i + j + k))
            k //= 2
        p *= 2
    return pairs


def sort_network(values):
    for a, b in comparators(len(values)):
        values[a], values[b] = jnp.minimum(values[a], values[b]), jnp.maximum(values[a], values[b])
    return values


def sorted_tiles(keys):
    shape = keys.shape
    sub = lax.broadcasted_iota(jnp.int32, shape, 1)
    lane = lax.broadcasted_iota(jnp.int32, shape, 2)
    at = sub * LANES + lane
    size = 2
    while size <= CHUNK:
        distance = size // 2
        while distance >= 1:
            axis, by, extent = (2, distance, LANES) if distance < LANES else (1, distance // LANES, 8)
            lower = (at & distance) == 0
            partner = jnp.where(
                lower, pltpu.roll(keys, extent - by, axis), pltpu.roll(keys, by, axis)
            )
            ascending = (at & size) == 0
            keys = jnp.where(
                lower == ascending, jnp.minimum(keys, partner), jnp.maximum(keys, partner)
            )
            distance //= 2
        size *= 2
    return keys


def slots_kernel(frame_rows, all_rows, nbr_ref, deg_ref, after_ref, near_ids, far_ids, full_ids, counts_ref):
    slots = nbr_ref.shape[0]
    first = lax.axis_index("feat") * 16
    rows = pl.ds(pl.multiple_of(first, 8), 8)
    degree = deg_ref[rows, :]
    near, far = [], []
    near_count = jnp.zeros((8, LANES), jnp.int32)
    for j in range(slots):
        nbr = nbr_ref[j, rows, :]
        used = degree > j
        is_near = used & (nbr < frame_rows)
        near.append(jnp.where(is_near, nbr, all_rows))
        far.append(jnp.where(used & (nbr >= frame_rows), nbr, all_rows))
        near_count = near_count + is_near.astype(jnp.int32)
    for j, ids in enumerate(sort_network(near)):
        near_ids[j] = ids
    for j, ids in enumerate(sort_network(far)):
        far_ids[j] = ids
    counts_ref[0] = near_count
    counts_ref[1] = degree - near_count
    rows = pl.ds(pl.multiple_of(first + 8, 8), 8)
    degree = deg_ref[rows, :]
    for j in range(slots):
        full_ids[j] = jnp.where(degree > j, nbr_ref[j, rows, :], all_rows)
    counts_ref[2] = degree


def order_kernel(counts_ref, after_ref, *refs):
    orders, classes = refs[:3], refs[3:]
    at = lax.broadcasted_iota(jnp.int32, (8, LANES), 0) * LANES + lax.broadcasted_iota(
        jnp.int32, (8, LANES), 1
    )
    keys = sorted_tiles(counts_ref[...] * CHUNK + at[None])
    for i in range(3):
        orders[i][...] = keys[i] & (CHUNK - 1)
        classes[i][...] = keys[i] >> 10


def constants_kernel(deg_ref, weight_ref, bias_ref, after_ref, scale_ref, weight_out, bias_out):
    tiles = scale_ref.shape[0] // LANES
    first = pl.multiple_of(lax.axis_index("feat") * tiles, tiles)
    inverse = 1.0 / (deg_ref[pl.ds(first, tiles), :] + 1).astype(jnp.float32)
    for t in range(tiles):
        scale_ref[LANES * t : LANES * (t + 1), :] = jnp.broadcast_to(
            inverse[t : t + 1, :], (LANES, LANES)
        ).T
    weight_out[...] = weight_ref[...].astype(jnp.float32).T.astype(jnp.bfloat16)
    bias_out[...] = jnp.broadcast_to(bias_ref[...], (LANES, LANES)).T


def add_tree(parts):
    while len(parts) > 1:
        tail = [parts[-1]] if len(parts) % 2 else []
        parts = [parts[i] + parts[i + 1] for i in range(0, len(parts) - 1, 2)] + tail
    return parts[0]


def load_plan(slots, start, ids_ref, order_ref, class_ref, slot_ids, order, classes, sem):
    size = order.shape[0]
    rows = pl.ds(start, size)
    first = [
        pltpu.make_async_copy(order_ref.at[rows], order, sem.at[slots]),
        pltpu.make_async_copy(class_ref.at[rows], classes.at[pl.ds(0, size)], sem.at[slots + 1]),
    ]
    by_slot = [
        pltpu.make_async_copy(
            ids_ref.at[pl.ds(j * CHUNK + start, size)], slot_ids.at[pl.ds(j * size, size)], sem.at[j]
        )
        for j in range(slots)
    ]
    for copy in first + by_slot:
        copy.start()
    return first, by_slot


def sum_slots(slots, start, part, parts, plan_refs, frame_ref, total_ref, slot_ids, order, classes, sem):
    size = order.shape[0]
    first, by_slot = load_plan(slots, start, *plan_refs, slot_ids, order, classes, sem)
    total_ref[...] = jnp.zeros_like(total_ref)
    for copy in first:
        copy.wait()
    last = GROUP - 1
    classes[size + part * GROUP + last] = slots + 1
    of_slot = [slot_ids.at[pl.ds(j * size, size)] for j in range(slots)]

    def body(count, carry):
        base, _ = carry
        for k in range(GROUP):
            node = order[base + k]
            total_ref[pl.ds(node, 1), :] = add_tree(
                [frame_ref[pl.ds(of_slot[j][node], 1), :] for j in range(count)]
            )
        return base + parts * GROUP, classes[base + parts * GROUP + last]

    def skip(carry):
        base, _ = carry
        return base + parts * GROUP, classes[base + parts * GROUP + last]

    carry = (jnp.int32(part * GROUP), classes[part * GROUP + last])
    carry = lax.while_loop(lambda carry: carry[1] == 0, skip, carry)
    for count in range(1, slots + 1):
        by_slot[count - 1].wait()
        carry = lax.while_loop(
            lambda carry, count=count: carry[1] == count, functools.partial(body, count), carry
        )


def near_kernel(slots, part, parts, ids_ref, order_ref, class_ref, frame_ref, after_ref, total_ref, *plan):
    sum_slots(slots, 0, part, parts, (ids_ref, order_ref, class_ref), frame_ref, total_ref, *plan)


def layer_kernel(slots, first, start, parts, own, ids_ref, order_ref, class_ref, frame_ref, scale_ref, weight_ref, bias_ref, after_ref, *refs):
    near, (keep_ref, send_ref, total_ref), plan = refs[:parts], refs[parts : parts + 3], refs[parts + 3 :]
    sum_slots(slots, start, 0, 1, (ids_ref, order_ref, class_ref), frame_ref, total_ref, *plan)
    chans, size = keep_ref.shape
    feat = lax.axis_index("feat")
    step = 256
    for at in range(0, size, step):
        rows = slice(at, at + step)
        own_at = pl.multiple_of(own + feat * own + first + at, step)
        total = total_ref[rows, :] + frame_ref[pl.ds(own_at, step), :]
        for ref in near:
            total = total + ref[rows, :]
        product = lax.dot_general(
            weight_ref[...],
            (total * scale_ref[first + at : first + at + step, :]).astype(jnp.bfloat16),
            (((1,), (1,)), ((), ())),
            preferred_element_type=jnp.float32,
        )
        bias = jnp.concatenate([bias_ref[...]] * (step // LANES), axis=1)
        result = jnp.maximum(product + bias, 0.0)
        low, high = result[:chans], result[chans:]
        keep_ref[:, rows] = jnp.where(feat == 0, low, high).astype(jnp.bfloat16)
        if send_ref.shape[0] == chans:
            result = jnp.where(feat == 0, high, low)
        send_ref[:, rows] = result.astype(jnp.bfloat16)


def output_kernel(*refs):
    out_ref = refs[-1]
    count = len(refs) // 2
    feat = lax.axis_index("feat")
    chans = out_ref.shape[0]
    for refs, part in ((refs[:count], feat), (refs[count:-1], 1 - feat)):
        at = part * (out_ref.shape[1] // 2)
        for ref in refs:
            size = ref.shape[1]
            rows = pl.ds(pl.multiple_of(feat * chans, chans), chans) if ref.shape[0] > chans else slice(None)
            out_ref[:, pl.ds(pl.multiple_of(at, size), size)] = ref[rows, :]
            at = at + size


def pallas(kernel, out_shape, in_specs, scratch=(), us=1.0, aliases=None):
    return pl.pallas_call(
        kernel,
        out_shape=out_shape,
        in_specs=in_specs,
        out_specs=jax.tree.map(lambda _: IN_VMEM, out_shape),
        scratch_shapes=list(scratch),
        input_output_aliases=aliases or {},
        compiler_params=pltpu.CompilerParams(vmem_limit_bytes=6 * 2**20),
        cost_estimate=pl.CostEstimate(flops=0, bytes_accessed=int(us * 3_000_000), transcendentals=0),
    )


IN_VMEM = pl.BlockSpec(memory_space=VMEM)
ANYWHERE = pl.BlockSpec(memory_space=pl.ANY)


def local(node_feats, neighbours, degrees, hub_rows, weight, bias_terms):
    chans, nodes = node_feats.shape
    slots = neighbours.shape[0]
    hubs = hub_rows.shape[0]
    slabs = lax.axis_size("slab")
    half = nodes // 2
    chunks = half // CHUNK
    frame_rows, hub_count = 2 * half + nodes, slabs * hubs
    swap = [(0, 1), (1, 0)]

    def bf16(*shape):
        return jax.ShapeDtypeStruct(shape, jnp.bfloat16)

    def f32(*shape):
        return jax.ShapeDtypeStruct(shape, jnp.float32)

    def i32(*shape):
        return jax.ShapeDtypeStruct(shape, jnp.int32)

    block, own_feats = pallas(
        hub_pick_kernel, (bf16(hubs // 2, 2 * chans), bf16(chans, nodes)), [IN_VMEM] * 2
    )(hub_rows[None, :], node_feats)
    arrived = None

    def stage(block, bits):
        return [lax.ppermute(block, "slab", [(i, i ^ bit) for i in range(slabs)]) for bit in bits]

    def join(block, arrived, after):
        rows = block.shape[0] * (1 + len(arrived))
        specs = [IN_VMEM] * (1 + len(arrived)) + [ANYWHERE]
        return pallas(join_kernel, bf16(rows, 2 * chans), specs, us=0.5)(block, *arrived, after)

    arrived = stage(block, STAGES[0])
    deg_tiles = degrees.reshape(nodes // LANES, LANES)
    table, tile = i32(slots, 8, LANES), i32(8, LANES)
    *ids, counts = pallas(
        functools.partial(slots_kernel, frame_rows, frame_rows + hub_count),
        (table, table, table, i32(3, 8, LANES)),
        [IN_VMEM, IN_VMEM, ANYWHERE],
        us=1.0,
    )(neighbours.reshape(slots, nodes // LANES, LANES), deg_tiles, block)
    other = lax.ppermute(node_feats, "feat", swap)

    block = join(block, arrived, counts)
    arrived = stage(block, STAGES[1])
    order = pallas(order_kernel, (tile,) * 6, [IN_VMEM, ANYWHERE], us=3.0)(counts, block)
    near_plan, far_plan, full_plan = (
        [a.reshape(-1) for a in (ids[i], order[i], order[3 + i])] for i in range(3)
    )

    block = join(block, arrived, order[0])
    arrived = stage(block, STAGES[2])

    block = join(block, arrived, order[0])
    outer, inner = pallas(
        halves_kernel,
        (bf16(2 * chans, half),) * 2,
        [ANYWHERE] * 3,
        [pltpu.SemaphoreType.DMA((4,))],
        us=0.1,
    )(own_feats, other, block)
    inner_halo = lax.ppermute(inner, "slab", [(i, i ^ 1) for i in range(slabs)])
    outer_halo = lax.ppermute(
        outer, "slab", [(i, j) for i in range(slabs) for j in [i + 2 * (i & 1) - 1] if 0 <= j < slabs]
    )

    arrived = lax.ppermute(block, "feat", swap)
    scale, by_out, bias = pallas(
        constants_kernel,
        (f32(half, LANES), bf16(2 * chans, 2 * chans), f32(LANES, LANES)),
        [IN_VMEM] * 3 + [ANYWHERE],
        us=0.1,
    )(deg_tiles, weight, bias_terms[None, :], outer)
    block = pallas(
        join_feat_kernel, bf16(2 * block.shape[0], 2 * chans), [IN_VMEM] * 2 + [ANYWHERE], us=0.1
    )(block, arrived, scale)
    arrived = stage(block, STAGES[3])
    frame = pallas(
        frame_kernel,
        f32(frame_rows + hub_count + 8, LANES),
        [IN_VMEM] * 4 + [ANYWHERE],
        us=2.0,
    )(outer_halo, outer, inner, inner_halo, block)

    def plan_scratch(size):
        return [
            SMEM((slots * size,), jnp.int32),
            SMEM((size,), jnp.int32),
            SMEM((size + 2 * GROUP,), jnp.int32),
            pltpu.SemaphoreType.DMA((slots + 2,)),
        ]

    def near_sum(part, after):
        return pallas(
            functools.partial(near_kernel, slots, part, 2),
            f32(CHUNK, LANES),
            [ANYWHERE] * 3 + [IN_VMEM, ANYWHERE],
            plan_scratch(CHUNK),
            us=4.0,
        )(*near_plan, frame, after)

    near = [near_sum(0, block)]
    block = join(block, arrived, near[0])
    arrived = stage(block, STAGES[4])
    near.append(near_sum(1, block))
    block = join(block, arrived, near[1])
    arrived = stage(block, STAGES[5])
    frame = pallas(
        functools.partial(hub_frame_kernel, frame_rows, hubs),
        f32(*frame.shape),
        [IN_VMEM] * 3 + [ANYWHERE],
        us=0.5,
        aliases={0: 0},
    )(frame, block, arrived[0], near[1])

    def layer(plan, first, start, size, sent_chans, near, after, us):
        return pallas(
            functools.partial(layer_kernel, slots, first, start, len(near), half),
            (bf16(chans, size), bf16(sent_chans, size)),
            [ANYWHERE] * 3 + [IN_VMEM] * 4 + [ANYWHERE] + [IN_VMEM] * len(near),
            [VMEM((size, LANES), jnp.float32)] + plan_scratch(size),
            us=us,
        )(*plan, frame, scale, by_out, bias, after, *near)

    keep, received = [near[1]], []
    for plan, first, start, size, sent_chans, near, us in (
        (far_plan, 0, 0, CHUNK, 2 * chans, near, 3.0),
        (full_plan, CHUNK, 0, CHUNK, chans, [], 8.0),
    ):
        kept, sent = layer(plan, first, start, size, sent_chans, near, keep[-1], us)
        keep.append(kept)
        received.append(lax.ppermute(sent, "feat", swap))
    pieces = keep[1:] + received
    return pallas(output_kernel, bf16(chans, nodes), [IN_VMEM] * len(pieces), us=0.5)(*pieces)


def solution(mesh):
    in_specs = (P("feat", "slab"), P(None, "slab"), P("slab"), P("slab"), P(), P())
    return jax.shard_map(local, mesh=mesh, in_specs=in_specs, out_specs=P("feat", "slab"), check_vma=False)
```

```python
import functools

import jax
import jax.numpy as jnp
from jax import lax
from jax.experimental import pallas as pl
from jax.experimental.pallas import tpu as pltpu
from jax.sharding import PartitionSpec as P

VMEM = pltpu.VMEM
SMEM = pltpu.SMEM
LANES = 128
CHUNK = 1024
GROUP = 32
STAGES = ((32,), (64,), (8, 16, 24), (2, 4, 6), (1,))


def hub_pick_kernel(rows_ref, x_ref, out_ref, x_out_ref):
    hubs, nodes = rows_ref.shape[1], x_ref.shape[1]
    diagonal = lax.broadcasted_iota(jnp.int32, (hubs, hubs), 0) == lax.broadcasted_iota(
        jnp.int32, (hubs, hubs), 1
    )
    rows = jnp.sum(jnp.where(diagonal, rows_ref[...], 0), axis=1, keepdims=True)
    onehot = (lax.broadcasted_iota(jnp.int32, (hubs, nodes), 1) == rows).astype(jnp.bfloat16)
    picked = lax.dot_general(
        onehot, x_ref[...], (((1,), (1,)), ((), ())), preferred_element_type=jnp.float32
    ).astype(jnp.bfloat16)
    out_ref[...] = jnp.concatenate([picked[: hubs // 2], picked[hubs // 2 :]], axis=1)
    x_out_ref[...] = x_ref[...]


def join_kernel(*refs):
    blocks, out_ref = refs[:-2], refs[-1]
    rows = blocks[0].shape[0]
    for i, ref in enumerate(blocks):
        out_ref[i * rows : (i + 1) * rows] = ref[...]


def join_feat_kernel(mine_ref, other_ref, after_ref, out_ref):
    first = lax.axis_index("feat") == 0
    lane = lax.broadcasted_iota(jnp.int32, (16, LANES), 1)
    for i in range(mine_ref.shape[0] // 16):
        mine = mine_ref[16 * i : 16 * i + 16, :].astype(jnp.float32)
        other = other_ref[16 * i : 16 * i + 16, :].astype(jnp.float32)
        low = jnp.where(first, mine, other)
        high = jnp.where(first, other, mine)
        row = jnp.where(lane < LANES // 2, low, pltpu.roll(high, LANES // 2, 1))
        out_ref[32 * i : 32 * i + 16, :] = row.astype(jnp.bfloat16)
        row = jnp.where(lane < LANES // 2, pltpu.roll(low, LANES // 2, 1), high)
        out_ref[32 * i + 16 : 32 * i + 32, :] = row.astype(jnp.bfloat16)


def halves_kernel(x_ref, other_ref, after_ref, outer_ref, inner_ref, sem):
    feat = lax.axis_index("feat")
    odd = lax.axis_index("slab") & 1
    chans, half = x_ref.shape[0], outer_ref.shape[1]
    copies = []
    for ref, channels in ((x_ref, feat), (other_ref, 1 - feat)):
        rows = pl.ds(pl.multiple_of(channels * chans, chans), chans)
        for out_ref, part in ((outer_ref, odd), (inner_ref, 1 - odd)):
            cols = pl.ds(pl.multiple_of(part * half, half), half)
            copies.append(
                pltpu.make_async_copy(ref.at[:, cols], out_ref.at[rows, :], sem.at[len(copies)])
            )
    for copy in copies:
        copy.start()
    for copy in copies:
        copy.wait()


def frame_kernel(outer_halo_ref, outer_ref, inner_ref, inner_halo_ref, after_ref, frame_ref):
    odd = lax.axis_index("slab") & 1
    half = outer_ref.shape[1]
    step = 256
    unit = (
        lax.broadcasted_iota(jnp.int32, (step, step), 0)
        == lax.broadcasted_iota(jnp.int32, (step, step), 1)
    ).astype(jnp.bfloat16)
    for place, ref in enumerate((outer_halo_ref, outer_ref, inner_ref, inner_halo_ref)):
        first = (place + odd * (3 - 2 * place)) * half
        for at in range(0, half, step):
            frame_ref[pl.ds(pl.multiple_of(first + at, step), step), :] = lax.dot_general(
                unit,
                ref[:, at : at + step],
                (((1,), (1,)), ((), ())),
                preferred_element_type=jnp.float32,
            )
    rows = frame_ref.shape[0]
    frame_ref[rows - 8 :, :] = jnp.zeros((8, LANES), jnp.float32)


def origins():
    differs = [0]
    for bits in STAGES:
        differs = [d ^ bit for bit in (0,) + bits for d in differs]
    return differs


def hub_frame_kernel(first, hubs, frame_in, near_ref, far_ref, after_ref, frame_ref):
    blocks = near_ref.shape[0] // hubs
    me = lax.axis_index("slab")
    for p, differs in enumerate(origins()):
        ref, i = (near_ref, p) if p < blocks else (far_ref, p - blocks)
        at = pl.multiple_of(first + (me ^ differs) * hubs, hubs)
        frame_ref[pl.ds(at, hubs), :] = ref[hubs * i : hubs * (i + 1), :].astype(jnp.float32)


def comparators(count):
    pairs, p = [], 1
    while p < count:
        k = p
        while k >= 1:
            for j in range(k % p, count - k, 2 * k):
                for i in range(min(k, count - j - k)):
                    if (i + j) // (2 * p) == (i + j + k) // (2 * p):
                        pairs.append((i + j, i + j + k))
            k //= 2
        p *= 2
    return pairs


def sort_network(values):
    for a, b in comparators(len(values)):
        values[a], values[b] = jnp.minimum(values[a], values[b]), jnp.maximum(values[a], values[b])
    return values


def sorted_tiles(keys):
    shape = keys.shape
    sub = lax.broadcasted_iota(jnp.int32, shape, 1)
    lane = lax.broadcasted_iota(jnp.int32, shape, 2)
    at = sub * LANES + lane
    size = 2
    while size <= CHUNK:
        distance = size // 2
        while distance >= 1:
            axis, by, extent = (2, distance, LANES) if distance < LANES else (1, distance // LANES, 8)
            lower = (at & distance) == 0
            partner = jnp.where(
                lower, pltpu.roll(keys, extent - by, axis), pltpu.roll(keys, by, axis)
            )
            ascending = (at & size) == 0
            keys = jnp.where(
                lower == ascending, jnp.minimum(keys, partner), jnp.maximum(keys, partner)
            )
            distance //= 2
        size *= 2
    return keys


def slots_kernel(frame_rows, all_rows, nbr_ref, deg_ref, after_ref, near_ids, far_ids, full_ids, counts_ref):
    slots = nbr_ref.shape[0]
    first = lax.axis_index("feat") * 16
    rows = pl.ds(pl.multiple_of(first, 8), 8)
    degree = deg_ref[rows, :]
    near, far = [], []
    near_count = jnp.zeros((8, LANES), jnp.int32)
    for j in range(slots):
        nbr = nbr_ref[j, rows, :]
        used = degree > j
        is_near = used & (nbr < frame_rows)
        near.append(jnp.where(is_near, nbr, all_rows))
        far.append(jnp.where(used & (nbr >= frame_rows), nbr, all_rows))
        near_count = near_count + is_near.astype(jnp.int32)
    for j, ids in enumerate(sort_network(near)):
        near_ids[j] = ids
    for j, ids in enumerate(sort_network(far)):
        far_ids[j] = ids
    counts_ref[0] = near_count
    counts_ref[1] = degree - near_count
    rows = pl.ds(pl.multiple_of(first + 8, 8), 8)
    degree = deg_ref[rows, :]
    for j in range(slots):
        full_ids[j] = jnp.where(degree > j, nbr_ref[j, rows, :], all_rows)
    counts_ref[2] = degree


def order_kernel(counts_ref, after_ref, *refs):
    orders, classes = refs[:3], refs[3:]
    at = lax.broadcasted_iota(jnp.int32, (8, LANES), 0) * LANES + lax.broadcasted_iota(
        jnp.int32, (8, LANES), 1
    )
    keys = sorted_tiles(counts_ref[...] * CHUNK + at[None])
    for i in range(3):
        orders[i][...] = keys[i] & (CHUNK - 1)
        classes[i][...] = keys[i] >> 10


def constants_kernel(deg_ref, weight_ref, bias_ref, after_ref, scale_ref, weight_out, bias_out):
    tiles = scale_ref.shape[0] // LANES
    first = pl.multiple_of(lax.axis_index("feat") * tiles, tiles)
    inverse = 1.0 / (deg_ref[pl.ds(first, tiles), :] + 1).astype(jnp.float32)
    for t in range(tiles):
        scale_ref[LANES * t : LANES * (t + 1), :] = jnp.broadcast_to(
            inverse[t : t + 1, :], (LANES, LANES)
        ).T
    weight_out[...] = weight_ref[...].astype(jnp.float32).T.astype(jnp.bfloat16)
    bias_out[...] = jnp.broadcast_to(bias_ref[...], (LANES, LANES)).T


def add_tree(parts):
    while len(parts) > 1:
        tail = [parts[-1]] if len(parts) % 2 else []
        parts = [parts[i] + parts[i + 1] for i in range(0, len(parts) - 1, 2)] + tail
    return parts[0]


def load_plan(slots, start, ids_ref, order_ref, class_ref, slot_ids, order, classes, sem):
    size = order.shape[0]
    rows = pl.ds(start, size)
    first = [
        pltpu.make_async_copy(order_ref.at[rows], order, sem.at[slots]),
        pltpu.make_async_copy(class_ref.at[rows], classes.at[pl.ds(0, size)], sem.at[slots + 1]),
    ]
    by_slot = [
        pltpu.make_async_copy(
            ids_ref.at[pl.ds(j * CHUNK + start, size)], slot_ids.at[pl.ds(j * size, size)], sem.at[j]
        )
        for j in range(slots)
    ]
    for copy in first + by_slot:
        copy.start()
    return first, by_slot


def sum_slots(slots, start, part, parts, plan_refs, frame_ref, total_ref, slot_ids, order, classes, sem):
    size = order.shape[0]
    first, by_slot = load_plan(slots, start, *plan_refs, slot_ids, order, classes, sem)
    total_ref[...] = jnp.zeros_like(total_ref)
    for copy in first:
        copy.wait()
    last = GROUP - 1
    classes[size + part * GROUP + last] = slots + 1
    of_slot = [slot_ids.at[pl.ds(j * size, size)] for j in range(slots)]

    def body(count, carry):
        base, _ = carry
        for k in range(GROUP):
            node = order[base + k]
            total_ref[pl.ds(node, 1), :] = add_tree(
                [frame_ref[pl.ds(of_slot[j][node], 1), :] for j in range(count)]
            )
        return base + parts * GROUP, classes[base + parts * GROUP + last]

    def skip(carry):
        base, _ = carry
        return base + parts * GROUP, classes[base + parts * GROUP + last]

    carry = (jnp.int32(part * GROUP), classes[part * GROUP + last])
    carry = lax.while_loop(lambda carry: carry[1] == 0, skip, carry)
    for count in range(1, slots + 1):
        by_slot[count - 1].wait()
        carry = lax.while_loop(
            lambda carry, count=count: carry[1] == count, functools.partial(body, count), carry
        )


def near_kernel(slots, part, parts, ids_ref, order_ref, class_ref, frame_ref, after_ref, total_ref, *plan):
    sum_slots(slots, 0, part, parts, (ids_ref, order_ref, class_ref), frame_ref, total_ref, *plan)


def layer_kernel(slots, first, start, parts, own, ids_ref, order_ref, class_ref, frame_ref, scale_ref, weight_ref, bias_ref, after_ref, *refs):
    near, (keep_ref, send_ref, total_ref), plan = refs[:parts], refs[parts : parts + 3], refs[parts + 3 :]
    sum_slots(slots, start, 0, 1, (ids_ref, order_ref, class_ref), frame_ref, total_ref, *plan)
    chans, size = keep_ref.shape
    feat = lax.axis_index("feat")
    step = 256
    for at in range(0, size, step):
        rows = slice(at, at + step)
        own_at = pl.multiple_of(own + feat * own + first + at, step)
        total = total_ref[rows, :] + frame_ref[pl.ds(own_at, step), :]
        for ref in near:
            total = total + ref[rows, :]
        product = lax.dot_general(
            weight_ref[...],
            (total * scale_ref[first + at : first + at + step, :]).astype(jnp.bfloat16),
            (((1,), (1,)), ((), ())),
            preferred_element_type=jnp.float32,
        )
        bias = jnp.concatenate([bias_ref[...]] * (step // LANES), axis=1)
        result = jnp.maximum(product + bias, 0.0)
        low, high = result[:chans], result[chans:]
        keep_ref[:, rows] = jnp.where(feat == 0, low, high).astype(jnp.bfloat16)
        if send_ref.shape[0] == chans:
            result = jnp.where(feat == 0, high, low)
        send_ref[:, rows] = result.astype(jnp.bfloat16)


def output_kernel(*refs):
    out_ref = refs[-1]
    count = len(refs) // 2
    feat = lax.axis_index("feat")
    chans = out_ref.shape[0]
    for refs, part in ((refs[:count], feat), (refs[count:-1], 1 - feat)):
        at = part * (out_ref.shape[1] // 2)
        for ref in refs:
            size = ref.shape[1]
            rows = pl.ds(pl.multiple_of(feat * chans, chans), chans) if ref.shape[0] > chans else slice(None)
            out_ref[:, pl.ds(pl.multiple_of(at, size), size)] = ref[rows, :]
            at = at + size


def pallas(kernel, out_shape, in_specs, scratch=(), us=1.0, aliases=None):
    return pl.pallas_call(
        kernel,
        out_shape=out_shape,
        in_specs=in_specs,
        out_specs=jax.tree.map(lambda _: IN_VMEM, out_shape),
        scratch_shapes=list(scratch),
        input_output_aliases=aliases or {},
        compiler_params=pltpu.CompilerParams(vmem_limit_bytes=6 * 2**20),
        cost_estimate=pl.CostEstimate(flops=0, bytes_accessed=int(us * 3_000_000), transcendentals=0),
    )


IN_VMEM = pl.BlockSpec(memory_space=VMEM)
ANYWHERE = pl.BlockSpec(memory_space=pl.ANY)


def local(node_feats, neighbours, degrees, hub_rows, weight, bias_terms):
    chans, nodes = node_feats.shape
    slots = neighbours.shape[0]
    hubs = hub_rows.shape[0]
    slabs = lax.axis_size("slab")
    half = nodes // 2
    chunks = half // CHUNK
    frame_rows, hub_count = 2 * half + nodes, slabs * hubs
    swap = [(0, 1), (1, 0)]

    def bf16(*shape):
        return jax.ShapeDtypeStruct(shape, jnp.bfloat16)

    def f32(*shape):
        return jax.ShapeDtypeStruct(shape, jnp.float32)

    def i32(*shape):
        return jax.ShapeDtypeStruct(shape, jnp.int32)

    block, own_feats = pallas(
        hub_pick_kernel, (bf16(hubs // 2, 2 * chans), bf16(chans, nodes)), [IN_VMEM] * 2
    )(hub_rows[None, :], node_feats)
    arrived = None

    def stage(block, bits):
        return [lax.ppermute(block, "slab", [(i, i ^ bit) for i in range(slabs)]) for bit in bits]

    def join(block, arrived, after):
        rows = block.shape[0] * (1 + len(arrived))
        specs = [IN_VMEM] * (1 + len(arrived)) + [ANYWHERE]
        return pallas(join_kernel, bf16(rows, 2 * chans), specs, us=0.5)(block, *arrived, after)

    arrived = stage(block, STAGES[0])
    deg_tiles = degrees.reshape(nodes // LANES, LANES)
    table, tile = i32(slots, 8, LANES), i32(8, LANES)
    *ids, counts = pallas(
        functools.partial(slots_kernel, frame_rows, frame_rows + hub_count),
        (table, table, table, i32(3, 8, LANES)),
        [IN_VMEM, IN_VMEM, ANYWHERE],
        us=1.0,
    )(neighbours.reshape(slots, nodes // LANES, LANES), deg_tiles, block)
    other = lax.ppermute(node_feats, "feat", swap)

    block = join(block, arrived, counts)
    arrived = stage(block, STAGES[1])
    scale, by_out, bias = pallas(
        constants_kernel,
        (f32(half, LANES), bf16(2 * chans, 2 * chans), f32(LANES, LANES)),
        [IN_VMEM] * 3 + [ANYWHERE],
        us=0.1,
    )(deg_tiles, weight, bias_terms[None, :], block)

    block = join(block, arrived, scale)
    arrived = lax.ppermute(block, "feat", swap)
    block = pallas(
        join_feat_kernel, bf16(2 * block.shape[0], 2 * chans), [IN_VMEM] * 2 + [ANYWHERE], us=0.1
    )(block, arrived, scale)

    outer, inner = pallas(
        halves_kernel,
        (bf16(2 * chans, half),) * 2,
        [ANYWHERE] * 3,
        [pltpu.SemaphoreType.DMA((4,))],
        us=0.1,
    )(own_feats, other, block)
    inner_halo = lax.ppermute(inner, "slab", [(i, i ^ 1) for i in range(slabs)])
    outer_halo = lax.ppermute(
        outer, "slab", [(i, j) for i in range(slabs) for j in [i + 2 * (i & 1) - 1] if 0 <= j < slabs]
    )
    arrived = stage(block, STAGES[2])
    order = pallas(order_kernel, (tile,) * 6, [IN_VMEM, ANYWHERE], us=3.0)(counts, outer)
    near_plan, far_plan, full_plan = (
        [a.reshape(-1) for a in (ids[i], order[i], order[3 + i])] for i in range(3)
    )
    block = join(block, arrived, order[0])
    arrived = stage(block, STAGES[3])
    frame = pallas(
        frame_kernel,
        f32(frame_rows + hub_count + 8, LANES),
        [IN_VMEM] * 4 + [ANYWHERE],
        us=2.0,
    )(outer_halo, outer, inner, inner_halo, block)

    def plan_scratch(size):
        return [
            SMEM((slots * size,), jnp.int32),
            SMEM((size,), jnp.int32),
            SMEM((size + 2 * GROUP,), jnp.int32),
            pltpu.SemaphoreType.DMA((slots + 2,)),
        ]

    def near_sum(part, after):
        return pallas(
            functools.partial(near_kernel, slots, part, 2),
            f32(CHUNK, LANES),
            [ANYWHERE] * 3 + [IN_VMEM, ANYWHERE],
            plan_scratch(CHUNK),
            us=4.0,
        )(*near_plan, frame, after)

    near = [near_sum(0, block)]
    block = join(block, arrived, near[0])
    arrived = stage(block, STAGES[4])
    near.append(near_sum(1, block))
    frame = pallas(
        functools.partial(hub_frame_kernel, frame_rows, hubs),
        f32(*frame.shape),
        [IN_VMEM] * 3 + [ANYWHERE],
        us=0.5,
        aliases={0: 0},
    )(frame, block, arrived[0], near[1])

    def layer(plan, first, start, size, sent_chans, near, after, us):
        return pallas(
            functools.partial(layer_kernel, slots, first, start, len(near), half),
            (bf16(chans, size), bf16(sent_chans, size)),
            [ANYWHERE] * 3 + [IN_VMEM] * 4 + [ANYWHERE] + [IN_VMEM] * len(near),
            [VMEM((size, LANES), jnp.float32)] + plan_scratch(size),
            us=us,
        )(*plan, frame, scale, by_out, bias, after, *near)

    keep, received = [near[1]], []
    for plan, first, start, size, sent_chans, near, us in (
        (far_plan, 0, 0, CHUNK, 2 * chans, near, 3.0),
        (full_plan, CHUNK, 0, CHUNK, chans, [], 8.0),
    ):
        kept, sent = layer(plan, first, start, size, sent_chans, near, keep[-1], us)
        keep.append(kept)
        received.append(lax.ppermute(sent, "feat", swap))
    pieces = keep[1:] + received
    return pallas(output_kernel, bf16(chans, nodes), [IN_VMEM] * len(pieces), us=0.5)(*pieces)


def solution(mesh):
    in_specs = (P("feat", "slab"), P(None, "slab"), P("slab"), P("slab"), P(), P())
    return jax.shard_map(local, mesh=mesh, in_specs=in_specs, out_specs=P("feat", "slab"), check_vma=False)
```

```python
import functools

import jax
import jax.numpy as jnp
from jax import lax
from jax.experimental import pallas as pl
from jax.experimental.pallas import tpu as pltpu
from jax.sharding import PartitionSpec as P

VMEM = pltpu.VMEM
SMEM = pltpu.SMEM
LANES = 128
CHUNK = 1024
GROUP = 32
STAGES = ((32,), (64,), (8, 16, 24), (2, 4, 6), (1,))


def hub_pick_kernel(rows_ref, x_ref, out_ref, x_out_ref):
    hubs, nodes = rows_ref.shape[1], x_ref.shape[1]
    diagonal = lax.broadcasted_iota(jnp.int32, (hubs, hubs), 0) == lax.broadcasted_iota(
        jnp.int32, (hubs, hubs), 1
    )
    rows = jnp.sum(jnp.where(diagonal, rows_ref[...], 0), axis=1, keepdims=True)
    onehot = (lax.broadcasted_iota(jnp.int32, (hubs, nodes), 1) == rows).astype(jnp.bfloat16)
    picked = lax.dot_general(
        onehot, x_ref[...], (((1,), (1,)), ((), ())), preferred_element_type=jnp.float32
    ).astype(jnp.bfloat16)
    out_ref[...] = jnp.concatenate([picked[: hubs // 2], picked[hubs // 2 :]], axis=1)
    x_out_ref[...] = x_ref[...]


def join_kernel(*refs):
    blocks, out_ref = refs[:-2], refs[-1]
    rows = blocks[0].shape[0]
    for i, ref in enumerate(blocks):
        out_ref[i * rows : (i + 1) * rows] = ref[...]


def join_feat_kernel(*refs):
    count = len(refs) // 2 - 1
    out_ref = refs[-1]
    rows = refs[0].shape[0]
    first = lax.axis_index("feat") == 0
    lane = lax.broadcasted_iota(jnp.int32, (16, LANES), 1)
    for b, (mine_ref, other_ref) in enumerate(zip(refs[:count], refs[count : 2 * count])):
        for at in range(0, rows, 16):
            mine = mine_ref[at : at + 16, :].astype(jnp.float32)
            other = other_ref[at : at + 16, :].astype(jnp.float32)
            low = jnp.where(first, mine, other)
            high = jnp.where(first, other, mine)
            to = 2 * (b * rows + at)
            row = jnp.where(lane < LANES // 2, low, pltpu.roll(high, LANES // 2, 1))
            out_ref[to : to + 16, :] = row.astype(jnp.bfloat16)
            row = jnp.where(lane < LANES // 2, pltpu.roll(low, LANES // 2, 1), high)
            out_ref[to + 16 : to + 32, :] = row.astype(jnp.bfloat16)


def halves_kernel(x_ref, other_ref, after_ref, outer_ref, inner_ref, sem):
    feat = lax.axis_index("feat")
    odd = lax.axis_index("slab") & 1
    chans, half = x_ref.shape[0], outer_ref.shape[1]
    copies = []
    for ref, channels in ((x_ref, feat), (other_ref, 1 - feat)):
        rows = pl.ds(pl.multiple_of(channels * chans, chans), chans)
        for out_ref, part in ((outer_ref, odd), (inner_ref, 1 - odd)):
            cols = pl.ds(pl.multiple_of(part * half, half), half)
            copies.append(
                pltpu.make_async_copy(ref.at[:, cols], out_ref.at[rows, :], sem.at[len(copies)])
            )
    for copy in copies:
        copy.start()
    for copy in copies:
        copy.wait()


def frame_kernel(outer_halo_ref, outer_ref, inner_ref, inner_halo_ref, after_ref, frame_ref):
    odd = lax.axis_index("slab") & 1
    half = outer_ref.shape[1]
    step = 256
    unit = (
        lax.broadcasted_iota(jnp.int32, (step, step), 0)
        == lax.broadcasted_iota(jnp.int32, (step, step), 1)
    ).astype(jnp.bfloat16)
    for place, ref in enumerate((outer_halo_ref, outer_ref, inner_ref, inner_halo_ref)):
        first = (place + odd * (3 - 2 * place)) * half
        for at in range(0, half, step):
            frame_ref[pl.ds(pl.multiple_of(first + at, step), step), :] = lax.dot_general(
                unit,
                ref[:, at : at + step],
                (((1,), (1,)), ((), ())),
                preferred_element_type=jnp.float32,
            )
    rows = frame_ref.shape[0]
    frame_ref[rows - 8 :, :] = jnp.zeros((8, LANES), jnp.float32)


def origins():
    differs = [0]
    for bits in STAGES:
        differs = [d ^ bit for bit in (0,) + bits for d in differs]
    return differs


def hub_frame_kernel(first, hubs, frame_in, near_ref, far_ref, after_ref, frame_ref):
    blocks = near_ref.shape[0] // hubs
    me = lax.axis_index("slab")
    for p, differs in enumerate(origins()):
        ref, i = (near_ref, p) if p < blocks else (far_ref, p - blocks)
        at = pl.multiple_of(first + (me ^ differs) * hubs, hubs)
        frame_ref[pl.ds(at, hubs), :] = ref[hubs * i : hubs * (i + 1), :].astype(jnp.float32)


def comparators(count):
    pairs, p = [], 1
    while p < count:
        k = p
        while k >= 1:
            for j in range(k % p, count - k, 2 * k):
                for i in range(min(k, count - j - k)):
                    if (i + j) // (2 * p) == (i + j + k) // (2 * p):
                        pairs.append((i + j, i + j + k))
            k //= 2
        p *= 2
    return pairs


def sort_network(values):
    for a, b in comparators(len(values)):
        values[a], values[b] = jnp.minimum(values[a], values[b]), jnp.maximum(values[a], values[b])
    return values


def sorted_tiles(keys):
    shape = keys.shape
    sub = lax.broadcasted_iota(jnp.int32, shape, 1)
    lane = lax.broadcasted_iota(jnp.int32, shape, 2)
    at = sub * LANES + lane
    size = 2
    while size <= CHUNK:
        distance = size // 2
        while distance >= 1:
            axis, by, extent = (2, distance, LANES) if distance < LANES else (1, distance // LANES, 8)
            lower = (at & distance) == 0
            partner = jnp.where(
                lower, pltpu.roll(keys, extent - by, axis), pltpu.roll(keys, by, axis)
            )
            ascending = (at & size) == 0
            keys = jnp.where(
                lower == ascending, jnp.minimum(keys, partner), jnp.maximum(keys, partner)
            )
            distance //= 2
        size *= 2
    return keys


def slots_kernel(frame_rows, all_rows, nbr_ref, deg_ref, after_ref, near_ids, far_ids, full_ids, counts_ref):
    slots = nbr_ref.shape[0]
    first = lax.axis_index("feat") * 16
    rows = pl.ds(pl.multiple_of(first, 8), 8)
    degree = deg_ref[rows, :]
    near, far = [], []
    near_count = jnp.zeros((8, LANES), jnp.int32)
    for j in range(slots):
        nbr = nbr_ref[j, rows, :]
        used = degree > j
        is_near = used & (nbr < frame_rows)
        near.append(jnp.where(is_near, nbr, all_rows))
        far.append(jnp.where(used & (nbr >= frame_rows), nbr, all_rows))
        near_count = near_count + is_near.astype(jnp.int32)
    for j, ids in enumerate(sort_network(near)):
        near_ids[j] = ids
    for j, ids in enumerate(sort_network(far)):
        far_ids[j] = ids
    counts_ref[0] = near_count
    counts_ref[1] = degree - near_count
    rows = pl.ds(pl.multiple_of(first + 8, 8), 8)
    degree = deg_ref[rows, :]
    for j in range(slots):
        full_ids[j] = jnp.where(degree > j, nbr_ref[j, rows, :], all_rows)
    counts_ref[2] = degree


def order_kernel(counts_ref, after_ref, *refs):
    orders, classes = refs[:3], refs[3:]
    at = lax.broadcasted_iota(jnp.int32, (8, LANES), 0) * LANES + lax.broadcasted_iota(
        jnp.int32, (8, LANES), 1
    )
    keys = sorted_tiles(counts_ref[...] * CHUNK + at[None])
    for i in range(3):
        orders[i][...] = keys[i] & (CHUNK - 1)
        classes[i][...] = keys[i] >> 10


def constants_kernel(deg_ref, weight_ref, bias_ref, after_ref, scale_ref, weight_out, bias_out):
    tiles = scale_ref.shape[0] // LANES
    first = pl.multiple_of(lax.axis_index("feat") * tiles, tiles)
    inverse = 1.0 / (deg_ref[pl.ds(first, tiles), :] + 1).astype(jnp.float32)
    for t in range(tiles):
        scale_ref[LANES * t : LANES * (t + 1), :] = jnp.broadcast_to(
            inverse[t : t + 1, :], (LANES, LANES)
        ).T
    weight_out[...] = weight_ref[...].astype(jnp.float32).T.astype(jnp.bfloat16)
    bias_out[...] = jnp.broadcast_to(bias_ref[...], (LANES, LANES)).T


def add_tree(parts):
    while len(parts) > 1:
        tail = [parts[-1]] if len(parts) % 2 else []
        parts = [parts[i] + parts[i + 1] for i in range(0, len(parts) - 1, 2)] + tail
    return parts[0]


def load_plan(slots, start, ids_ref, order_ref, class_ref, slot_ids, order, classes, sem):
    size = order.shape[0]
    rows = pl.ds(start, size)
    first = [
        pltpu.make_async_copy(order_ref.at[rows], order, sem.at[slots]),
        pltpu.make_async_copy(class_ref.at[rows], classes.at[pl.ds(0, size)], sem.at[slots + 1]),
    ]
    by_slot = [
        pltpu.make_async_copy(
            ids_ref.at[pl.ds(j * CHUNK + start, size)], slot_ids.at[pl.ds(j * size, size)], sem.at[j]
        )
        for j in range(slots)
    ]
    for copy in first + by_slot:
        copy.start()
    return first, by_slot


def sum_slots(slots, start, part, parts, plan_refs, frame_ref, total_ref, slot_ids, order, classes, sem):
    size = order.shape[0]
    first, by_slot = load_plan(slots, start, *plan_refs, slot_ids, order, classes, sem)
    total_ref[...] = jnp.zeros_like(total_ref)
    for copy in first:
        copy.wait()
    last = GROUP - 1
    classes[size + part * GROUP + last] = slots + 1
    of_slot = [slot_ids.at[pl.ds(j * size, size)] for j in range(slots)]

    def body(count, carry):
        base, _ = carry
        for k in range(GROUP):
            node = order[base + k]
            total_ref[pl.ds(node, 1), :] = add_tree(
                [frame_ref[pl.ds(of_slot[j][node], 1), :] for j in range(count)]
            )
        return base + parts * GROUP, classes[base + parts * GROUP + last]

    def skip(carry):
        base, _ = carry
        return base + parts * GROUP, classes[base + parts * GROUP + last]

    carry = (jnp.int32(part * GROUP), classes[part * GROUP + last])
    carry = lax.while_loop(lambda carry: carry[1] == 0, skip, carry)
    for count in range(1, slots + 1):
        by_slot[count - 1].wait()
        carry = lax.while_loop(
            lambda carry, count=count: carry[1] == count, functools.partial(body, count), carry
        )


def near_kernel(slots, part, parts, ids_ref, order_ref, class_ref, frame_ref, after_ref, total_ref, *plan):
    sum_slots(slots, 0, part, parts, (ids_ref, order_ref, class_ref), frame_ref, total_ref, *plan)


def layer_kernel(slots, first, start, parts, own, ids_ref, order_ref, class_ref, frame_ref, scale_ref, weight_ref, bias_ref, after_ref, *refs):
    near, (keep_ref, send_ref, total_ref), plan = refs[:parts], refs[parts : parts + 3], refs[parts + 3 :]
    sum_slots(slots, start, 0, 1, (ids_ref, order_ref, class_ref), frame_ref, total_ref, *plan)
    chans, size = keep_ref.shape
    feat = lax.axis_index("feat")
    step = 256
    for at in range(0, size, step):
        rows = slice(at, at + step)
        own_at = pl.multiple_of(own + feat * own + first + at, step)
        total = total_ref[rows, :] + frame_ref[pl.ds(own_at, step), :]
        for ref in near:
            total = total + ref[rows, :]
        product = lax.dot_general(
            weight_ref[...],
            (total * scale_ref[first + at : first + at + step, :]).astype(jnp.bfloat16),
            (((1,), (1,)), ((), ())),
            preferred_element_type=jnp.float32,
        )
        bias = jnp.concatenate([bias_ref[...]] * (step // LANES), axis=1)
        result = jnp.maximum(product + bias, 0.0)
        low, high = result[:chans], result[chans:]
        keep_ref[:, rows] = jnp.where(feat == 0, low, high).astype(jnp.bfloat16)
        if send_ref.shape[0] == chans:
            result = jnp.where(feat == 0, high, low)
        send_ref[:, rows] = result.astype(jnp.bfloat16)


def output_kernel(*refs):
    out_ref = refs[-1]
    count = len(refs) // 2
    feat = lax.axis_index("feat")
    chans = out_ref.shape[0]
    for refs, part in ((refs[:count], feat), (refs[count:-1], 1 - feat)):
        at = part * (out_ref.shape[1] // 2)
        for ref in refs:
            size = ref.shape[1]
            rows = pl.ds(pl.multiple_of(feat * chans, chans), chans) if ref.shape[0] > chans else slice(None)
            out_ref[:, pl.ds(pl.multiple_of(at, size), size)] = ref[rows, :]
            at = at + size


def pallas(kernel, out_shape, in_specs, scratch=(), us=1.0, aliases=None):
    return pl.pallas_call(
        kernel,
        out_shape=out_shape,
        in_specs=in_specs,
        out_specs=jax.tree.map(lambda _: IN_VMEM, out_shape),
        scratch_shapes=list(scratch),
        input_output_aliases=aliases or {},
        compiler_params=pltpu.CompilerParams(vmem_limit_bytes=6 * 2**20),
        cost_estimate=pl.CostEstimate(flops=0, bytes_accessed=int(us * 3_000_000), transcendentals=0),
    )


IN_VMEM = pl.BlockSpec(memory_space=VMEM)
ANYWHERE = pl.BlockSpec(memory_space=pl.ANY)


def local(node_feats, neighbours, degrees, hub_rows, weight, bias_terms):
    chans, nodes = node_feats.shape
    slots = neighbours.shape[0]
    hubs = hub_rows.shape[0]
    slabs = lax.axis_size("slab")
    half = nodes // 2
    chunks = half // CHUNK
    frame_rows, hub_count = 2 * half + nodes, slabs * hubs
    swap = [(0, 1), (1, 0)]

    def bf16(*shape):
        return jax.ShapeDtypeStruct(shape, jnp.bfloat16)

    def f32(*shape):
        return jax.ShapeDtypeStruct(shape, jnp.float32)

    def i32(*shape):
        return jax.ShapeDtypeStruct(shape, jnp.int32)

    block, own_feats = pallas(
        hub_pick_kernel, (bf16(hubs // 2, 2 * chans), bf16(chans, nodes)), [IN_VMEM] * 2
    )(hub_rows[None, :], node_feats)
    arrived = None

    def stage(block, bits):
        return [lax.ppermute(block, "slab", [(i, i ^ bit) for i in range(slabs)]) for bit in bits]

    def join(block, arrived, after):
        rows = block.shape[0] * (1 + len(arrived))
        specs = [IN_VMEM] * (1 + len(arrived)) + [ANYWHERE]
        return pallas(join_kernel, bf16(rows, 2 * chans), specs, us=0.5)(block, *arrived, after)

    arrived = stage(block, STAGES[0])
    deg_tiles = degrees.reshape(nodes // LANES, LANES)
    table, tile = i32(slots, 8, LANES), i32(8, LANES)
    *ids, counts = pallas(
        functools.partial(slots_kernel, frame_rows, frame_rows + hub_count),
        (table, table, table, i32(3, 8, LANES)),
        [IN_VMEM, IN_VMEM, ANYWHERE],
        us=1.0,
    )(neighbours.reshape(slots, nodes // LANES, LANES), deg_tiles, block)
    other = lax.ppermute(node_feats, "feat", swap)

    block = join(block, arrived, counts)
    arrived = stage(block, STAGES[1])
    arrived.append(lax.ppermute(block, "feat", swap))
    across = [(2 * i + f, 2 * (i ^ STAGES[1][0]) + 1 - f) for i in range(slabs) for f in range(2)]
    arrived.append(lax.ppermute(block, ("slab", "feat"), across))
    scale, by_out, bias = pallas(
        constants_kernel,
        (f32(half, LANES), bf16(2 * chans, 2 * chans), f32(LANES, LANES)),
        [IN_VMEM] * 3 + [ANYWHERE],
        us=0.1,
    )(deg_tiles, weight, bias_terms[None, :], block)
    block = pallas(
        join_feat_kernel, bf16(4 * block.shape[0], 2 * chans), [IN_VMEM] * 4 + [ANYWHERE], us=0.1
    )(block, *arrived, scale)

    outer, inner = pallas(
        halves_kernel,
        (bf16(2 * chans, half),) * 2,
        [ANYWHERE] * 3,
        [pltpu.SemaphoreType.DMA((4,))],
        us=0.1,
    )(own_feats, other, block)
    inner_halo = lax.ppermute(inner, "slab", [(i, i ^ 1) for i in range(slabs)])
    outer_halo = lax.ppermute(
        outer, "slab", [(i, j) for i in range(slabs) for j in [i + 2 * (i & 1) - 1] if 0 <= j < slabs]
    )
    arrived = stage(block, STAGES[2])
    order = pallas(order_kernel, (tile,) * 6, [IN_VMEM, ANYWHERE], us=3.0)(counts, outer)
    near_plan, far_plan, full_plan = (
        [a.reshape(-1) for a in (ids[i], order[i], order[3 + i])] for i in range(3)
    )
    block = join(block, arrived, order[0])
    arrived = stage(block, STAGES[3])
    frame = pallas(
        frame_kernel,
        f32(frame_rows + hub_count + 8, LANES),
        [IN_VMEM] * 4 + [ANYWHERE],
        us=2.0,
    )(outer_halo, outer, inner, inner_halo, block)

    def plan_scratch(size):
        return [
            SMEM((slots * size,), jnp.int32),
            SMEM((size,), jnp.int32),
            SMEM((size + 2 * GROUP,), jnp.int32),
            pltpu.SemaphoreType.DMA((slots + 2,)),
        ]

    def near_sum(part, after):
        return pallas(
            functools.partial(near_kernel, slots, part, 2),
            f32(CHUNK, LANES),
            [ANYWHERE] * 3 + [IN_VMEM, ANYWHERE],
            plan_scratch(CHUNK),
            us=4.0,
        )(*near_plan, frame, after)

    near = [near_sum(0, block)]
    block = join(block, arrived, near[0])
    arrived = stage(block, STAGES[4])
    near.append(near_sum(1, block))
    frame = pallas(
        functools.partial(hub_frame_kernel, frame_rows, hubs),
        f32(*frame.shape),
        [IN_VMEM] * 3 + [ANYWHERE],
        us=0.5,
        aliases={0: 0},
    )(frame, block, arrived[0], near[1])

    def layer(plan, first, start, size, sent_chans, near, after, us):
        return pallas(
            functools.partial(layer_kernel, slots, first, start, len(near), half),
            (bf16(chans, size), bf16(sent_chans, size)),
            [ANYWHERE] * 3 + [IN_VMEM] * 4 + [ANYWHERE] + [IN_VMEM] * len(near),
            [VMEM((size, LANES), jnp.float32)] + plan_scratch(size),
            us=us,
        )(*plan, frame, scale, by_out, bias, after, *near)

    keep, received = [near[1]], []
    for plan, first, start, size, sent_chans, near, us in (
        (far_plan, 0, 0, CHUNK, 2 * chans, near, 3.0),
        (full_plan, CHUNK, 0, CHUNK, chans, [], 8.0),
    ):
        kept, sent = layer(plan, first, start, size, sent_chans, near, keep[-1], us)
        keep.append(kept)
        received.append(lax.ppermute(sent, "feat", swap))
    pieces = keep[1:] + received
    return pallas(output_kernel, bf16(chans, nodes), [IN_VMEM] * len(pieces), us=0.5)(*pieces)


def solution(mesh):
    in_specs = (P("feat", "slab"), P(None, "slab"), P("slab"), P("slab"), P(), P())
    return jax.shard_map(local, mesh=mesh, in_specs=in_specs, out_specs=P("feat", "slab"), check_vma=False)
```

```python
import functools

import jax
import jax.numpy as jnp
from jax import lax
from jax.experimental import pallas as pl
from jax.experimental.pallas import tpu as pltpu
from jax.sharding import PartitionSpec as P

VMEM = pltpu.VMEM
SMEM = pltpu.SMEM
LANES = 128
CHUNK = 1024
GROUP = 32
STAGES = ((32,), (64,), (8, 16, 24), (2, 4, 6), (1,))


def hub_pick_kernel(rows_ref, x_ref, out_ref, x_out_ref):
    hubs, nodes = rows_ref.shape[1], x_ref.shape[1]
    diagonal = lax.broadcasted_iota(jnp.int32, (hubs, hubs), 0) == lax.broadcasted_iota(
        jnp.int32, (hubs, hubs), 1
    )
    rows = jnp.sum(jnp.where(diagonal, rows_ref[...], 0), axis=1, keepdims=True)
    onehot = (lax.broadcasted_iota(jnp.int32, (hubs, nodes), 1) == rows).astype(jnp.bfloat16)
    picked = lax.dot_general(
        onehot, x_ref[...], (((1,), (1,)), ((), ())), preferred_element_type=jnp.float32
    ).astype(jnp.bfloat16)
    out_ref[...] = jnp.concatenate([picked[: hubs // 2], picked[hubs // 2 :]], axis=1)
    x_out_ref[...] = x_ref[...]


def join_kernel(*refs):
    blocks, out_ref = refs[:-2], refs[-1]
    rows = blocks[0].shape[0]
    for i, ref in enumerate(blocks):
        out_ref[i * rows : (i + 1) * rows] = ref[...]


def join_feat_kernel(*refs):
    count = len(refs) // 2 - 1
    out_ref = refs[-1]
    rows = refs[0].shape[0]
    first = lax.axis_index("feat") == 0
    lane = lax.broadcasted_iota(jnp.int32, (16, LANES), 1)
    for b, (mine_ref, other_ref) in enumerate(zip(refs[:count], refs[count : 2 * count])):
        for at in range(0, rows, 16):
            mine = mine_ref[at : at + 16, :].astype(jnp.float32)
            other = other_ref[at : at + 16, :].astype(jnp.float32)
            low = jnp.where(first, mine, other)
            high = jnp.where(first, other, mine)
            to = 2 * (b * rows + at)
            row = jnp.where(lane < LANES // 2, low, pltpu.roll(high, LANES // 2, 1))
            out_ref[to : to + 16, :] = row.astype(jnp.bfloat16)
            row = jnp.where(lane < LANES // 2, pltpu.roll(low, LANES // 2, 1), high)
            out_ref[to + 16 : to + 32, :] = row.astype(jnp.bfloat16)


def halves_kernel(x_ref, other_ref, after_ref, outer_ref, inner_ref, sem):
    feat = lax.axis_index("feat")
    odd = lax.axis_index("slab") & 1
    chans, half = x_ref.shape[0], outer_ref.shape[1]
    copies = []
    for ref, channels in ((x_ref, feat), (other_ref, 1 - feat)):
        rows = pl.ds(pl.multiple_of(channels * chans, chans), chans)
        for out_ref, part in ((outer_ref, odd), (inner_ref, 1 - odd)):
            cols = pl.ds(pl.multiple_of(part * half, half), half)
            copies.append(
                pltpu.make_async_copy(ref.at[:, cols], out_ref.at[rows, :], sem.at[len(copies)])
            )
    for copy in copies:
        copy.start()
    for copy in copies:
        copy.wait()


def frame_kernel(outer_halo_ref, outer_ref, inner_ref, inner_halo_ref, after_ref, frame_ref):
    odd = lax.axis_index("slab") & 1
    half = outer_ref.shape[1]
    step = 256
    unit = (
        lax.broadcasted_iota(jnp.int32, (step, step), 0)
        == lax.broadcasted_iota(jnp.int32, (step, step), 1)
    ).astype(jnp.bfloat16)
    for place, ref in enumerate((outer_halo_ref, outer_ref, inner_ref, inner_halo_ref)):
        first = (place + odd * (3 - 2 * place)) * half
        for at in range(0, half, step):
            frame_ref[pl.ds(pl.multiple_of(first + at, step), step), :] = lax.dot_general(
                unit,
                ref[:, at : at + step],
                (((1,), (1,)), ((), ())),
                preferred_element_type=jnp.float32,
            )
    rows = frame_ref.shape[0]
    frame_ref[rows - 8 :, :] = jnp.zeros((8, LANES), jnp.float32)


def origins():
    differs = [0]
    for bits in STAGES:
        differs = [d ^ bit for bit in (0,) + bits for d in differs]
    return differs


def hub_frame_kernel(first, hubs, frame_in, near_ref, far_ref, after_ref, frame_ref):
    blocks = near_ref.shape[0] // hubs
    me = lax.axis_index("slab")
    for p, differs in enumerate(origins()):
        ref, i = (near_ref, p) if p < blocks else (far_ref, p - blocks)
        at = pl.multiple_of(first + (me ^ differs) * hubs, hubs)
        frame_ref[pl.ds(at, hubs), :] = ref[hubs * i : hubs * (i + 1), :].astype(jnp.float32)


def comparators(count):
    pairs, p = [], 1
    while p < count:
        k = p
        while k >= 1:
            for j in range(k % p, count - k, 2 * k):
                for i in range(min(k, count - j - k)):
                    if (i + j) // (2 * p) == (i + j + k) // (2 * p):
                        pairs.append((i + j, i + j + k))
            k //= 2
        p *= 2
    return pairs


def sort_network(values):
    for a, b in comparators(len(values)):
        values[a], values[b] = jnp.minimum(values[a], values[b]), jnp.maximum(values[a], values[b])
    return values


def sorted_tiles(keys):
    shape = keys.shape
    sub = lax.broadcasted_iota(jnp.int32, shape, 1)
    lane = lax.broadcasted_iota(jnp.int32, shape, 2)
    at = sub * LANES + lane
    size = 2
    while size <= CHUNK:
        distance = size // 2
        while distance >= 1:
            axis, by, extent = (2, distance, LANES) if distance < LANES else (1, distance // LANES, 8)
            lower = (at & distance) == 0
            partner = jnp.where(
                lower, pltpu.roll(keys, extent - by, axis), pltpu.roll(keys, by, axis)
            )
            ascending = (at & size) == 0
            keys = jnp.where(
                lower == ascending, jnp.minimum(keys, partner), jnp.maximum(keys, partner)
            )
            distance //= 2
        size *= 2
    return keys


def slots_kernel(frame_rows, all_rows, nbr_ref, deg_ref, after_ref, near_ids, far_ids, full_ids, counts_ref):
    slots = nbr_ref.shape[0]
    first = lax.axis_index("feat") * 16
    rows = pl.ds(pl.multiple_of(first, 8), 8)
    degree = deg_ref[rows, :]
    near, far = [], []
    near_count = jnp.zeros((8, LANES), jnp.int32)
    for j in range(slots):
        nbr = nbr_ref[j, rows, :]
        used = degree > j
        is_near = used & (nbr < frame_rows)
        near.append(jnp.where(is_near, nbr, all_rows))
        far.append(jnp.where(used & (nbr >= frame_rows), nbr, all_rows))
        near_count = near_count + is_near.astype(jnp.int32)
    for j, ids in enumerate(sort_network(near)):
        near_ids[j] = ids
    for j, ids in enumerate(sort_network(far)):
        far_ids[j] = ids
    counts_ref[0] = near_count
    counts_ref[1] = degree - near_count
    rows = pl.ds(pl.multiple_of(first + 8, 8), 8)
    degree = deg_ref[rows, :]
    for j in range(slots):
        full_ids[j] = jnp.where(degree > j, nbr_ref[j, rows, :], all_rows)
    counts_ref[2] = degree


def order_kernel(counts_ref, after_ref, *refs):
    orders, classes = refs[:3], refs[3:]
    at = lax.broadcasted_iota(jnp.int32, (8, LANES), 0) * LANES + lax.broadcasted_iota(
        jnp.int32, (8, LANES), 1
    )
    keys = sorted_tiles(counts_ref[...] * CHUNK + at[None])
    for i in range(3):
        orders[i][...] = keys[i] & (CHUNK - 1)
        classes[i][...] = keys[i] >> 10


def constants_kernel(deg_ref, weight_ref, bias_ref, after_ref, scale_ref, weight_out, bias_out):
    tiles = scale_ref.shape[0] // LANES
    first = pl.multiple_of(lax.axis_index("feat") * tiles, tiles)
    inverse = 1.0 / (deg_ref[pl.ds(first, tiles), :] + 1).astype(jnp.float32)
    for t in range(tiles):
        scale_ref[LANES * t : LANES * (t + 1), :] = jnp.broadcast_to(
            inverse[t : t + 1, :], (LANES, LANES)
        ).T
    weight_out[...] = weight_ref[...].astype(jnp.float32).T.astype(jnp.bfloat16)
    bias_out[...] = jnp.broadcast_to(bias_ref[...], (LANES, LANES)).T


def add_tree(parts):
    while len(parts) > 1:
        tail = [parts[-1]] if len(parts) % 2 else []
        parts = [parts[i] + parts[i + 1] for i in range(0, len(parts) - 1, 2)] + tail
    return parts[0]


def load_plan(slots, start, ids_ref, order_ref, class_ref, slot_ids, order, classes, sem):
    size = order.shape[0]
    rows = pl.ds(start, size)
    first = [
        pltpu.make_async_copy(order_ref.at[rows], order, sem.at[slots]),
        pltpu.make_async_copy(class_ref.at[rows], classes.at[pl.ds(0, size)], sem.at[slots + 1]),
    ]
    by_slot = [
        pltpu.make_async_copy(
            ids_ref.at[pl.ds(j * CHUNK + start, size)], slot_ids.at[pl.ds(j * size, size)], sem.at[j]
        )
        for j in range(slots)
    ]
    for copy in first + by_slot:
        copy.start()
    return first, by_slot


def sum_slots(slots, start, part, parts, plan_refs, frame_ref, total_ref, slot_ids, order, classes, sem):
    size = order.shape[0]
    first, by_slot = load_plan(slots, start, *plan_refs, slot_ids, order, classes, sem)
    total_ref[...] = jnp.zeros_like(total_ref)
    for copy in first:
        copy.wait()
    last = GROUP - 1
    classes[size + part * GROUP + last] = slots + 1
    of_slot = [slot_ids.at[pl.ds(j * size, size)] for j in range(slots)]

    def body(count, carry):
        base, _ = carry
        for k in range(GROUP):
            node = order[base + k]
            total_ref[pl.ds(node, 1), :] = add_tree(
                [frame_ref[pl.ds(of_slot[j][node], 1), :] for j in range(count)]
            )
        return base + parts * GROUP, classes[base + parts * GROUP + last]

    def skip(carry):
        base, _ = carry
        return base + parts * GROUP, classes[base + parts * GROUP + last]

    carry = (jnp.int32(part * GROUP), classes[part * GROUP + last])
    carry = lax.while_loop(lambda carry: carry[1] == 0, skip, carry)
    for count in range(1, slots + 1):
        by_slot[count - 1].wait()
        carry = lax.while_loop(
            lambda carry, count=count: carry[1] == count, functools.partial(body, count), carry
        )


def near_kernel(slots, part, parts, ids_ref, order_ref, class_ref, frame_ref, after_ref, total_ref, *plan):
    sum_slots(slots, 0, part, parts, (ids_ref, order_ref, class_ref), frame_ref, total_ref, *plan)


def layer_kernel(slots, first, start, parts, own, ids_ref, order_ref, class_ref, frame_ref, scale_ref, weight_ref, bias_ref, after_ref, *refs):
    near, (keep_ref, send_ref, total_ref), plan = refs[:parts], refs[parts : parts + 3], refs[parts + 3 :]
    sum_slots(slots, start, 0, 1, (ids_ref, order_ref, class_ref), frame_ref, total_ref, *plan)
    chans, size = keep_ref.shape
    feat = lax.axis_index("feat")
    step = 256
    for at in range(0, size, step):
        rows = slice(at, at + step)
        own_at = pl.multiple_of(own + feat * own + first + at, step)
        total = total_ref[rows, :] + frame_ref[pl.ds(own_at, step), :]
        for ref in near:
            total = total + ref[rows, :]
        product = lax.dot_general(
            weight_ref[...],
            (total * scale_ref[first + at : first + at + step, :]).astype(jnp.bfloat16),
            (((1,), (1,)), ((), ())),
            preferred_element_type=jnp.float32,
        )
        bias = jnp.concatenate([bias_ref[...]] * (step // LANES), axis=1)
        result = jnp.maximum(product + bias, 0.0)
        low, high = result[:chans], result[chans:]
        keep_ref[:, rows] = jnp.where(feat == 0, low, high).astype(jnp.bfloat16)
        if send_ref.shape[0] == chans:
            result = jnp.where(feat == 0, high, low)
        send_ref[:, rows] = result.astype(jnp.bfloat16)


def output_kernel(*refs):
    out_ref = refs[-1]
    count = len(refs) // 2
    feat = lax.axis_index("feat")
    chans = out_ref.shape[0]
    for refs, part in ((refs[:count], feat), (refs[count:-1], 1 - feat)):
        at = part * (out_ref.shape[1] // 2)
        for ref in refs:
            size = ref.shape[1]
            rows = pl.ds(pl.multiple_of(feat * chans, chans), chans) if ref.shape[0] > chans else slice(None)
            out_ref[:, pl.ds(pl.multiple_of(at, size), size)] = ref[rows, :]
            at = at + size


def pallas(kernel, out_shape, in_specs, scratch=(), us=1.0, aliases=None):
    return pl.pallas_call(
        kernel,
        out_shape=out_shape,
        in_specs=in_specs,
        out_specs=jax.tree.map(lambda _: IN_VMEM, out_shape),
        scratch_shapes=list(scratch),
        input_output_aliases=aliases or {},
        compiler_params=pltpu.CompilerParams(vmem_limit_bytes=6 * 2**20),
        cost_estimate=pl.CostEstimate(flops=0, bytes_accessed=int(us * 3_000_000), transcendentals=0),
    )


IN_VMEM = pl.BlockSpec(memory_space=VMEM)
ANYWHERE = pl.BlockSpec(memory_space=pl.ANY)


def local(node_feats, neighbours, degrees, hub_rows, weight, bias_terms):
    chans, nodes = node_feats.shape
    slots = neighbours.shape[0]
    hubs = hub_rows.shape[0]
    slabs = lax.axis_size("slab")
    half = nodes // 2
    chunks = half // CHUNK
    frame_rows, hub_count = 2 * half + nodes, slabs * hubs
    swap = [(0, 1), (1, 0)]

    def bf16(*shape):
        return jax.ShapeDtypeStruct(shape, jnp.bfloat16)

    def f32(*shape):
        return jax.ShapeDtypeStruct(shape, jnp.float32)

    def i32(*shape):
        return jax.ShapeDtypeStruct(shape, jnp.int32)

    block, own_feats = pallas(
        hub_pick_kernel, (bf16(hubs // 2, 2 * chans), bf16(chans, nodes)), [IN_VMEM] * 2
    )(hub_rows[None, :], node_feats)
    arrived = None

    def stage(block, bits):
        return [lax.ppermute(block, "slab", [(i, i ^ bit) for i in range(slabs)]) for bit in bits]

    def join(block, arrived, after):
        rows = block.shape[0] * (1 + len(arrived))
        specs = [IN_VMEM] * (1 + len(arrived)) + [ANYWHERE]
        return pallas(join_kernel, bf16(rows, 2 * chans), specs, us=0.5)(block, *arrived, after)

    arrived = stage(block, STAGES[0])
    deg_tiles = degrees.reshape(nodes // LANES, LANES)
    table, tile = i32(slots, 8, LANES), i32(8, LANES)
    *ids, counts = pallas(
        functools.partial(slots_kernel, frame_rows, frame_rows + hub_count),
        (table, table, table, i32(3, 8, LANES)),
        [IN_VMEM, IN_VMEM, ANYWHERE],
        us=1.0,
    )(neighbours.reshape(slots, nodes // LANES, LANES), deg_tiles, block)
    other = lax.ppermute(own_feats, "feat", swap)

    block = join(block, arrived, counts)
    arrived = stage(block, STAGES[1])
    arrived.append(lax.ppermute(block, "feat", swap))
    across = [(2 * i + f, 2 * (i ^ STAGES[1][0]) + 1 - f) for i in range(slabs) for f in range(2)]
    arrived.append(lax.ppermute(block, ("slab", "feat"), across))
    scale, by_out, bias = pallas(
        constants_kernel,
        (f32(half, LANES), bf16(2 * chans, 2 * chans), f32(LANES, LANES)),
        [IN_VMEM] * 3 + [ANYWHERE],
        us=0.1,
    )(deg_tiles, weight, bias_terms[None, :], block)
    block = pallas(
        join_feat_kernel, bf16(4 * block.shape[0], 2 * chans), [IN_VMEM] * 4 + [ANYWHERE], us=0.1
    )(block, *arrived, scale)

    outer, inner = pallas(
        halves_kernel,
        (bf16(2 * chans, half),) * 2,
        [ANYWHERE] * 3,
        [pltpu.SemaphoreType.DMA((4,))],
        us=0.1,
    )(own_feats, other, block)
    inner_halo = lax.ppermute(inner, "slab", [(i, i ^ 1) for i in range(slabs)])
    outer_halo = lax.ppermute(
        outer, "slab", [(i, j) for i in range(slabs) for j in [i + 2 * (i & 1) - 1] if 0 <= j < slabs]
    )
    arrived = stage(block, STAGES[2])
    order = pallas(order_kernel, (tile,) * 6, [IN_VMEM, ANYWHERE], us=3.0)(counts, outer)
    near_plan, far_plan, full_plan = (
        [a.reshape(-1) for a in (ids[i], order[i], order[3 + i])] for i in range(3)
    )
    block = join(block, arrived, order[0])
    arrived = stage(block, STAGES[3])
    frame = pallas(
        frame_kernel,
        f32(frame_rows + hub_count + 8, LANES),
        [IN_VMEM] * 4 + [ANYWHERE],
        us=2.0,
    )(outer_halo, outer, inner, inner_halo, block)

    def plan_scratch(size):
        return [
            SMEM((slots * size,), jnp.int32),
            SMEM((size,), jnp.int32),
            SMEM((size + 2 * GROUP,), jnp.int32),
            pltpu.SemaphoreType.DMA((slots + 2,)),
        ]

    def near_sum(part, after):
        return pallas(
            functools.partial(near_kernel, slots, part, 2),
            f32(CHUNK, LANES),
            [ANYWHERE] * 3 + [IN_VMEM, ANYWHERE],
            plan_scratch(CHUNK),
            us=4.0,
        )(*near_plan, frame, after)

    near = [near_sum(0, block)]
    block = join(block, arrived, near[0])
    arrived = stage(block, STAGES[4])
    near.append(near_sum(1, block))
    frame = pallas(
        functools.partial(hub_frame_kernel, frame_rows, hubs),
        f32(*frame.shape),
        [IN_VMEM] * 3 + [ANYWHERE],
        us=0.5,
        aliases={0: 0},
    )(frame, block, arrived[0], near[1])

    def layer(plan, first, start, size, sent_chans, near, after, us):
        return pallas(
            functools.partial(layer_kernel, slots, first, start, len(near), half),
            (bf16(chans, size), bf16(sent_chans, size)),
            [ANYWHERE] * 3 + [IN_VMEM] * 4 + [ANYWHERE] + [IN_VMEM] * len(near),
            [VMEM((size, LANES), jnp.float32)] + plan_scratch(size),
            us=us,
        )(*plan, frame, scale, by_out, bias, after, *near)

    keep, received = [near[1]], []
    for plan, first, start, size, sent_chans, near, us in (
        (far_plan, 0, 0, CHUNK, 2 * chans, near, 3.0),
        (full_plan, CHUNK, 0, CHUNK, chans, [], 8.0),
    ):
        kept, sent = layer(plan, first, start, size, sent_chans, near, keep[-1], us)
        keep.append(kept)
        received.append(lax.ppermute(sent, "feat", swap))
    pieces = keep[1:] + received
    return pallas(output_kernel, bf16(chans, nodes), [IN_VMEM] * len(pieces), us=0.5)(*pieces)


def solution(mesh):
    in_specs = (P("feat", "slab"), P(None, "slab"), P("slab"), P("slab"), P(), P())
    return jax.shard_map(local, mesh=mesh, in_specs=in_specs, out_specs=P("feat", "slab"), check_vma=False)
```
